512 devices in a mesh: tp: 8 (over z_lo, core), dp: 4 (over z_hi), draft: 16 (over x, y).
Axes of the slice: x: 4, y: 4, z: 16 (z_hi: 4, z_lo: 4; z = z_hi * 4 + z_lo), core: 2. Of those that a mesh axis runs over, the one named last changes fastest.
Arguments:
- features: bfloat16 [4096, 3, 8192], P(('dp', 'draft'), None, 'tp'), may hold values from -6 to 6
- fc_weight: bfloat16 [8192, 3, 8192], P('tp', None, 'draft'), may hold values from -0.0390625 to 0.0390625
- mix_gain: float32 [8192], P('draft'), may hold values from 0.3 to 1.5
- lengths: int32 [4], replicated, may hold values from 1 to 1024, 3072 in all
Outputs:
- fc_grad: bfloat16 [8192, 3, 8192], P(('tp', 'dp'), None, 'draft')
- mix_grad: float32 [8192], P('draft')
The draws below stay inside these ranges and needn't reach their ends.
Inputs may be any that keep to these rules, and one draw needn't show every extreme that they name: `lengths`: valid tokens of each sequence; they sum to 3072.
All inputs are finite; a program needn't handle non-finite values.
Results may differ from the reference program's by a relative error of at most 0.025.
Values may be sent and summed in bfloat16 or wider, within the bound.
No kernel may reach another device: no remote copies, remote signals or barrier semaphores. Data moves between devices by JAX's collectives and lax.ppermute only.
A program may use at most 128 MiB of HBM per device.

```python
import math
import jax
import jax.numpy as jnp
import numpy as np
from jax import lax

D = 8192
LEVELS = 3
UNROLL = 3
SEQ = 1024
SEQS = 4
TOKENS = 4096


def steps_of(own_key, extent, pieces, low, high):
    factor_of, own = 1.0, jax.random.fold_in(own_key, 6)
    for axis_at, shards_of in pieces:
        heights = jnp.exp(jax.random.uniform(jax.random.fold_in(own, axis_at), (shards_of,), jnp.float32, low / len(pieces), high / len(pieces)))
        factor_of = factor_of * jnp.repeat(heights, extent[axis_at] // shards_of).reshape([-1 if axis == axis_at else 1 for axis in range(len(extent))])
    return factor_of


def profile(count, total, most, skew):
    loads = [(1 << 20) // math.isqrt(standing ** skew) + 1 for standing in range(2, count + 1)]
    rest, counts = total - most - (count - 1), [1] * (count - 1)
    while rest > 0:
        movable = [i for i in range(count - 1) if counts[i] < most]
        mass, left = sum([loads[i] for i in movable]), rest
        for i in movable:
            extra = min(most - counts[i], max(1, left * loads[i] // mass), rest)
            counts[i] = counts[i] + extra
            rest = rest - extra
    return np.array([most] + counts)


def ragged(rng, count, total, limit, slope):
    if count == 2:
        one = jax.random.randint(rng, (), max(1, total - limit), min(limit, total - 1) + 1)
        return jnp.stack([one, total - one])
    tallies = jnp.asarray(profile(count, total, limit, slope), jnp.int32)
    twos = (count - 1) // 2
    donor, sink = tallies[1:1 + 2 * twos:2], tallies[2:2 + 2 * twos:2]
    room = jnp.minimum(donor - 1, limit - sink)
    shifted = jax.random.randint(jax.random.fold_in(rng, 1), (twos,), 0, 1 << 20) % (room + 1)
    tallies = tallies.at[1:1 + 2 * twos:2].set(donor - shifted).at[2:2 + 2 * twos:2].set(sink + shifted)
    return tallies[jax.random.permutation(jax.random.fold_in(rng, 2), count)]


def gaussian(own_key, dims, deviation, limit, shards=(), held_as=jnp.bfloat16):
    result = deviation * jax.random.normal(own_key, dims, jnp.float32)
    if shards:
        result = result * steps_of(own_key, dims, shards, -0.22, 0.18)
    return jnp.clip(result, -limit, limit).astype(held_as)


def setup_inputs(seed: int = 0) -> dict:
    keys = jax.random.split(jax.random.key(seed), 5)
    return {
        "features": gaussian(keys[0], (TOKENS, LEVELS, D), 1.0, 6.0, ((0, 64), (2, 8))),
        "fc_weight": gaussian(keys[1], (D, LEVELS, D), (LEVELS * D) ** -0.5, 0.0390625, ((0, 8), (2, 16))),
        "mix_gain": jnp.clip(0.3 + 1.2 * jax.random.uniform(keys[2], (D,), jnp.float32) ** steps_of(keys[2], (D,), ((0, 16),), -0.2, 0.2), 0.3, 1.5),
        "lengths": ragged(keys[3], SEQS, SEQ * SEQS // 2 + SEQ, SEQ, 0).astype(jnp.int32),
    }


loss_scale = 64.0

def shifted_down(values, amount):
    padding = jnp.zeros((amount,) + values.shape[1:], values.dtype)
    return jnp.concatenate([padding, values[:-amount]], axis=0)

def shifted_up(values, amount):
    padding = jnp.zeros((amount,) + values.shape[1:], values.dtype)
    return jnp.concatenate([values[amount:], padding], axis=0)

def draft_loss(joined, mix_gain, high_rows, length, valid_count):
    positions = jnp.arange(joined.shape[0], dtype=jnp.int32)
    draft_state = jax.nn.silu(joined)
    running_total = jnp.zeros((), jnp.float32)
    for unroll in range(UNROLL):
        if unroll > 0:
            draft_state = jax.nn.silu(joined + mix_gain * shifted_down(draft_state, 1))
        target = shifted_up(high_rows, unroll + 1)
        valid_rows = (positions + unroll + 1 < length).astype(jnp.float32)
        residual_error = (draft_state - target) * valid_rows[:, None]
        running_total = running_total + jnp.sum(residual_error * residual_error)
    return running_total * (loss_scale / (2.0 * valid_count))

def chain_grads(joined, mix_gain, high_rows, length, valid_count):

    def loss_of(joined_in, mix_in):
        return draft_loss(joined_in, mix_in, high_rows, length, valid_count)
    loss_value, pullback = jax.vjp(loss_of, joined, mix_gain)
    return pullback(jnp.ones_like(loss_value))

def valid_total(lengths):
    running = jnp.zeros((), jnp.float32)
    for unroll in range(1, UNROLL + 1):
        running = running + jnp.sum(jnp.maximum(lengths - unroll, 0)).astype(jnp.float32)
    return running

def reference(features, fc_weight, mix_gain, lengths):
    flat_rows = features.reshape(TOKENS, LEVELS * D).astype(jnp.float32)
    matrix = jnp.transpose(fc_weight, (1, 0, 2)).reshape(LEVELS * D, D).astype(jnp.float32)
    joined = jnp.dot(flat_rows, matrix, precision=lax.Precision.HIGHEST).reshape(SEQS, SEQ, D)
    high_rows = features[:, LEVELS - 1, :].astype(jnp.float32).reshape(SEQS, SEQ, D)
    valid_count = valid_total(lengths)
    grad_joined, grad_mix = jax.vmap(chain_grads, in_axes=(0, None, 0, 0, None))(joined, mix_gain, high_rows, lengths, valid_count)
    mix_grad = lax.optimization_barrier(jnp.sum(grad_mix, axis=0))
    joined_grad = grad_joined.astype(jnp.bfloat16)
    grad_total = jnp.zeros((LEVELS * D, D), jnp.float32)
    for sequence in range(SEQS):
        rows_block = flat_rows[sequence * SEQ:(sequence + 1) * SEQ]
        term = jnp.dot(rows_block.T, joined_grad[sequence].astype(jnp.float32), precision=lax.Precision.HIGHEST)
        rounded = lax.optimization_barrier(term.astype(jnp.bfloat16))
        grad_total = grad_total + rounded.astype(jnp.float32)
    fc_grad = jnp.transpose(grad_total.astype(jnp.bfloat16).reshape(LEVELS, D, D), (1, 0, 2))
    return (fc_grad, mix_grad)
```

```python
import jax
import jax.numpy as jnp
from jax import lax
from jax.experimental import pallas as pl
from jax.experimental.pallas import tpu as pltpu
from jax.sharding import PartitionSpec as P

LEVELS = 3
UNROLL = 3
LOSS_SCALE = 64.0
HALO = 8
TAIL = 16


def sigmoid(v):
    return 1.0 / (1.0 + jnp.exp(-v))


def chain_kernel(meta_ref, scale_ref, parts_ref, high_ref, gain_ref, grad_ref, mix_ref):
    rows = parts_ref.shape[1]
    own = rows - 2 * HALO
    joined = parts_ref[0].astype(jnp.float32)
    for member in range(1, parts_ref.shape[0]):
        joined = joined + parts_ref[member].astype(jnp.float32)
    high = high_ref[...].astype(jnp.float32)
    width = joined.shape[1]
    gain = gain_ref[...]
    scale = scale_ref[0]
    start, length = meta_ref[0], meta_ref[1]
    position = start - HALO + lax.broadcasted_iota(jnp.int32, (rows, width), 0)

    def down(values):
        return jnp.concatenate([jnp.zeros((1, width), jnp.float32), values[:-1]], axis=0)

    def up(values):
        return jnp.concatenate([values[1:], jnp.zeros((1, width), jnp.float32)], axis=0)

    def target(step):
        lead = jnp.zeros((HALO - step, width), jnp.float32)
        return jnp.concatenate([lead, high[: rows - HALO + step]], axis=0)

    def state_and_slope(v):
        gate = sigmoid(v)
        return v * gate, gate * (1.0 + v * (1.0 - gate))

    def residual(state, step):
        return jnp.where(position + step < length, scale * (state - target(step)), 0.0)

    state_1, slope_1 = state_and_slope(joined)
    before_1 = down(state_1)
    state_2, slope_2 = state_and_slope(joined + gain * before_1)
    before_2 = down(state_2)
    state_3, slope_3 = state_and_slope(joined + gain * before_2)
    delta_3 = residual(state_3, 3) * slope_3
    delta_2 = (residual(state_2, 2) + up(gain * delta_3)) * slope_2
    delta_1 = (residual(state_1, 1) + up(gain * delta_2)) * slope_1
    total = delta_1 + delta_2 + delta_3
    grad_ref[...] = total[HALO : HALO + own].astype(jnp.bfloat16)
    mix = (delta_2 * before_1 + delta_3 * before_2)[HALO : HALO + own]
    mix_ref[...] = jnp.sum(mix, axis=0, keepdims=True)


def chain(parts, high, gain, start, length, scale):
    members, rows, width = parts.shape
    own = rows - 2 * HALO
    vmem = pl.BlockSpec(memory_space=pltpu.VMEM)
    smem = pl.BlockSpec(memory_space=pltpu.SMEM)
    return pl.pallas_call(
        chain_kernel,
        out_shape=(
            jax.ShapeDtypeStruct((own, width), jnp.bfloat16),
            jax.ShapeDtypeStruct((1, width), jnp.float32),
        ),
        in_specs=[smem, smem, vmem, vmem, vmem],
        out_specs=(vmem, vmem),
        compiler_params=pltpu.CompilerParams(vmem_limit_bytes=32 << 20),
        cost_estimate=pl.CostEstimate(
            flops=60 * rows * width, bytes_accessed=2 * parts.size, transcendentals=3 * rows * width
        ),
        name="chain",
    )(jnp.stack([start, length]), scale.reshape(1), parts, high, gain.reshape(1, width))


def valid_total(lengths):
    running = jnp.zeros((), jnp.float32)
    for unroll in range(1, UNROLL + 1):
        running = running + jnp.sum(jnp.maximum(lengths - unroll, 0)).astype(jnp.float32)
    return running


def high_of(top, tp_count, draft_count, draft_index):
    width = top.shape[1] // 2
    even = draft_index % 2 == 0
    left, right = top[:, :width], top[:, width:]
    flat = lambda t, e: t * draft_count + e
    first, second = [], []
    for t in range(tp_count):
        for e in range(draft_count):
            first.append((flat(t, e), flat(e // 2, 2 * t + e % 2)))
            second.append((flat(t, e), flat(e // 2, 2 * t + 1 - e % 2)))
    axes = ("tp", "draft")
    one = lax.ppermute(jnp.where(even, left, right), axes, first)
    two = lax.ppermute(jnp.where(even, right, left), axes, second)
    rows = jnp.concatenate([jnp.where(even, one, two), jnp.where(even, two, one)], axis=0)
    following = lax.ppermute(rows[:TAIL], "tp", [(j, j - 1) for j in range(1, tp_count)])
    return jnp.concatenate([rows, following], axis=0)


def local(features, fc_weight, mix_gain, lengths):
    tp_count, dp_count = lax.axis_size("tp"), lax.axis_size("dp")
    draft_count = lax.axis_size("draft")
    tp_index, draft_index = lax.axis_index("tp"), lax.axis_index("draft")
    own_rows, _, depth = features.shape
    width = fc_weight.shape[2]
    rows = own_rows * draft_count
    piece = rows // tp_count
    part = depth // dp_count
    own = features.transpose(1, 0, 2)
    weight = fc_weight.transpose(1, 0, 2)

    gathered = lax.all_gather(own, "draft", axis=1, tiled=True)
    traded = lax.all_to_all(
        own.reshape(LEVELS, own_rows, dp_count, part), "dp", split_axis=2, concat_axis=0, tiled=False
    )
    high = high_of(own[LEVELS - 1], tp_count, draft_count, draft_index)

    gathered, traded = lax.optimization_barrier((gathered, traded))
    every = lax.all_gather(traded, "draft", axis=2, tiled=True)
    every = every.transpose(1, 0, 2, 3).reshape(LEVELS, dp_count * rows, part)

    partial = jnp.einsum("lrk,lkn->rn", gathered, weight, preferred_element_type=jnp.float32)
    middle = partial.astype(jnp.bfloat16).reshape(tp_count, piece, width)
    edge = jnp.zeros((1, HALO, width), jnp.bfloat16)
    before = jnp.concatenate([edge, middle[:-1, piece - HALO :]], axis=0)
    after = jnp.concatenate([middle[1:, :HALO], edge], axis=0)
    pieces = jnp.concatenate([before, middle, after], axis=1)
    parts = lax.all_to_all(pieces, "tp", split_axis=0, concat_axis=0, tiled=True)

    length = lengths[lax.axis_index("dp")]
    scale = LOSS_SCALE / valid_total(lengths)
    grad, mix = chain(parts, high, mix_gain, tp_index * piece, length, scale)
    grads = lax.all_gather(grad, ("dp", "tp"), axis=0, tiled=True)
    mix_total = lax.psum(mix[0], ("tp", "dp"))
    fc_grad = jnp.einsum("ltk,tn->lkn", every, grads, preferred_element_type=jnp.float32)
    return (fc_grad.astype(jnp.bfloat16).transpose(1, 0, 2), mix_total)


def solution(mesh):
    placed = (P(("dp", "draft"), None, "tp"), P("tp", None, "draft"), P("draft"), P())
    return jax.shard_map(
        local,
        mesh=mesh,
        in_specs=placed,
        out_specs=(P(("tp", "dp"), None, "draft"), P("draft")),
        check_vma=False,
    )
```

```python
import jax
import jax.numpy as jnp
from jax import lax
from jax.experimental import pallas as pl
from jax.experimental.pallas import tpu as pltpu
from jax.sharding import PartitionSpec as P

LEVELS = 3
UNROLL = 3
LOSS_SCALE = 64.0
HALO = 8
TAIL = 16
X, Y = 4, 4
ZL, CORES, ZH = 4, 2, 4
VMEM = pl.BlockSpec(memory_space=pltpu.VMEM)
SMEM = pl.BlockSpec(memory_space=pltpu.SMEM)
PARAMS = pltpu.CompilerParams(vmem_limit_bytes=48 << 20)


def plane_move(step, first):
    pairs = []
    for t in range(ZL * CORES):
        for x in range(X):
            for y in range(Y):
                along_x = (t % CORES == 0) == first
                source = (x + step) % X * Y + y if along_x else x * Y + (y + step) % Y
                pairs.append((t * X * Y + source, t * X * Y + x * Y + y))
    return lambda block: lax.ppermute(block, ("tp", "draft"), pairs)


def from_other_core(block):
    return lax.ppermute(block, "tp", [(t ^ 1, t) for t in range(ZL * CORES)])


def from_zl(block, step):
    pairs = [((t // CORES + step) % ZL * CORES + t % CORES, t) for t in range(ZL * CORES)]
    return lax.ppermute(block, "tp", pairs)


def from_zh(block, step):
    return lax.ppermute(block, "dp", [((s + step) % ZH, s) for s in range(ZH)])


def from_z(block, step):
    pairs = []
    for t in range(ZL * CORES):
        for s in range(ZH):
            z = (s * ZL + t // CORES + step) % (ZL * ZH)
            pairs.append((((z % ZL) * CORES + t % CORES) * ZH + z // ZL, t * ZH + s))
    return lax.ppermute(block, ("tp", "dp"), pairs)


def project_kernel(*refs):
    *block_refs, weight_ref, out_ref, total_ref = refs
    level = pl.program_id(0)
    rows = jnp.concatenate([r[...].reshape(-1, r.shape[-1]) for r in block_refs], axis=0)
    term = jnp.dot(rows, weight_ref[0], preferred_element_type=jnp.float32)

    @pl.when(level == 0)
    def _():
        total_ref[...] = term

    @pl.when(level > 0)
    def _():
        total_ref[...] += term

    @pl.when(level == LEVELS - 1)
    def _():
        out_ref[...] = total_ref[...].astype(jnp.bfloat16).reshape(out_ref.shape)


def project(blocks, weight):
    _, _, rows, depth = blocks[0].shape
    count = sum(b.shape[0] for b in blocks)
    width = weight.shape[2]
    return pl.pallas_call(
        project_kernel,
        grid=(LEVELS,),
        out_shape=jax.ShapeDtypeStruct((count, rows, width), jnp.bfloat16),
        in_specs=[
            pl.BlockSpec((b.shape[0], 1, rows, depth), lambda l: (0, l, 0, 0)) for b in blocks
        ]
        + [pl.BlockSpec((1, depth, width), lambda l: (l, 0, 0))],
        out_specs=pl.BlockSpec((count, rows, width), lambda l: (0, 0, 0)),
        scratch_shapes=[pltpu.VMEM((count * rows, width), jnp.float32)],
        compiler_params=PARAMS,
        cost_estimate=pl.CostEstimate(
            flops=2 * count * rows * LEVELS * depth * width,
            bytes_accessed=2 * (weight.size + count * rows * LEVELS * depth),
            transcendentals=0,
        ),
        name="project",
    )(*blocks, weight)


def place_kernel(meta_ref, *refs):
    *group_refs, keep_ref, send_ref, token_ref = refs
    core, x, y = meta_ref[0], meta_ref[1], meta_ref[2]
    rows = group_refs[0].shape[1]
    total = rows * X * Y
    edge = jnp.zeros((HALO, token_ref.shape[1]), jnp.float32)
    token_ref[pl.ds(0, HALO), :] = edge
    token_ref[pl.ds(HALO + total, HALO), :] = edge
    for second, group_ref in zip((0, 1, 2, 3), group_refs):
        for first in range(4):
            dx = jnp.where(core == 0, first, second)
            dy = jnp.where(core == 0, second, first)
            e = lax.rem(x + dx, X) * Y + lax.rem(y + dy, Y)
            at = pl.multiple_of(e * rows + HALO, 8)
            token_ref[pl.ds(at, rows), :] = group_ref[first].astype(jnp.float32)
    piece = total // (ZL * CORES)
    for zl in range(ZL):
        for out_ref, whose in ((keep_ref, core), (send_ref, 1 - core)):
            at = pl.multiple_of((zl * CORES + whose) * piece, 8)
            out_ref[zl] = token_ref[pl.ds(at, piece + 2 * HALO), :].astype(jnp.bfloat16)


def place(groups, core, x, y):
    _, rows, width = groups[0].shape
    total = rows * X * Y
    pieces = jax.ShapeDtypeStruct((ZL, total // (ZL * CORES) + 2 * HALO, width), jnp.bfloat16)
    return pl.pallas_call(
        place_kernel,
        out_shape=(pieces, pieces),
        in_specs=[SMEM] + [VMEM] * 4,
        out_specs=(VMEM, VMEM),
        scratch_shapes=[pltpu.VMEM((total + 2 * HALO, width), jnp.float32)],
        compiler_params=PARAMS,
        cost_estimate=pl.CostEstimate(
            flops=total * width, bytes_accessed=4 * total * width, transcendentals=0
        ),
        name="place",
    )(jnp.stack([core, x, y]), *groups)


def join_kernel(meta_ref, keep_ref, got_ref, own_ref, *away_refs):
    zl = meta_ref[0]

    def piece(index):
        return keep_ref[index].astype(jnp.float32) + got_ref[index].astype(jnp.float32)

    own_ref[...] = piece(zl).astype(jnp.bfloat16)
    for step, away_ref in zip((1, 2, 3), away_refs):
        away_ref[...] = piece(lax.rem(zl + ZL - step, ZL)).astype(jnp.bfloat16)


def join(keep, got, zl):
    piece = jax.ShapeDtypeStruct(keep.shape[1:], jnp.bfloat16)
    return pl.pallas_call(
        join_kernel,
        out_shape=(piece,) * ZL,
        in_specs=[SMEM, VMEM, VMEM],
        out_specs=(VMEM,) * ZL,
        compiler_params=PARAMS,
        cost_estimate=pl.CostEstimate(
            flops=keep.size, bytes_accessed=6 * keep.size, transcendentals=0
        ),
        name="join",
    )(zl.reshape(1), keep, got)


def sigmoid(v):
    return 1.0 / (1.0 + jnp.exp(-v))


def chain_kernel(meta_ref, scale_ref, *refs):
    *part_refs, high_ref, gain_ref, grad_ref = refs
    rows, width = part_refs[0].shape
    own = rows - 2 * HALO
    joined = part_refs[0][...].astype(jnp.float32)
    for part_ref in part_refs[1:]:
        joined = joined + part_ref[...].astype(jnp.float32)
    high = high_ref[...].astype(jnp.float32)
    gain = gain_ref[...]
    scale = scale_ref[0]
    start, length = meta_ref[0], meta_ref[1]
    position = start - HALO + lax.broadcasted_iota(jnp.int32, (rows, width), 0)

    def down(values):
        return jnp.concatenate([jnp.zeros((1, width), jnp.float32), values[:-1]], axis=0)

    def up(values):
        return jnp.concatenate([values[1:], jnp.zeros((1, width), jnp.float32)], axis=0)

    def target(step):
        lead = jnp.zeros((HALO - step, width), jnp.float32)
        return jnp.concatenate([lead, high[: rows - HALO + step]], axis=0)

    def state_and_slope(v):
        gate = sigmoid(v)
        return v * gate, gate * (1.0 + v * (1.0 - gate))

    def residual(state, step):
        return jnp.where(position + step < length, scale * (state - target(step)), 0.0)

    state_1, slope_1 = state_and_slope(joined)
    before_1 = down(state_1)
    state_2, slope_2 = state_and_slope(joined + gain * before_1)
    before_2 = down(state_2)
    state_3, slope_3 = state_and_slope(joined + gain * before_2)
    delta_3 = residual(state_3, 3) * slope_3
    delta_2 = (residual(state_2, 2) + up(gain * delta_3)) * slope_2
    delta_1 = (residual(state_1, 1) + up(gain * delta_2)) * slope_1
    total = delta_1 + delta_2 + delta_3
    mix = (delta_2 * before_1 + delta_3 * before_2)[HALO : HALO + own]
    rest = jnp.sum(mix, axis=0, keepdims=True)
    tail = []
    for _ in range(3):
        term = rest.astype(jnp.bfloat16).astype(jnp.float32)
        tail.append(term)
        rest = rest - term
    tail.append(jnp.zeros((TAIL - 3, width), jnp.float32))
    grad_ref[pl.ds(0, own), :] = total[HALO : HALO + own].astype(jnp.bfloat16)
    grad_ref[pl.ds(own, TAIL), :] = jnp.concatenate(tail, axis=0).astype(jnp.bfloat16)


def chain(parts, high, gain, start, length, scale):
    rows, width = parts[0].shape
    own = rows - 2 * HALO
    return pl.pallas_call(
        chain_kernel,
        out_shape=jax.ShapeDtypeStruct((own + TAIL, width), jnp.bfloat16),
        in_specs=[SMEM, SMEM] + [VMEM] * (len(parts) + 2),
        out_specs=VMEM,
        compiler_params=PARAMS,
        cost_estimate=pl.CostEstimate(
            flops=60 * rows * width, bytes_accessed=10 * rows * width, transcendentals=3 * rows * width
        ),
        name="chain",
    )(jnp.stack([start, length]), scale.reshape(1), *parts, high, gain.reshape(1, width))


def pieces_of(zl, zh, core):
    found = []

    def chip(step):
        z = lax.rem(zh * ZL + zl + step + ZL * ZH, ZL * ZH)
        return lax.rem(z, ZL), z // ZL

    layout = [(0, 0, 0, (0, 1, 2, 3)), (1, 0, 1, (0, 1, 2, 3))]
    layout += [(2, 1, 0, (0, 1, 2, 3)), (3, -1, 0, (0, 1, 2, 3))]
    layout += [(4, 1, 1, (0, 1, 2, 3)), (5, -1, 1, (0, 1, 2, 3))]
    layout += [(6, 2, 0, (2, 3)), (7, -2, 0, (1, 2)), (8, 2, 1, (2, 3)), (9, -2, 1, (1, 2))]
    for group, step, other, rows in layout:
        there_zl, there_zh = chip(step)
        member = there_zl * CORES + (1 - core if other else core)
        for at, row in enumerate(rows):
            found.append((group, at, member, lax.rem(there_zh + row, ZH)))
    return found


def weight_grad_kernel(meta_ref, features_ref, *refs):
    *group_refs, out_ref, mix_ref, grads_ref = refs
    zl, zh, core = meta_ref[0], meta_ref[1], meta_ref[2]
    half = grads_ref.shape[1] // ZH
    width = grads_ref.shape[2]

    @pl.when(pl.program_id(0) == 0)
    def _():
        mix = jnp.zeros((TAIL, width), jnp.float32)
        for group, at, member, sequence in pieces_of(zl, zh, core):
            rank = lax.rem(sequence - zh + ZH, ZH)
            slot = pl.ds(pl.multiple_of(rank * half, 16), half)
            for part in range(2):
                rows = group_refs[group][at, pl.ds(part * half, half), :]
                grads_ref[member * 2 + part, slot, :] = rows
            mix = mix + group_refs[group][at, pl.ds(2 * half, TAIL), :].astype(jnp.float32)
        mix_ref[...] = jnp.sum(mix, axis=0, keepdims=True)

    blocks = features_ref.shape[0]
    left = jnp.concatenate([features_ref[e, 0] for e in range(blocks)], axis=1)
    right = grads_ref[...].reshape(-1, width)
    out_ref[0] = jnp.dot(left, right, preferred_element_type=jnp.float32).astype(jnp.bfloat16)


def weight_grad(features, groups, zl, zh, core):
    draft, _, columns, tokens = features.shape
    width = groups[0].shape[2]
    whole = [pl.BlockSpec(g.shape, lambda l: (0, 0, 0)) for g in groups]
    return pl.pallas_call(
        weight_grad_kernel,
        grid=(LEVELS,),
        out_shape=(
            jax.ShapeDtypeStruct((LEVELS, columns, width), jnp.bfloat16),
            jax.ShapeDtypeStruct((1, width), jnp.float32),
        ),
        in_specs=[SMEM, pl.BlockSpec((draft, 1, columns, tokens), lambda l: (0, l, 0, 0))] + whole,
        out_specs=(
            pl.BlockSpec((1, columns, width), lambda l: (l, 0, 0)),
            pl.BlockSpec((1, width), lambda l: (0, 0)),
        ),
        scratch_shapes=[pltpu.VMEM((draft, tokens, width), jnp.bfloat16)],
        compiler_params=PARAMS,
        cost_estimate=pl.CostEstimate(
            flops=2 * draft * LEVELS * columns * tokens * width,
            bytes_accessed=2 * features.size + 2 * draft * tokens * width,
            transcendentals=0,
        ),
        name="weight_grad",
    )(jnp.stack([zl, zh, core]), features, *groups)


def valid_total(lengths):
    running = jnp.zeros((), jnp.float32)
    for unroll in range(1, UNROLL + 1):
        running = running + jnp.sum(jnp.maximum(lengths - unroll, 0)).astype(jnp.float32)
    return running


def high_halves(top, draft_index):
    members, draft_count = ZL * CORES, X * Y
    width = top.shape[1] // 2
    even = draft_index % 2 == 0
    left, right = top[:, :width], top[:, width:]
    first, second = [], []
    for t in range(members):
        for e in range(draft_count):
            target = e // 2 * draft_count + 2 * t
            first.append((t * draft_count + e, target + e % 2))
            second.append((t * draft_count + e, target + 1 - e % 2))
    axes = ("tp", "draft")
    one = lax.ppermute(jnp.where(even, left, right), axes, first)
    two = lax.ppermute(jnp.where(even, right, left), axes, second)
    return one, two


def high_rows(one, two, draft_index):
    even = draft_index % 2 == 0
    return jnp.concatenate([jnp.where(even, one, two), jnp.where(even, two, one)], axis=0)


def high_after(rows):
    return lax.ppermute(rows[:TAIL], "tp", [(j, j - 1) for j in range(1, ZL * CORES)])


def trade_columns(own, zh):
    part = own.shape[2] // ZH

    def quarter(index):
        return lax.dynamic_slice_in_dim(own, index * part, part, 2)

    blocks = [quarter(zh)]
    for step in (1, 2, 3):
        blocks.append(from_zh(quarter((zh + ZH - step) % ZH), step))
    return [b.transpose(0, 2, 1) for b in blocks]


def gather_grads(grad):
    stack = jnp.stack([grad] + [from_zh(grad, step) for step in (1, 2, 3)])
    above, below = from_z(stack, 1), from_z(stack, -1)
    other = from_other_core(stack)
    far_above, far_below = from_z(above[2:4], 1), from_z(below[1:3], -1)
    other_above, other_below = from_other_core(above), from_other_core(below)
    far = from_other_core(jnp.concatenate([far_above, far_below]))
    return [stack, other, above, below, other_above, other_below, far_above, far_below, far[:2], far[2:]]


def local(features, fc_weight, mix_gain, lengths):
    tp_index, zh = lax.axis_index("tp"), lax.axis_index("dp")
    draft_index = lax.axis_index("draft")
    zl, core = tp_index // CORES, tp_index % CORES
    x, y = draft_index // Y, draft_index % Y
    own_rows = features.shape[0]
    piece = own_rows * X * Y // (ZL * CORES)
    own = features.transpose(1, 0, 2)
    weight = fc_weight.transpose(1, 0, 2)

    along = jnp.stack([own] + [plane_move(step, True)(own) for step in (1, 2, 3)])
    along, later = lax.optimization_barrier((along, own))
    up, down = plane_move(1, False)(along), plane_move(-1, False)(along)
    traded = trade_columns(later, zh)
    halves = high_halves(later[LEVELS - 1], draft_index)
    zero = project([along], weight)
    up, down, traded, halves, zero = lax.optimization_barrier((up, down, traded, halves, zero))
    opposite = [plane_move(1, False)(up[:2]), plane_move(-1, False)(down[2:])]
    high = high_rows(*halves, draft_index)
    after = high_after(high)
    one, three = project([up], weight), project([down], weight)
    traded = jnp.concatenate(traded, axis=2)
    opposite, after, one, three, traded = lax.optimization_barrier((opposite, after, one, three, traded))
    every = lax.all_gather(traded, "draft", axis=0, tiled=False)
    groups = [zero, one, project(opposite, weight), three]
    high = jnp.concatenate([high, after], axis=0)

    keep, send = place(groups, core, x, y)
    mine, *away = join(keep, from_other_core(send), zl)
    parts = [mine] + [from_zl(block, step) for step, block in zip((1, 2, 3), away)]
    scale = LOSS_SCALE / valid_total(lengths)
    grad = chain(parts, high, mix_gain, tp_index * piece, lengths[zh], scale)
    fc_grad, mix_total = weight_grad(every, gather_grads(grad), zl, zh, core)
    return (fc_grad.transpose(1, 0, 2), mix_total[0])


def solution(mesh):
    placed = (P(("dp", "draft"), None, "tp"), P("tp", None, "draft"), P("draft"), P())
    return jax.shard_map(
        local,
        mesh=mesh,
        in_specs=placed,
        out_specs=(P(("tp", "dp"), None, "draft"), P("draft")),
        check_vma=False,
    )
```

```python
import jax
import jax.numpy as jnp
from jax import lax
from jax.experimental import pallas as pl
from jax.experimental.pallas import tpu as pltpu
from jax.sharding import PartitionSpec as P

LEVELS = 3
UNROLL = 3
LOSS_SCALE = 64.0
HALO = 8
TAIL = 16
X, Y = 4, 4
ZL, CORES, ZH = 4, 2, 4
VMEM = pl.BlockSpec(memory_space=pltpu.VMEM)
SMEM = pl.BlockSpec(memory_space=pltpu.SMEM)
PARAMS = pltpu.CompilerParams(vmem_limit_bytes=48 << 20)


def plane_move(step, first):
    pairs = []
    for t in range(ZL * CORES):
        for x in range(X):
            for y in range(Y):
                along_x = (t % CORES == 0) == first
                source = (x + step) % X * Y + y if along_x else x * Y + (y + step) % Y
                pairs.append((t * X * Y + source, t * X * Y + x * Y + y))
    return lambda block: lax.ppermute(block, ("tp", "draft"), pairs)


def from_other_core(block):
    return lax.ppermute(block, "tp", [(t ^ 1, t) for t in range(ZL * CORES)])


def from_zl(block, step):
    pairs = [((t // CORES + step) % ZL * CORES + t % CORES, t) for t in range(ZL * CORES)]
    return lax.ppermute(block, "tp", pairs)


def from_zh(block, step):
    return lax.ppermute(block, "dp", [((s + step) % ZH, s) for s in range(ZH)])


def from_z(block, step):
    pairs = []
    for t in range(ZL * CORES):
        for s in range(ZH):
            z = (s * ZL + t // CORES + step) % (ZL * ZH)
            pairs.append((((z % ZL) * CORES + t % CORES) * ZH + z // ZL, t * ZH + s))
    return lax.ppermute(block, ("tp", "dp"), pairs)


def project_kernel(*refs):
    *block_refs, weight_ref, out_ref, total_ref = refs
    level = pl.program_id(0)
    rows = jnp.concatenate([r[...].reshape(-1, r.shape[-1]) for r in block_refs], axis=0)
    term = jnp.dot(rows, weight_ref[0], preferred_element_type=jnp.float32)

    @pl.when(level == 0)
    def _():
        total_ref[...] = term

    @pl.when(level > 0)
    def _():
        total_ref[...] += term

    @pl.when(level == LEVELS - 1)
    def _():
        out_ref[...] = total_ref[...].astype(jnp.bfloat16).reshape(out_ref.shape)


def project(blocks, weight):
    _, _, rows, depth = blocks[0].shape
    count = sum(b.shape[0] for b in blocks)
    width = weight.shape[2]
    return pl.pallas_call(
        project_kernel,
        grid=(LEVELS,),
        out_shape=jax.ShapeDtypeStruct((count, rows, width), jnp.bfloat16),
        in_specs=[
            pl.BlockSpec((b.shape[0], 1, rows, depth), lambda l: (0, l, 0, 0)) for b in blocks
        ]
        + [pl.BlockSpec((1, depth, width), lambda l: (l, 0, 0))],
        out_specs=pl.BlockSpec((count, rows, width), lambda l: (0, 0, 0)),
        scratch_shapes=[pltpu.VMEM((count * rows, width), jnp.float32)],
        compiler_params=PARAMS,
        cost_estimate=pl.CostEstimate(
            flops=2 * count * rows * LEVELS * depth * width,
            bytes_accessed=2 * (weight.size + count * rows * LEVELS * depth),
            transcendentals=0,
        ),
        name="project",
    )(*blocks, weight)


def place_kernel(meta_ref, *refs):
    *group_refs, keep_ref, send_ref, token_ref = refs
    core, x, y = meta_ref[0], meta_ref[1], meta_ref[2]
    rows = group_refs[0].shape[1]
    total = rows * X * Y
    edge = jnp.zeros((HALO, token_ref.shape[1]), jnp.float32)
    token_ref[pl.ds(0, HALO), :] = edge
    token_ref[pl.ds(HALO + total, HALO), :] = edge
    for second, group_ref in zip((0, 1, 2, 3), group_refs):
        for first in range(4):
            dx = jnp.where(core == 0, first, second)
            dy = jnp.where(core == 0, second, first)
            e = lax.rem(x + dx, X) * Y + lax.rem(y + dy, Y)
            at = pl.multiple_of(e * rows + HALO, 8)
            token_ref[pl.ds(at, rows), :] = group_ref[first].astype(jnp.float32)
    piece = total // (ZL * CORES)
    for zl in range(ZL):
        for out_ref, whose in ((keep_ref, core), (send_ref, 1 - core)):
            at = pl.multiple_of((zl * CORES + whose) * piece, 8)
            out_ref[zl] = token_ref[pl.ds(at, piece + 2 * HALO), :].astype(jnp.bfloat16)


def place(groups, core, x, y):
    _, rows, width = groups[0].shape
    total = rows * X * Y
    pieces = jax.ShapeDtypeStruct((ZL, total // (ZL * CORES) + 2 * HALO, width), jnp.bfloat16)
    return pl.pallas_call(
        place_kernel,
        out_shape=(pieces, pieces),
        in_specs=[SMEM] + [VMEM] * 4,
        out_specs=(VMEM, VMEM),
        scratch_shapes=[pltpu.VMEM((total + 2 * HALO, width), jnp.float32)],
        compiler_params=PARAMS,
        cost_estimate=pl.CostEstimate(
            flops=total * width, bytes_accessed=4 * total * width, transcendentals=0
        ),
        name="place",
    )(jnp.stack([core, x, y]), *groups)


def join_kernel(meta_ref, keep_ref, got_ref, own_ref, *away_refs):
    zl = meta_ref[0]

    def piece(index):
        return keep_ref[index].astype(jnp.float32) + got_ref[index].astype(jnp.float32)

    own_ref[...] = piece(zl).astype(jnp.bfloat16)
    for step, away_ref in zip((1, 2, 3), away_refs):
        away_ref[...] = piece(lax.rem(zl + ZL - step, ZL)).astype(jnp.bfloat16)


def join(keep, got, zl):
    piece = jax.ShapeDtypeStruct(keep.shape[1:], jnp.bfloat16)
    return pl.pallas_call(
        join_kernel,
        out_shape=(piece,) * ZL,
        in_specs=[SMEM, VMEM, VMEM],
        out_specs=(VMEM,) * ZL,
        compiler_params=PARAMS,
        cost_estimate=pl.CostEstimate(
            flops=keep.size, bytes_accessed=6 * keep.size, transcendentals=0
        ),
        name="join",
    )(zl.reshape(1), keep, got)


def sigmoid(v):
    return 1.0 / (1.0 + jnp.exp(-v))


def chain_kernel(meta_ref, scale_ref, *refs):
    *part_refs, high_ref, gain_ref, grad_ref = refs
    rows, width = part_refs[0].shape
    own = rows - 2 * HALO
    joined = part_refs[0][...].astype(jnp.float32)
    for part_ref in part_refs[1:]:
        joined = joined + part_ref[...].astype(jnp.float32)
    high = high_ref[...].astype(jnp.float32)
    gain = gain_ref[...]
    scale = scale_ref[0]
    start, length = meta_ref[0], meta_ref[1]
    position = start - HALO + lax.broadcasted_iota(jnp.int32, (rows, width), 0)

    def down(values):
        return jnp.concatenate([jnp.zeros((1, width), jnp.float32), values[:-1]], axis=0)

    def up(values):
        return jnp.concatenate([values[1:], jnp.zeros((1, width), jnp.float32)], axis=0)

    def target(step):
        lead = jnp.zeros((HALO - step, width), jnp.float32)
        return jnp.concatenate([lead, high[: rows - HALO + step]], axis=0)

    def state_and_slope(v):
        gate = sigmoid(v)
        return v * gate, gate * (1.0 + v * (1.0 - gate))

    def residual(state, step):
        return jnp.where(position + step < length, scale * (state - target(step)), 0.0)

    state_1, slope_1 = state_and_slope(joined)
    before_1 = down(state_1)
    state_2, slope_2 = state_and_slope(joined + gain * before_1)
    before_2 = down(state_2)
    state_3, slope_3 = state_and_slope(joined + gain * before_2)
    delta_3 = residual(state_3, 3) * slope_3
    delta_2 = (residual(state_2, 2) + up(gain * delta_3)) * slope_2
    delta_1 = (residual(state_1, 1) + up(gain * delta_2)) * slope_1
    total = delta_1 + delta_2 + delta_3
    mix = (delta_2 * before_1 + delta_3 * before_2)[HALO : HALO + own]
    rest = jnp.sum(mix, axis=0, keepdims=True)
    tail = []
    for _ in range(3):
        term = rest.astype(jnp.bfloat16).astype(jnp.float32)
        tail.append(term)
        rest = rest - term
    tail.append(jnp.zeros((TAIL - 3, width), jnp.float32))
    grad_ref[pl.ds(0, own), :] = total[HALO : HALO + own].astype(jnp.bfloat16)
    grad_ref[pl.ds(own, TAIL), :] = jnp.concatenate(tail, axis=0).astype(jnp.bfloat16)


def chain(parts, high, gain, start, length, scale):
    rows, width = parts[0].shape
    own = rows - 2 * HALO
    return pl.pallas_call(
        chain_kernel,
        out_shape=jax.ShapeDtypeStruct((own + TAIL, width), jnp.bfloat16),
        in_specs=[SMEM, SMEM] + [VMEM] * (len(parts) + 2),
        out_specs=VMEM,
        compiler_params=PARAMS,
        cost_estimate=pl.CostEstimate(
            flops=60 * rows * width, bytes_accessed=10 * rows * width, transcendentals=3 * rows * width
        ),
        name="chain",
    )(jnp.stack([start, length]), scale.reshape(1), *parts, high, gain.reshape(1, width))


def pieces_of(zl, core):
    found = []
    for step, other in ((0, 0), (0, 1), (1, 0), (-1, 0), (1, 1), (-1, 1), (2, 0), (2, 1)):
        found.append(lax.rem(zl + step + ZL, ZL) * CORES + (1 - core if other else core))
    return found


def weight_grad_kernel(meta_ref, features_ref, *refs):
    *group_refs, out_ref, mix_ref, grads_ref = refs
    zl, zh, core = meta_ref[0], meta_ref[1], meta_ref[2]
    half = grads_ref.shape[1] // ZH
    width = grads_ref.shape[2]

    @pl.when(pl.program_id(0) == 0)
    def _():
        mix = jnp.zeros((TAIL, width), jnp.float32)
        for group_ref, member in zip(group_refs, pieces_of(zl, core)):
            for sequence in range(ZH):
                slot = pl.ds(pl.multiple_of(lax.rem(sequence - zh + ZH, ZH) * half, 16), half)
                for part in range(2):
                    rows = group_ref[sequence, pl.ds(part * half, half), :]
                    grads_ref[member * 2 + part, slot, :] = rows
                mix = mix + group_ref[sequence, pl.ds(2 * half, TAIL), :].astype(jnp.float32)
        mix_ref[...] = jnp.sum(mix, axis=0, keepdims=True)

    blocks = features_ref.shape[0]
    left = jnp.concatenate([features_ref[e, 0] for e in range(blocks)], axis=1)
    right = grads_ref[...].reshape(-1, width)
    out_ref[0] = jnp.dot(left, right, preferred_element_type=jnp.float32).astype(jnp.bfloat16)


def weight_grad(features, groups, zl, zh, core):
    draft, _, columns, tokens = features.shape
    width = groups[0].shape[2]
    whole = [pl.BlockSpec(g.shape, lambda l: (0, 0, 0)) for g in groups]
    return pl.pallas_call(
        weight_grad_kernel,
        grid=(LEVELS,),
        out_shape=(
            jax.ShapeDtypeStruct((LEVELS, columns, width), jnp.bfloat16),
            jax.ShapeDtypeStruct((1, width), jnp.float32),
        ),
        in_specs=[SMEM, pl.BlockSpec((draft, 1, columns, tokens), lambda l: (0, l, 0, 0))] + whole,
        out_specs=(
            pl.BlockSpec((1, columns, width), lambda l: (l, 0, 0)),
            pl.BlockSpec((1, width), lambda l: (0, 0)),
        ),
        scratch_shapes=[pltpu.VMEM((draft, tokens, width), jnp.bfloat16)],
        compiler_params=PARAMS,
        cost_estimate=pl.CostEstimate(
            flops=2 * draft * LEVELS * columns * tokens * width,
            bytes_accessed=2 * features.size + 2 * draft * tokens * width,
            transcendentals=0,
        ),
        name="weight_grad",
    )(jnp.stack([zl, zh, core]), features, *groups)


def valid_total(lengths):
    running = jnp.zeros((), jnp.float32)
    for unroll in range(1, UNROLL + 1):
        running = running + jnp.sum(jnp.maximum(lengths - unroll, 0)).astype(jnp.float32)
    return running


def high_halves(top, draft_index):
    members, draft_count = ZL * CORES, X * Y
    width = top.shape[1] // 2
    even = draft_index % 2 == 0
    left, right = top[:, :width], top[:, width:]
    first, second = [], []
    for t in range(members):
        for e in range(draft_count):
            target = e // 2 * draft_count + 2 * t
            first.append((t * draft_count + e, target + e % 2))
            second.append((t * draft_count + e, target + 1 - e % 2))
    axes = ("tp", "draft")
    one = lax.ppermute(jnp.where(even, left, right), axes, first)
    two = lax.ppermute(jnp.where(even, right, left), axes, second)
    return one, two


def high_rows(one, two, draft_index):
    even = draft_index % 2 == 0
    return jnp.concatenate([jnp.where(even, one, two), jnp.where(even, two, one)], axis=0)


def high_after(rows):
    return lax.ppermute(rows[:TAIL], "tp", [(j, j - 1) for j in range(1, ZL * CORES)])


def trade_quarter(own, zh, step):
    part = own.shape[2] // ZH
    quarter = lax.dynamic_slice_in_dim(own, (zh + ZH - step) % ZH * part, part, 2)
    return from_zh(quarter, step) if step else quarter


def gather_grads(grad):
    stack = lax.all_gather(grad, "dp", axis=0, tiled=False)
    above, below, other = from_z(stack, 1), from_z(stack, -1), from_other_core(stack)
    above, below, other = lax.optimization_barrier((above, below, other))
    far_above, far_below = from_z(above[:2], 1), from_z(below[2:], -1)
    other_above, other_below = from_other_core(above), from_other_core(below)
    far, other_above, other_below = lax.optimization_barrier(
        (jnp.concatenate([far_above, far_below]), other_above, other_below)
    )
    return [stack, other, above, below, other_above, other_below, far, from_other_core(far)]


def local(features, fc_weight, mix_gain, lengths):
    tp_index, zh = lax.axis_index("tp"), lax.axis_index("dp")
    draft_index = lax.axis_index("draft")
    zl, core = tp_index // CORES, tp_index % CORES
    x, y = draft_index // Y, draft_index % Y
    own_rows = features.shape[0]
    piece = own_rows * X * Y // (ZL * CORES)
    own = features.transpose(1, 0, 2)
    weight = fc_weight.transpose(1, 0, 2)

    next_, last, across = (plane_move(step, True)(own) for step in (1, 3, 2))
    trades = [trade_quarter(own, zh, 0), trade_quarter(own, zh, 1)]
    next_, last, across, trades, later = lax.optimization_barrier((next_, last, across, trades, own))
    low, high = jnp.stack([own, next_]), jnp.stack([across, last])
    up_low, down_high = plane_move(1, False)(low), plane_move(-1, False)(high)
    up_high, down_low = plane_move(1, False)(high), plane_move(-1, False)(low)
    trades += [trade_quarter(later, zh, 2), trade_quarter(later, zh, 3)]
    zero = project([low, high], weight)
    up_low, down_high, trades, zero, later = lax.optimization_barrier(
        (up_low, down_high, trades, zero, later)
    )
    far_low, far_high = plane_move(1, False)(up_low), plane_move(-1, False)(down_high)
    halves = high_halves(later[LEVELS - 1], draft_index)
    traded = jnp.concatenate([t.transpose(0, 2, 1) for t in trades], axis=2)
    one, three = project([up_low, up_high], weight), project([down_low, down_high], weight)
    far_low, far_high, traded, one, three, halves = lax.optimization_barrier(
        (far_low, far_high, traded, one, three, halves)
    )
    every = lax.all_gather(traded, "draft", axis=0, tiled=False)
    groups = [zero, one, project([far_low, far_high], weight), three]
    target = high_rows(*halves, draft_index)

    keep, send = place(groups, core, x, y)
    got, after = lax.optimization_barrier((from_other_core(send), high_after(target)))
    mine, *away = join(keep, got, zl)
    parts = [mine] + [from_zl(block, step) for step, block in zip((1, 2, 3), away)]
    scale = LOSS_SCALE / valid_total(lengths)
    target = jnp.concatenate([target, after], axis=0)
    grad = chain(parts, target, mix_gain, tp_index * piece, lengths[zh], scale)
    fc_grad, mix_total = weight_grad(every, gather_grads(grad), zl, zh, core)
    return (fc_grad.transpose(1, 0, 2), mix_total[0])


def solution(mesh):
    placed = (P(("dp", "draft"), None, "tp"), P("tp", None, "draft"), P("draft"), P())
    return jax.shard_map(
        local,
        mesh=mesh,
        in_specs=placed,
        out_specs=(P(("tp", "dp"), None, "draft"), P("draft")),
        check_vma=False,
    )
```

```python
import jax
import jax.numpy as jnp
from jax import lax
from jax.experimental import pallas as pl
from jax.experimental.pallas import tpu as pltpu
from jax.sharding import PartitionSpec as P

LEVELS = 3
UNROLL = 3
LOSS_SCALE = 64.0
HALO = 8
TAIL = 16
X, Y = 4, 4
ZL, CORES, ZH = 4, 2, 4
VMEM = pl.BlockSpec(memory_space=pltpu.VMEM)
SMEM = pl.BlockSpec(memory_space=pltpu.SMEM)


def params(mebibytes):
    return pltpu.CompilerParams(vmem_limit_bytes=mebibytes << 20)


def plane_move(step, first):
    pairs = []
    for t in range(ZL * CORES):
        for x in range(X):
            for y in range(Y):
                along_x = (t % CORES == 0) == first
                source = (x + step) % X * Y + y if along_x else x * Y + (y + step) % Y
                pairs.append((t * X * Y + source, t * X * Y + x * Y + y))
    return lambda block: lax.ppermute(block, ("tp", "draft"), pairs)


def from_other_core(block):
    return lax.ppermute(block, "tp", [(t ^ 1, t) for t in range(ZL * CORES)])


def from_zl(block, step):
    pairs = [((t // CORES + step) % ZL * CORES + t % CORES, t) for t in range(ZL * CORES)]
    return lax.ppermute(block, "tp", pairs)


def from_zh(block, step):
    return lax.ppermute(block, "dp", [((s + step) % ZH, s) for s in range(ZH)])


def from_z(block, step):
    pairs = []
    for t in range(ZL * CORES):
        for s in range(ZH):
            z = (s * ZL + t // CORES + step) % (ZL * ZH)
            pairs.append((((z % ZL) * CORES + t % CORES) * ZH + z // ZL, t * ZH + s))
    return lax.ppermute(block, ("tp", "dp"), pairs)


def project_kernel(*refs):
    *block_refs, weight_ref, out_ref, total_ref = refs
    level = pl.program_id(0)
    rows = jnp.concatenate([r[...].reshape(-1, r.shape[-1]) for r in block_refs], axis=0)
    term = jnp.dot(rows, weight_ref[0], preferred_element_type=jnp.float32)

    @pl.when(level == 0)
    def _():
        total_ref[...] = term

    @pl.when(level > 0)
    def _():
        total_ref[...] += term

    @pl.when(level == LEVELS - 1)
    def _():
        out_ref[...] = total_ref[...].astype(jnp.bfloat16).reshape(out_ref.shape)


def project(blocks, weight):
    _, _, rows, depth = blocks[0].shape
    count = sum(b.shape[0] for b in blocks)
    width = weight.shape[2]
    return pl.pallas_call(
        project_kernel,
        grid=(LEVELS,),
        out_shape=jax.ShapeDtypeStruct((count, rows, width), jnp.bfloat16),
        in_specs=[
            pl.BlockSpec((b.shape[0], 1, rows, depth), lambda l: (0, l, 0, 0)) for b in blocks
        ]
        + [pl.BlockSpec((1, depth, width), lambda l: (l, 0, 0))],
        out_specs=pl.BlockSpec((count, rows, width), lambda l: (0, 0, 0)),
        scratch_shapes=[pltpu.VMEM((count * rows, width), jnp.float32)],
        compiler_params=params(12),
        cost_estimate=pl.CostEstimate(
            flops=2 * count * rows * LEVELS * depth * width,
            bytes_accessed=2 * (weight.size + count * rows * LEVELS * depth),
            transcendentals=0,
        ),
        name="project",
    )(*blocks, weight)


def place_kernel(meta_ref, *refs):
    *group_refs, keep_ref, send_ref, token_ref = refs
    core, x, y = meta_ref[0], meta_ref[1], meta_ref[2]
    rows = group_refs[0].shape[1]
    total = rows * X * Y
    edge = jnp.zeros((HALO, token_ref.shape[1]), jnp.float32)
    token_ref[pl.ds(0, HALO), :] = edge
    token_ref[pl.ds(HALO + total, HALO), :] = edge
    for second, group_ref in zip((0, 1, 2, 3), group_refs):
        for first in range(4):
            dx = jnp.where(core == 0, first, second)
            dy = jnp.where(core == 0, second, first)
            e = lax.rem(x + dx, X) * Y + lax.rem(y + dy, Y)
            at = pl.multiple_of(e * rows + HALO, 8)
            token_ref[pl.ds(at, rows), :] = group_ref[first].astype(jnp.float32)
    piece = total // (ZL * CORES)
    for zl in range(ZL):
        for out_ref, whose in ((keep_ref, core), (send_ref, 1 - core)):
            at = pl.multiple_of((zl * CORES + whose) * piece, 8)
            out_ref[zl] = token_ref[pl.ds(at, piece + 2 * HALO), :].astype(jnp.bfloat16)


def place(groups, core, x, y):
    _, rows, width = groups[0].shape
    total = rows * X * Y
    pieces = jax.ShapeDtypeStruct((ZL, total // (ZL * CORES) + 2 * HALO, width), jnp.bfloat16)
    return pl.pallas_call(
        place_kernel,
        out_shape=(pieces, pieces),
        in_specs=[SMEM] + [VMEM] * 4,
        out_specs=(VMEM, VMEM),
        scratch_shapes=[pltpu.VMEM((total + 2 * HALO, width), jnp.float32)],
        compiler_params=params(12),
        cost_estimate=pl.CostEstimate(
            flops=total * width, bytes_accessed=4 * total * width, transcendentals=0
        ),
        name="place",
    )(jnp.stack([core, x, y]), *groups)


def join_kernel(meta_ref, keep_ref, got_ref, own_ref, *away_refs):
    zl = meta_ref[0]

    def piece(index):
        return keep_ref[index].astype(jnp.float32) + got_ref[index].astype(jnp.float32)

    own_ref[...] = piece(zl).astype(jnp.bfloat16)
    for step, away_ref in zip((1, 2, 3), away_refs):
        away_ref[...] = piece(lax.rem(zl + ZL - step, ZL)).astype(jnp.bfloat16)


def join(keep, got, zl):
    piece = jax.ShapeDtypeStruct(keep.shape[1:], jnp.bfloat16)
    return pl.pallas_call(
        join_kernel,
        out_shape=(piece,) * ZL,
        in_specs=[SMEM, VMEM, VMEM],
        out_specs=(VMEM,) * ZL,
        compiler_params=params(8),
        cost_estimate=pl.CostEstimate(
            flops=keep.size, bytes_accessed=6 * keep.size, transcendentals=0
        ),
        name="join",
    )(zl.reshape(1), keep, got)


def sigmoid(v):
    return 1.0 / (1.0 + jnp.exp(-v))


def chain_kernel(meta_ref, scale_ref, *refs):
    *part_refs, high_ref, gain_ref, grad_ref = refs
    rows, width = part_refs[0].shape
    own = rows - 2 * HALO
    joined = part_refs[0][...].astype(jnp.float32)
    for part_ref in part_refs[1:]:
        joined = joined + part_ref[...].astype(jnp.float32)
    high = high_ref[...].astype(jnp.float32)
    gain = gain_ref[...]
    scale = scale_ref[0]
    start, length = meta_ref[0], meta_ref[1]
    position = start - HALO + lax.broadcasted_iota(jnp.int32, (rows, width), 0)

    def down(values):
        return jnp.concatenate([jnp.zeros((1, width), jnp.float32), values[:-1]], axis=0)

    def up(values):
        return jnp.concatenate([values[1:], jnp.zeros((1, width), jnp.float32)], axis=0)

    def target(step):
        lead = jnp.zeros((HALO - step, width), jnp.float32)
        return jnp.concatenate([lead, high[: rows - HALO + step]], axis=0)

    def state_and_slope(v):
        gate = sigmoid(v)
        return v * gate, gate * (1.0 + v * (1.0 - gate))

    def residual(state, step):
        return jnp.where(position + step < length, scale * (state - target(step)), 0.0)

    state_1, slope_1 = state_and_slope(joined)
    before_1 = down(state_1)
    state_2, slope_2 = state_and_slope(joined + gain * before_1)
    before_2 = down(state_2)
    state_3, slope_3 = state_and_slope(joined + gain * before_2)
    delta_3 = residual(state_3, 3) * slope_3
    delta_2 = (residual(state_2, 2) + up(gain * delta_3)) * slope_2
    delta_1 = (residual(state_1, 1) + up(gain * delta_2)) * slope_1
    total = delta_1 + delta_2 + delta_3
    mix = (delta_2 * before_1 + delta_3 * before_2)[HALO : HALO + own]
    rest = jnp.sum(mix, axis=0, keepdims=True)
    tail = []
    for _ in range(3):
        term = rest.astype(jnp.bfloat16).astype(jnp.float32)
        tail.append(term)
        rest = rest - term
    tail.append(jnp.zeros((TAIL - 3, width), jnp.float32))
    grad_ref[pl.ds(0, own), :] = total[HALO : HALO + own].astype(jnp.bfloat16)
    grad_ref[pl.ds(own, TAIL), :] = jnp.concatenate(tail, axis=0).astype(jnp.bfloat16)


def chain(parts, high, gain, start, length, scale):
    rows, width = parts[0].shape
    own = rows - 2 * HALO
    return pl.pallas_call(
        chain_kernel,
        out_shape=jax.ShapeDtypeStruct((own + TAIL, width), jnp.bfloat16),
        in_specs=[SMEM, SMEM] + [VMEM] * (len(parts) + 2),
        out_specs=VMEM,
        compiler_params=params(14),
        cost_estimate=pl.CostEstimate(
            flops=60 * rows * width, bytes_accessed=10 * rows * width, transcendentals=3 * rows * width
        ),
        name="chain",
    )(jnp.stack([start, length]), scale.reshape(1), *parts, high, gain.reshape(1, width))


def pieces_of(zl, core):
    found = []
    for step, other in ((0, 0), (0, 1), (1, 0), (-1, 0), (1, 1), (-1, 1), (2, 0), (2, 1)):
        found.append(lax.rem(zl + step + ZL, ZL) * CORES + (1 - core if other else core))
    return found


def weight_grad_kernel(meta_ref, features_ref, *refs):
    *group_refs, out_ref, mix_ref, grads_ref = refs
    zl, core = meta_ref[0], meta_ref[1]
    half = grads_ref.shape[1] // ZH
    width = grads_ref.shape[2]

    @pl.when(pl.program_id(0) == 0)
    def _():
        mix = jnp.zeros((TAIL, width), jnp.float32)
        for group_ref, member in zip(group_refs, pieces_of(zl, core)):
            for sequence in range(ZH):
                slot = pl.ds(sequence * half, half)
                for part in range(2):
                    rows = group_ref[sequence, pl.ds(part * half, half), :]
                    grads_ref[member * 2 + part, slot, :] = rows
                mix = mix + group_ref[sequence, pl.ds(2 * half, TAIL), :].astype(jnp.float32)
        mix_ref[...] = jnp.sum(mix, axis=0, keepdims=True)

    blocks = features_ref.shape[0]
    left = jnp.concatenate([features_ref[e, 0] for e in range(blocks)], axis=1)
    right = grads_ref[...].reshape(-1, width)
    out_ref[0] = jnp.dot(left, right, preferred_element_type=jnp.float32).astype(jnp.bfloat16)


def weight_grad(features, groups, zl, core):
    draft, _, columns, tokens = features.shape
    width = groups[0].shape[2]
    return pl.pallas_call(
        weight_grad_kernel,
        grid=(LEVELS,),
        out_shape=(
            jax.ShapeDtypeStruct((LEVELS, columns, width), jnp.bfloat16),
            jax.ShapeDtypeStruct((1, width), jnp.float32),
        ),
        in_specs=[SMEM, pl.BlockSpec((draft, 1, columns, tokens), lambda l: (0, l, 0, 0))]
        + [VMEM] * len(groups),
        out_specs=(
            pl.BlockSpec((1, columns, width), lambda l: (l, 0, 0)),
            pl.BlockSpec((1, width), lambda l: (0, 0)),
        ),
        scratch_shapes=[pltpu.VMEM((draft, tokens, width), jnp.bfloat16)],
        compiler_params=params(26),
        cost_estimate=pl.CostEstimate(
            flops=2 * draft * LEVELS * columns * tokens * width,
            bytes_accessed=2 * features.size + 2 * draft * tokens * width,
            transcendentals=0,
        ),
        name="weight_grad",
    )(jnp.stack([zl, core]), features, *groups)


def valid_total(lengths):
    running = jnp.zeros((), jnp.float32)
    for unroll in range(1, UNROLL + 1):
        running = running + jnp.sum(jnp.maximum(lengths - unroll, 0)).astype(jnp.float32)
    return running


def high_halves(top, draft_index):
    members, draft_count = ZL * CORES, X * Y
    width = top.shape[1] // 2
    even = draft_index % 2 == 0
    left, right = top[:, :width], top[:, width:]
    first, second = [], []
    for t in range(members):
        for e in range(draft_count):
            target = e // 2 * draft_count + 2 * t
            first.append((t * draft_count + e, target + e % 2))
            second.append((t * draft_count + e, target + 1 - e % 2))
    axes = ("tp", "draft")
    one = lax.ppermute(jnp.where(even, left, right), axes, first)
    two = lax.ppermute(jnp.where(even, right, left), axes, second)
    return one, two


def high_rows(one, two, draft_index):
    even = draft_index % 2 == 0
    first = jnp.where(even, one, two)[:-TAIL]
    return jnp.concatenate([first, jnp.where(even, two, one)], axis=0)


def rows_ahead(top):
    return lax.ppermute(top[:TAIL], "draft", [(e, e - 1) for e in range(1, X * Y)])


def trade_columns(own):
    levels, rows, depth = own.shape
    quarters = own.reshape(levels, rows, ZH, depth // ZH).transpose(2, 0, 1, 3)
    return lax.all_to_all(quarters, "dp", split_axis=0, concat_axis=0, tiled=True)


def gather_grads(grad):
    stack = lax.all_gather(grad, "dp", axis=0, tiled=False)
    above, below = from_z(stack, 1), from_z(stack, -1)
    far = [from_z(stack[:2], 2), from_z(stack[2:], -2)]
    other = from_other_core(stack)
    above, below, other = lax.optimization_barrier((above, below, other))
    other_above, other_below = from_other_core(above), from_other_core(below)
    far = jnp.concatenate(far)
    return [stack, other, above, below, other_above, other_below, far, from_other_core(far)]


def local(features, fc_weight, mix_gain, lengths):
    tp_index, zh = lax.axis_index("tp"), lax.axis_index("dp")
    draft_index = lax.axis_index("draft")
    zl, core = tp_index // CORES, tp_index % CORES
    x, y = draft_index // Y, draft_index % Y
    own_rows = features.shape[0]
    piece = own_rows * X * Y // (ZL * CORES)
    own = features.transpose(1, 0, 2)
    weight = fc_weight.transpose(1, 0, 2)

    next_, last, across = (plane_move(step, True)(own) for step in (1, 3, 2))
    traded = trade_columns(own)
    ahead = rows_ahead(own[LEVELS - 1])
    next_, last, across, ahead, later = lax.optimization_barrier((next_, last, across, ahead, own))
    low, high = jnp.stack([own, next_]), jnp.stack([across, last])
    up_low, down_high = plane_move(1, False)(low), plane_move(-1, False)(high)
    up_high, down_low = plane_move(1, False)(high), plane_move(-1, False)(low)
    zero = project([low, high], weight)
    up_low, down_high, traded, zero, later = lax.optimization_barrier(
        (up_low, down_high, traded, zero, later)
    )
    far_low, far_high = plane_move(1, False)(up_low), plane_move(-1, False)(down_high)
    halves = high_halves(jnp.concatenate([later[LEVELS - 1], ahead], axis=0), draft_index)
    traded = traded.transpose(1, 3, 0, 2).reshape(LEVELS, traded.shape[3], -1)
    one, three = project([up_low, up_high], weight), project([down_low, down_high], weight)
    far_low, far_high, traded, one, three, halves = lax.optimization_barrier(
        (far_low, far_high, traded, one, three, halves)
    )
    every = lax.all_gather(traded, "draft", axis=0, tiled=False)
    groups = [zero, one, project([far_low, far_high], weight), three]

    keep, send = place(groups, core, x, y)
    mine, *away = join(keep, from_other_core(send), zl)
    parts = [mine] + [from_zl(block, step) for step, block in zip((1, 2, 3), away)]
    scale = LOSS_SCALE / valid_total(lengths)
    target = high_rows(*halves, draft_index)
    grad = chain(parts, target, mix_gain, tp_index * piece, lengths[zh], scale)
    fc_grad, mix_total = weight_grad(every, gather_grads(grad), zl, core)
    return (fc_grad.transpose(1, 0, 2), mix_total[0])


def solution(mesh):
    placed = (P(("dp", "draft"), None, "tp"), P("tp", None, "draft"), P("draft"), P())
    return jax.shard_map(
        local,
        mesh=mesh,
        in_specs=placed,
        out_specs=(P(("tp", "dp"), None, "draft"), P("draft")),
        check_vma=False,
    )
```

```python
import jax
import jax.numpy as jnp
from jax import lax
from jax.experimental import pallas as pl
from jax.experimental.pallas import tpu as pltpu
from jax.sharding import PartitionSpec as P

LEVELS = 3
UNROLL = 3
LOSS_SCALE = 64.0
HALO = 8
TAIL = 16
X, Y = 4, 4
ZL, CORES, ZH = 4, 2, 4
VMEM = pl.BlockSpec(memory_space=pltpu.VMEM)
SMEM = pl.BlockSpec(memory_space=pltpu.SMEM)


def params(mebibytes):
    return pltpu.CompilerParams(vmem_limit_bytes=mebibytes << 20)


def plane_move(step, first):
    pairs = []
    for t in range(ZL * CORES):
        for x in range(X):
            for y in range(Y):
                along_x = (t % CORES == 0) == first
                source = (x + step) % X * Y + y if along_x else x * Y + (y + step) % Y
                pairs.append((t * X * Y + source, t * X * Y + x * Y + y))
    return lambda block: lax.ppermute(block, ("tp", "draft"), pairs)


def from_other_core(block):
    return lax.ppermute(block, "tp", [(t ^ 1, t) for t in range(ZL * CORES)])


def from_zl(block, step):
    pairs = [((t // CORES + step) % ZL * CORES + t % CORES, t) for t in range(ZL * CORES)]
    return lax.ppermute(block, "tp", pairs)


def from_zh(block, step):
    return lax.ppermute(block, "dp", [((s + step) % ZH, s) for s in range(ZH)])


def from_z(block, step):
    pairs = []
    for t in range(ZL * CORES):
        for s in range(ZH):
            z = (s * ZL + t // CORES + step) % (ZL * ZH)
            pairs.append((((z % ZL) * CORES + t % CORES) * ZH + z // ZL, t * ZH + s))
    return lax.ppermute(block, ("tp", "dp"), pairs)


def pair_kernel(first_ref, second_ref, out_ref, sem):
    first = pltpu.make_async_copy(first_ref, out_ref.at[0], sem.at[0])
    second = pltpu.make_async_copy(second_ref, out_ref.at[1], sem.at[1])
    first.start()
    second.start()
    first.wait()
    second.wait()


def pair(first, second):
    anywhere = pl.BlockSpec(memory_space=pl.ANY)
    return pl.pallas_call(
        pair_kernel,
        out_shape=jax.ShapeDtypeStruct((2,) + first.shape, first.dtype),
        in_specs=[anywhere] * 2,
        out_specs=anywhere,
        scratch_shapes=[pltpu.SemaphoreType.DMA((2,))],
        cost_estimate=pl.CostEstimate(flops=0, bytes_accessed=8 * first.size, transcendentals=0),
        name="pair",
    )(first, second)


def rows_of(block_refs):
    return jnp.concatenate([r[...].reshape(-1, r.shape[-1]) for r in block_refs], axis=0)


def accumulate(total_ref, term):
    level = pl.program_id(0)

    @pl.when(level == 0)
    def _():
        total_ref[...] = term

    @pl.when(level > 0)
    def _():
        total_ref[...] += term


def project_kernel(*refs):
    *block_refs, weight_ref, out_ref, total_ref = refs
    accumulate(
        total_ref, jnp.dot(rows_of(block_refs), weight_ref[0], preferred_element_type=jnp.float32)
    )

    @pl.when(pl.program_id(0) == LEVELS - 1)
    def _():
        out_ref[...] = total_ref[...].astype(jnp.bfloat16).reshape(out_ref.shape)


def product_specs(blocks, weight):
    _, _, rows, depth = blocks[0].shape
    specs = [pl.BlockSpec((b.shape[0], 1, rows, depth), lambda l, *_: (0, l, 0, 0)) for b in blocks]
    return specs + [pl.BlockSpec((1, depth, weight.shape[2]), lambda l, *_: (l, 0, 0))]


def product_cost(blocks, weight):
    size = sum(b.size for b in blocks)
    return pl.CostEstimate(
        flops=2 * size * weight.shape[2], bytes_accessed=2 * (weight.size + size), transcendentals=0
    )


def project(blocks, weight):
    rows, width = blocks[0].shape[2], weight.shape[2]
    count = sum(b.shape[0] for b in blocks)
    return pl.pallas_call(
        project_kernel,
        grid=(LEVELS,),
        out_shape=jax.ShapeDtypeStruct((count, rows, width), jnp.bfloat16),
        in_specs=product_specs(blocks, weight),
        out_specs=pl.BlockSpec((count, rows, width), lambda l: (0, 0, 0)),
        scratch_shapes=[pltpu.VMEM((count * rows, width), jnp.float32)],
        compiler_params=params(14),
        cost_estimate=product_cost(blocks, weight),
        name="project",
    )(*blocks, weight)


def project_place_kernel(meta_ref, *refs):
    *block_refs, weight_ref, zero_ref, sides_ref, keep_ref, send_ref, total_ref, token_ref = refs
    accumulate(
        total_ref, jnp.dot(rows_of(block_refs), weight_ref[0], preferred_element_type=jnp.float32)
    )

    @pl.when(pl.program_id(0) == LEVELS - 1)
    def _():
        core, x, y = meta_ref[0], meta_ref[1], meta_ref[2]
        rows = zero_ref.shape[1]
        total = rows * X * Y
        edge = jnp.zeros((HALO, token_ref.shape[1]), jnp.float32)
        token_ref[pl.ds(0, HALO), :] = edge
        token_ref[pl.ds(HALO + total, HALO), :] = edge
        for second in range(4):
            for first in range(4):
                dx = jnp.where(core == 0, first, second)
                dy = jnp.where(core == 0, second, first)
                e = lax.rem(x + dx, X) * Y + lax.rem(y + dy, Y)
                at = pl.multiple_of(e * rows + HALO, 8)
                if second == 0:
                    block = zero_ref[first].astype(jnp.float32)
                elif second == 2:
                    block = total_ref[pl.ds(first * rows, rows), :]
                else:
                    block = sides_ref[second // 2 * 4 + first].astype(jnp.float32)
                token_ref[pl.ds(at, rows), :] = block
        piece = total // (ZL * CORES)
        for zl in range(ZL):
            for out_ref, whose in ((keep_ref, core), (send_ref, 1 - core)):
                at = pl.multiple_of((zl * CORES + whose) * piece, 8)
                out_ref[zl] = token_ref[pl.ds(at, piece + 2 * HALO), :].astype(jnp.bfloat16)


def project_place(blocks, weight, zero, sides, core, x, y):
    _, rows, width = zero.shape
    count = sum(b.shape[0] for b in blocks)
    total = rows * X * Y
    pieces = (ZL, total // (ZL * CORES) + 2 * HALO, width)
    whole = lambda shape: pl.BlockSpec(shape, lambda l, *_: (0, 0, 0))
    return pl.pallas_call(
        project_place_kernel,
        out_shape=(jax.ShapeDtypeStruct(pieces, jnp.bfloat16),) * 2,
        grid_spec=pltpu.PrefetchScalarGridSpec(
            num_scalar_prefetch=1,
            grid=(LEVELS,),
            in_specs=product_specs(blocks, weight) + [whole(zero.shape), whole(sides.shape)],
            out_specs=(whole(pieces),) * 2,
            scratch_shapes=[
                pltpu.VMEM((count * rows, width), jnp.float32),
                pltpu.VMEM((total + 2 * HALO, width), jnp.float32),
            ],
        ),
        compiler_params=params(18),
        cost_estimate=product_cost(blocks, weight),
        name="project_place",
    )(jnp.stack([core, x, y]), *blocks, weight, zero, sides)


def join_kernel(meta_ref, keep_ref, got_ref, own_ref, *away_refs):
    zl = meta_ref[0]

    def piece(index):
        return keep_ref[index].astype(jnp.float32) + got_ref[index].astype(jnp.float32)

    own_ref[...] = piece(zl).astype(jnp.bfloat16)
    for step, away_ref in zip((1, 2, 3), away_refs):
        away_ref[...] = piece(lax.rem(zl + ZL - step, ZL)).astype(jnp.bfloat16)


def join(keep, got, zl):
    piece = jax.ShapeDtypeStruct(keep.shape[1:], jnp.bfloat16)
    return pl.pallas_call(
        join_kernel,
        out_shape=(piece,) * ZL,
        in_specs=[SMEM, VMEM, VMEM],
        out_specs=(VMEM,) * ZL,
        compiler_params=params(8),
        cost_estimate=pl.CostEstimate(
            flops=keep.size, bytes_accessed=6 * keep.size, transcendentals=0
        ),
        name="join",
    )(zl.reshape(1), keep, got)


def sigmoid(v):
    return 1.0 / (1.0 + jnp.exp(-v))


def chain_kernel(meta_ref, scale_ref, *refs):
    *part_refs, high_ref, gain_ref, grad_ref = refs
    rows, width = part_refs[0].shape
    own = rows - 2 * HALO
    joined = part_refs[0][...].astype(jnp.float32)
    for part_ref in part_refs[1:]:
        joined = joined + part_ref[...].astype(jnp.float32)
    high = high_ref[...].astype(jnp.float32)
    gain = gain_ref[...]
    scale = scale_ref[0]
    start, length = meta_ref[0], meta_ref[1]
    position = start - HALO + lax.broadcasted_iota(jnp.int32, (rows, width), 0)

    def down(values):
        return jnp.concatenate([jnp.zeros((1, width), jnp.float32), values[:-1]], axis=0)

    def up(values):
        return jnp.concatenate([values[1:], jnp.zeros((1, width), jnp.float32)], axis=0)

    def target(step):
        lead = jnp.zeros((HALO - step, width), jnp.float32)
        return jnp.concatenate([lead, high[: rows - HALO + step]], axis=0)

    def state_and_slope(v):
        gate = sigmoid(v)
        return v * gate, gate * (1.0 + v * (1.0 - gate))

    def residual(state, step):
        return jnp.where(position + step < length, scale * (state - target(step)), 0.0)

    state_1, slope_1 = state_and_slope(joined)
    before_1 = down(state_1)
    state_2, slope_2 = state_and_slope(joined + gain * before_1)
    before_2 = down(state_2)
    state_3, slope_3 = state_and_slope(joined + gain * before_2)
    delta_3 = residual(state_3, 3) * slope_3
    delta_2 = (residual(state_2, 2) + up(gain * delta_3)) * slope_2
    delta_1 = (residual(state_1, 1) + up(gain * delta_2)) * slope_1
    total = delta_1 + delta_2 + delta_3
    mix = (delta_2 * before_1 + delta_3 * before_2)[HALO : HALO + own]
    rest = jnp.sum(mix, axis=0, keepdims=True)
    tail = []
    for _ in range(3):
        term = rest.astype(jnp.bfloat16).astype(jnp.float32)
        tail.append(term)
        rest = rest - term
    tail.append(jnp.zeros((TAIL - 3, width), jnp.float32))
    grad_ref[pl.ds(0, own), :] = total[HALO : HALO + own].astype(jnp.bfloat16)
    grad_ref[pl.ds(own, TAIL), :] = jnp.concatenate(tail, axis=0).astype(jnp.bfloat16)


def chain(parts, high, gain, start, length, scale):
    rows, width = parts[0].shape
    own = rows - 2 * HALO
    return pl.pallas_call(
        chain_kernel,
        out_shape=jax.ShapeDtypeStruct((own + TAIL, width), jnp.bfloat16),
        in_specs=[SMEM, SMEM] + [VMEM] * (len(parts) + 2),
        out_specs=VMEM,
        compiler_params=params(14),
        cost_estimate=pl.CostEstimate(
            flops=60 * rows * width, bytes_accessed=10 * rows * width, transcendentals=3 * rows * width
        ),
        name="chain",
    )(jnp.stack([start, length]), scale.reshape(1), *parts, high, gain.reshape(1, width))


def pieces_of(zl, core):
    found = []
    for step, other in ((0, 0), (0, 1), (1, 0), (-1, 0), (1, 1), (-1, 1), (2, 0), (2, 1)):
        found.append(lax.rem(zl + step + ZL, ZL) * CORES + (1 - core if other else core))
    return found


def weight_grad_kernel(meta_ref, features_ref, *refs):
    *group_refs, out_ref, mix_ref, grads_ref, tail_ref, held_ref, sem, held_sem = refs
    level = pl.program_id(0)
    zl, core = meta_ref[0], meta_ref[1]
    half = grads_ref.shape[1] // ZH
    width = grads_ref.shape[2]

    def held(at):
        return pltpu.make_async_copy(features_ref.at[:, at], held_ref.at[at], held_sem.at[at])

    @pl.when(level == 0)
    def _():
        copies = []
        for group, (group_ref, member) in enumerate(zip(group_refs, pieces_of(zl, core))):
            for sequence in range(ZH):
                for part in range(2):
                    rows = group_ref.at[sequence, pl.ds(part * half, half), :]
                    slot = grads_ref.at[member * 2 + part, pl.ds(sequence * half, half), :]
                    copies.append((rows, slot))
            rows = group_ref.at[:, pl.ds(2 * half, TAIL), :]
            copies.append((rows, tail_ref.at[pl.ds(group * ZH, ZH)]))
        copies = [
            pltpu.make_async_copy(source, target, sem.at[at])
            for at, (source, target) in enumerate(copies)
        ]
        for copy in copies:
            copy.start()
        for at in range(LEVELS):
            held(at).start()
        for copy in copies:
            copy.wait()
        mix = jnp.sum(tail_ref[...].astype(jnp.float32), axis=0)
        mix_ref[...] = jnp.sum(mix, axis=0, keepdims=True)

    held(level).wait()
    blocks = features_ref.shape[0]
    left = jnp.concatenate([held_ref[level, e] for e in range(blocks)], axis=1)
    right = grads_ref[...].reshape(-1, width)
    out_ref[0] = jnp.dot(left, right, preferred_element_type=jnp.float32).astype(jnp.bfloat16)


def weight_grad(features, groups, zl, core):
    draft, _, columns, tokens = features.shape
    width = groups[0].shape[2]
    count = len(groups)
    return pl.pallas_call(
        weight_grad_kernel,
        grid=(LEVELS,),
        out_shape=(
            jax.ShapeDtypeStruct((LEVELS, columns, width), jnp.bfloat16),
            jax.ShapeDtypeStruct((1, width), jnp.float32),
        ),
        in_specs=[SMEM] + [pl.BlockSpec(memory_space=pltpu.HBM)] * (count + 1),
        out_specs=(
            pl.BlockSpec((1, columns, width), lambda l: (l, 0, 0)),
            pl.BlockSpec((1, width), lambda l: (0, 0)),
        ),
        scratch_shapes=[
            pltpu.VMEM((draft, tokens, width), jnp.bfloat16),
            pltpu.VMEM((count * ZH, TAIL, width), jnp.bfloat16),
            pltpu.VMEM((LEVELS, draft, columns, tokens), jnp.bfloat16),
            pltpu.SemaphoreType.DMA((count * (2 * ZH + 1),)),
            pltpu.SemaphoreType.DMA((LEVELS,)),
        ],
        compiler_params=params(58),
        cost_estimate=pl.CostEstimate(
            flops=2 * draft * LEVELS * columns * tokens * width,
            bytes_accessed=2 * features.size + 2 * draft * tokens * width,
            transcendentals=0,
        ),
        name="weight_grad",
    )(jnp.stack([zl, core]), features, *groups)


def turn_kernel(traded_ref, out_ref):
    rows = traded_ref[:, 0].reshape(-1, traded_ref.shape[3])
    out_ref[0] = rows.astype(jnp.float32).T.astype(jnp.bfloat16)


def turn(traded):
    sequences, levels, rows, columns = traded.shape
    return pl.pallas_call(
        turn_kernel,
        grid=(levels,),
        out_shape=jax.ShapeDtypeStruct((levels, columns, sequences * rows), jnp.bfloat16),
        in_specs=[pl.BlockSpec((sequences, 1, rows, columns), lambda l: (0, l, 0, 0))],
        out_specs=pl.BlockSpec((1, columns, sequences * rows), lambda l: (l, 0, 0)),
        compiler_params=params(8),
        cost_estimate=pl.CostEstimate(flops=0, bytes_accessed=4 * traded.size, transcendentals=0),
        name="turn",
    )(traded)


def valid_total(lengths):
    running = jnp.zeros((), jnp.float32)
    for unroll in range(1, UNROLL + 1):
        running = running + jnp.sum(jnp.maximum(lengths - unroll, 0)).astype(jnp.float32)
    return running


def high_halves(top, draft_index):
    members, draft_count = ZL * CORES, X * Y
    width = top.shape[1] // 2
    even = draft_index % 2 == 0
    left, right = top[:, :width], top[:, width:]
    first, second = [], []
    for t in range(members):
        for e in range(draft_count):
            target = e // 2 * draft_count + 2 * t
            first.append((t * draft_count + e, target + e % 2))
            second.append((t * draft_count + e, target + 1 - e % 2))
    axes = ("tp", "draft")
    one = lax.ppermute(jnp.where(even, left, right), axes, first)
    two = lax.ppermute(jnp.where(even, right, left), axes, second)
    return one, two


def high_rows(one, two, draft_index):
    even = draft_index % 2 == 0
    first = jnp.where(even, one, two)[:-TAIL]
    return jnp.concatenate([first, jnp.where(even, two, one)], axis=0)


def rows_ahead(top):
    return lax.ppermute(top[:TAIL], "draft", [(e, e - 1) for e in range(1, X * Y)])


def trade_columns(own):
    levels, rows, depth = own.shape
    quarters = own.reshape(levels, rows, ZH, depth // ZH).transpose(2, 0, 1, 3)
    return lax.all_to_all(quarters, "dp", split_axis=0, concat_axis=0, tiled=True)


def gather_grads(grad):
    stack = lax.all_gather(grad, "dp", axis=0, tiled=False)
    above, below = from_z(stack, 1), from_z(stack, -1)
    far = [from_z(stack[:2], 2), from_z(stack[2:], -2)]
    other = from_other_core(stack)
    above, below, other = lax.optimization_barrier((above, below, other))
    other_above, other_below = from_other_core(above), from_other_core(below)
    far = jnp.concatenate(far)
    return [stack, other, above, below, other_above, other_below, far, from_other_core(far)]


def local(features, fc_weight, mix_gain, lengths):
    tp_index, zh = lax.axis_index("tp"), lax.axis_index("dp")
    draft_index = lax.axis_index("draft")
    zl, core = tp_index // CORES, tp_index % CORES
    x, y = draft_index // Y, draft_index % Y
    own_rows = features.shape[0]
    piece = own_rows * X * Y // (ZL * CORES)
    own = features.transpose(1, 0, 2)
    weight = fc_weight.transpose(1, 0, 2)

    traded = trade_columns(own)
    next_, last, across = (plane_move(step, True)(own) for step in (1, 3, 2))
    low, high = pair(own, next_), pair(across, last)
    up_low, down_high = plane_move(1, False)(low), plane_move(-1, False)(high)
    up_high, down_low = plane_move(1, False)(high), plane_move(-1, False)(low)
    zero = project([low, high], weight)
    ahead = rows_ahead(own[LEVELS - 1])
    up_low, down_high, zero, ahead, traded, later = lax.optimization_barrier(
        (up_low, down_high, zero, ahead, traded, own)
    )
    far_low, far_high = plane_move(1, False)(up_low), plane_move(-1, False)(down_high)
    halves = high_halves(jnp.concatenate([later[LEVELS - 1], ahead], axis=0), draft_index)
    sides = project([up_low, up_high, down_low, down_high], weight)
    far_low, far_high, halves, sides, turned = lax.optimization_barrier(
        (far_low, far_high, halves, sides, turn(traded))
    )
    every = lax.all_gather(turned, "draft", axis=0, tiled=False)
    keep, send = project_place([far_low, far_high], weight, zero, sides, core, x, y)
    mine, *away = join(keep, from_other_core(send), zl)
    parts = [mine] + [from_zl(block, step) for step, block in zip((1, 2, 3), away)]
    scale = LOSS_SCALE / valid_total(lengths)
    target = high_rows(*halves, draft_index)
    grad = chain(parts, target, mix_gain, tp_index * piece, lengths[zh], scale)
    fc_grad, mix_total = weight_grad(every, gather_grads(grad), zl, core)
    return (fc_grad.transpose(1, 0, 2), mix_total[0])


def solution(mesh):
    placed = (P(("dp", "draft"), None, "tp"), P("tp", None, "draft"), P("draft"), P())
    return jax.shard_map(
        local,
        mesh=mesh,
        in_specs=placed,
        out_specs=(P(("tp", "dp"), None, "draft"), P("draft")),
        check_vma=False,
    )
```

```python
import jax
import jax.numpy as jnp
from jax import lax
from jax.experimental import pallas as pl
from jax.experimental.pallas import tpu as pltpu
from jax.sharding import PartitionSpec as P

LEVELS = 3
UNROLL = 3
LOSS_SCALE = 64.0
HALO = 8
TAIL = 16
X, Y = 4, 4
ZL, CORES, ZH = 4, 2, 4
VMEM = pl.BlockSpec(memory_space=pltpu.VMEM)
SMEM = pl.BlockSpec(memory_space=pltpu.SMEM)


def params(mebibytes):
    return pltpu.CompilerParams(vmem_limit_bytes=mebibytes << 20)


def plane_move(step, first):
    pairs = []
    for t in range(ZL * CORES):
        for x in range(X):
            for y in range(Y):
                along_x = (t % CORES == 0) == first
                source = (x + step) % X * Y + y if along_x else x * Y + (y + step) % Y
                pairs.append((t * X * Y + source, t * X * Y + x * Y + y))
    return lambda block: lax.ppermute(block, ("tp", "draft"), pairs)


def from_other_core(block):
    return lax.ppermute(block, "tp", [(t ^ 1, t) for t in range(ZL * CORES)])


def from_zl(block, step):
    pairs = [((t // CORES + step) % ZL * CORES + t % CORES, t) for t in range(ZL * CORES)]
    return lax.ppermute(block, "tp", pairs)


def from_zh(block, step):
    return lax.ppermute(block, "dp", [((s + step) % ZH, s) for s in range(ZH)])


def from_z(block, step):
    pairs = []
    for t in range(ZL * CORES):
        for s in range(ZH):
            z = (s * ZL + t // CORES + step) % (ZL * ZH)
            pairs.append((((z % ZL) * CORES + t % CORES) * ZH + z // ZL, t * ZH + s))
    return lax.ppermute(block, ("tp", "dp"), pairs)


def pair_kernel(first_ref, second_ref, out_ref):
    out_ref[0] = first_ref[...]
    out_ref[1] = second_ref[...]


def pair(first, second):
    levels, rows, depth = first.shape
    spec = pl.BlockSpec((1, rows, depth), lambda l: (l, 0, 0))
    return pl.pallas_call(
        pair_kernel,
        grid=(levels,),
        out_shape=jax.ShapeDtypeStruct((2,) + first.shape, first.dtype),
        in_specs=[spec] * 2,
        out_specs=pl.BlockSpec((2, 1, rows, depth), lambda l: (0, l, 0, 0)),
        compiler_params=params(8),
        cost_estimate=pl.CostEstimate(flops=0, bytes_accessed=8 * first.size, transcendentals=0),
        name="pair",
    )(first, second)


def rows_of(block_refs):
    return jnp.concatenate([r[...].reshape(-1, r.shape[-1]) for r in block_refs], axis=0)


def accumulate(total_ref, term):
    level = pl.program_id(0)

    @pl.when(level == 0)
    def _():
        total_ref[...] = term

    @pl.when(level > 0)
    def _():
        total_ref[...] += term


def project_kernel(*refs):
    *block_refs, weight_ref, out_ref, total_ref = refs
    accumulate(
        total_ref, jnp.dot(rows_of(block_refs), weight_ref[0], preferred_element_type=jnp.float32)
    )

    @pl.when(pl.program_id(0) == LEVELS - 1)
    def _():
        out_ref[...] = total_ref[...].astype(jnp.bfloat16).reshape(out_ref.shape)


def product_specs(blocks, weight):
    _, _, rows, depth = blocks[0].shape
    specs = [pl.BlockSpec((b.shape[0], 1, rows, depth), lambda l, *_: (0, l, 0, 0)) for b in blocks]
    return specs + [pl.BlockSpec((1, depth, weight.shape[2]), lambda l, *_: (l, 0, 0))]


def product_cost(blocks, weight):
    size = sum(b.size for b in blocks)
    return pl.CostEstimate(
        flops=2 * size * weight.shape[2], bytes_accessed=2 * (weight.size + size), transcendentals=0
    )


def project(blocks, weight):
    rows, width = blocks[0].shape[2], weight.shape[2]
    count = sum(b.shape[0] for b in blocks)
    return pl.pallas_call(
        project_kernel,
        grid=(LEVELS,),
        out_shape=jax.ShapeDtypeStruct((count, rows, width), jnp.bfloat16),
        in_specs=product_specs(blocks, weight),
        out_specs=pl.BlockSpec((count, rows, width), lambda l: (0, 0, 0)),
        scratch_shapes=[pltpu.VMEM((count * rows, width), jnp.float32)],
        compiler_params=params(14),
        cost_estimate=product_cost(blocks, weight),
        name="project",
    )(*blocks, weight)


def project_place_kernel(meta_ref, *refs):
    *block_refs, weight_ref, zero_ref, sides_ref, keep_ref, send_ref, total_ref, token_ref = refs
    accumulate(
        total_ref, jnp.dot(rows_of(block_refs), weight_ref[0], preferred_element_type=jnp.float32)
    )

    @pl.when(pl.program_id(0) == LEVELS - 1)
    def _():
        core, x, y = meta_ref[0], meta_ref[1], meta_ref[2]
        rows = zero_ref.shape[1]
        total = rows * X * Y
        edge = jnp.zeros((HALO, token_ref.shape[1]), jnp.float32)
        token_ref[pl.ds(0, HALO), :] = edge
        token_ref[pl.ds(HALO + total, HALO), :] = edge
        for second in range(4):
            for first in range(4):
                dx = jnp.where(core == 0, first, second)
                dy = jnp.where(core == 0, second, first)
                e = lax.rem(x + dx, X) * Y + lax.rem(y + dy, Y)
                at = pl.multiple_of(e * rows + HALO, 8)
                if second == 0:
                    block = zero_ref[first].astype(jnp.float32)
                elif second == 2:
                    block = total_ref[pl.ds(first * rows, rows), :]
                else:
                    block = sides_ref[second // 2 * 4 + first].astype(jnp.float32)
                token_ref[pl.ds(at, rows), :] = block
        piece = total // (ZL * CORES)
        for zl in range(ZL):
            for out_ref, whose in ((keep_ref, core), (send_ref, 1 - core)):
                at = pl.multiple_of((zl * CORES + whose) * piece, 8)
                out_ref[zl] = token_ref[pl.ds(at, piece + 2 * HALO), :].astype(jnp.bfloat16)


def project_place(blocks, weight, zero, sides, core, x, y):
    _, rows, width = zero.shape
    count = sum(b.shape[0] for b in blocks)
    total = rows * X * Y
    pieces = (ZL, total // (ZL * CORES) + 2 * HALO, width)
    whole = lambda shape: pl.BlockSpec(shape, lambda l, *_: (0, 0, 0))
    return pl.pallas_call(
        project_place_kernel,
        out_shape=(jax.ShapeDtypeStruct(pieces, jnp.bfloat16),) * 2,
        grid_spec=pltpu.PrefetchScalarGridSpec(
            num_scalar_prefetch=1,
            grid=(LEVELS,),
            in_specs=product_specs(blocks, weight) + [whole(zero.shape), whole(sides.shape)],
            out_specs=(whole(pieces),) * 2,
            scratch_shapes=[
                pltpu.VMEM((count * rows, width), jnp.float32),
                pltpu.VMEM((total + 2 * HALO, width), jnp.float32),
            ],
        ),
        compiler_params=params(58),
        cost_estimate=product_cost(blocks, weight),
        name="project_place",
    )(jnp.stack([core, x, y]), *blocks, weight, zero, sides)


def join_kernel(meta_ref, keep_ref, got_ref, own_ref, *away_refs):
    zl = meta_ref[0]

    def piece(index):
        return keep_ref[index].astype(jnp.float32) + got_ref[index].astype(jnp.float32)

    own_ref[...] = piece(zl).astype(jnp.bfloat16)
    for step, away_ref in zip((1, 2, 3), away_refs):
        away_ref[...] = piece(lax.rem(zl + ZL - step, ZL)).astype(jnp.bfloat16)


def join(keep, got, zl):
    count, rows, width = keep.shape
    whole = pl.BlockSpec(keep.shape, lambda i, m: (0, 0, 0))
    piece = pl.BlockSpec((rows, width), lambda i, m: (0, 0))
    return pl.pallas_call(
        join_kernel,
        out_shape=(jax.ShapeDtypeStruct((rows, width), jnp.bfloat16),) * count,
        grid_spec=pltpu.PrefetchScalarGridSpec(
            num_scalar_prefetch=1, grid=(1,), in_specs=[whole] * 2, out_specs=(piece,) * count
        ),
        compiler_params=params(58),
        cost_estimate=pl.CostEstimate(
            flops=keep.size, bytes_accessed=6 * keep.size, transcendentals=0
        ),
        name="join",
    )(zl.reshape(1), keep, got)


def sigmoid(v):
    return 1.0 / (1.0 + jnp.exp(-v))


def chain_kernel(meta_ref, scale_ref, *refs):
    *part_refs, high_ref, gain_ref, grad_ref = refs
    rows, width = part_refs[0].shape
    own = rows - 2 * HALO
    joined = part_refs[0][...].astype(jnp.float32)
    for part_ref in part_refs[1:]:
        joined = joined + part_ref[...].astype(jnp.float32)
    high = high_ref[...].astype(jnp.float32)
    gain = gain_ref[...]
    scale = scale_ref[0]
    start, length = meta_ref[0], meta_ref[1]
    position = start - HALO + lax.broadcasted_iota(jnp.int32, (rows, width), 0)

    def down(values):
        return jnp.concatenate([jnp.zeros((1, width), jnp.float32), values[:-1]], axis=0)

    def up(values):
        return jnp.concatenate([values[1:], jnp.zeros((1, width), jnp.float32)], axis=0)

    def target(step):
        lead = jnp.zeros((HALO - step, width), jnp.float32)
        return jnp.concatenate([lead, high[: rows - HALO + step]], axis=0)

    def state_and_slope(v):
        gate = sigmoid(v)
        return v * gate, gate * (1.0 + v * (1.0 - gate))

    def residual(state, step):
        return jnp.where(position + step < length, scale * (state - target(step)), 0.0)

    state_1, slope_1 = state_and_slope(joined)
    before_1 = down(state_1)
    state_2, slope_2 = state_and_slope(joined + gain * before_1)
    before_2 = down(state_2)
    state_3, slope_3 = state_and_slope(joined + gain * before_2)
    delta_3 = residual(state_3, 3) * slope_3
    delta_2 = (residual(state_2, 2) + up(gain * delta_3)) * slope_2
    delta_1 = (residual(state_1, 1) + up(gain * delta_2)) * slope_1
    total = delta_1 + delta_2 + delta_3
    mix = (delta_2 * before_1 + delta_3 * before_2)[HALO : HALO + own]
    rest = jnp.sum(mix, axis=0, keepdims=True)
    tail = []
    for _ in range(3):
        term = rest.astype(jnp.bfloat16).astype(jnp.float32)
        tail.append(term)
        rest = rest - term
    tail.append(jnp.zeros((TAIL - 3, width), jnp.float32))
    grad_ref[pl.ds(0, own), :] = total[HALO : HALO + own].astype(jnp.bfloat16)
    grad_ref[pl.ds(own, TAIL), :] = jnp.concatenate(tail, axis=0).astype(jnp.bfloat16)


def chain(parts, high, gain, start, length, scale):
    rows, width = parts[0].shape
    own = rows - 2 * HALO
    return pl.pallas_call(
        chain_kernel,
        out_shape=jax.ShapeDtypeStruct((own + TAIL, width), jnp.bfloat16),
        in_specs=[SMEM, SMEM] + [VMEM] * (len(parts) + 2),
        out_specs=VMEM,
        compiler_params=params(14),
        cost_estimate=pl.CostEstimate(
            flops=60 * rows * width, bytes_accessed=10 * rows * width, transcendentals=3 * rows * width
        ),
        name="chain",
    )(jnp.stack([start, length]), scale.reshape(1), *parts, high, gain.reshape(1, width))


def take_pieces(groups, members, features_ref, grads_ref, tails_ref, held_ref, sem):
    half = grads_ref.shape[1] // ZH
    copies, held = [], [[] for _ in range(LEVELS)]
    at = 0

    def start(source, target, into):
        nonlocal at
        copy = pltpu.make_async_copy(source, target, sem.at[at])
        copy.start()
        into.append(copy)
        at += 1

    for group, (group_ref, member) in enumerate(zip(groups, members)):
        for part in range(2):
            for sequence in range(ZH):
                source = group_ref.at[sequence, pl.ds(part * half, half), :]
                target = grads_ref.at[2 * group + part, pl.ds(sequence * half, half), :]
                start(source, target, copies)
        source = group_ref.at[:, pl.ds(2 * half, TAIL), :]
        start(source, tails_ref.at[pl.ds(group * ZH, ZH)], copies)
    for level in range(LEVELS):
        for group, member in enumerate(members):
            source = features_ref.at[pl.ds(member * 2, 2), level]
            start(source, held_ref.at[level, pl.ds(group * 2, 2)], held[level])
    return copies, held


def copy_count(groups):
    return groups * (2 * ZH + 1 + LEVELS)


def products(held_ref, grads_ref, held):
    right = grads_ref[...].reshape(-1, grads_ref.shape[2])
    for level in range(LEVELS):
        for copy in held[level]:
            copy.wait()
        left = jnp.concatenate([held_ref[level, e] for e in range(held_ref.shape[1])], axis=1)
        yield level, jnp.dot(left, right, preferred_element_type=jnp.float32)


def mix_of(tails_ref):
    return jnp.sum(jnp.sum(tails_ref[...].astype(jnp.float32), axis=0), axis=0, keepdims=True)


def near_kernel(meta_ref, features_ref, *refs):
    *group_refs, out_ref, mix_ref, grads_ref, tails_ref, held_ref, sem = refs
    members = [meta_ref[at] for at in range(len(group_refs))]
    copies, held = take_pieces(group_refs, members, features_ref, grads_ref, tails_ref, held_ref, sem)
    for copy in copies:
        copy.wait()
    mix_ref[...] = mix_of(tails_ref)
    for level, term in products(held_ref, grads_ref, held):
        out_ref[level] = term


def far_kernel(meta_ref, features_ref, near_ref, near_mix_ref, *refs):
    *group_refs, out_ref, mix_ref, grads_ref, tails_ref, held_ref, sem = refs
    members = [meta_ref[at] for at in range(len(group_refs))]
    copies, held = take_pieces(group_refs, members, features_ref, grads_ref, tails_ref, held_ref, sem)
    for copy in copies:
        copy.wait()
    mix_ref[...] = near_mix_ref[...] + mix_of(tails_ref)
    for level, term in products(held_ref, grads_ref, held):
        out_ref[level] = (near_ref[level] + term).astype(jnp.bfloat16)


def weight_grad(kernel, name, features, groups, members, before, held_as):
    _, _, columns, tokens = features.shape
    width = groups[0].shape[2]
    count = len(groups)
    hbm = pl.BlockSpec(memory_space=pltpu.HBM)
    whole = pl.BlockSpec((LEVELS, columns, width), lambda i, m: (0, 0, 0))
    line = pl.BlockSpec((1, width), lambda i, m: (0, 0))
    return pl.pallas_call(
        kernel,
        out_shape=(
            jax.ShapeDtypeStruct((LEVELS, columns, width), held_as),
            jax.ShapeDtypeStruct((1, width), jnp.float32),
        ),
        grid_spec=pltpu.PrefetchScalarGridSpec(
            num_scalar_prefetch=1,
            grid=(1,),
            in_specs=[hbm] + [whole, line][: len(before)] + [hbm] * count,
            out_specs=(whole, line),
            scratch_shapes=[
                pltpu.VMEM((2 * count, tokens, width), jnp.bfloat16),
                pltpu.VMEM((count * ZH, TAIL, width), jnp.bfloat16),
                pltpu.VMEM((LEVELS, 2 * count, columns, tokens), jnp.bfloat16),
                pltpu.SemaphoreType.DMA((copy_count(count),)),
            ],
        ),
        compiler_params=params(58),
        cost_estimate=pl.CostEstimate(
            flops=4 * count * LEVELS * columns * tokens * width,
            bytes_accessed=4 * count * tokens * (LEVELS * columns + width),
            transcendentals=0,
        ),
        name=name,
    )(jnp.stack(members), features, *before, *groups)


def turn_kernel(traded_ref, out_ref):
    rows = traded_ref[:, 0].reshape(-1, traded_ref.shape[3])
    out_ref[0] = rows.astype(jnp.float32).T.astype(jnp.bfloat16)


def turn(traded):
    sequences, levels, rows, columns = traded.shape
    return pl.pallas_call(
        turn_kernel,
        grid=(levels,),
        out_shape=jax.ShapeDtypeStruct((levels, columns, sequences * rows), jnp.bfloat16),
        in_specs=[pl.BlockSpec((sequences, 1, rows, columns), lambda l: (0, l, 0, 0))],
        out_specs=pl.BlockSpec((1, columns, sequences * rows), lambda l: (l, 0, 0)),
        compiler_params=params(8),
        cost_estimate=pl.CostEstimate(flops=0, bytes_accessed=4 * traded.size, transcendentals=0),
        name="turn",
    )(traded)


def valid_total(lengths):
    running = jnp.zeros((), jnp.float32)
    for unroll in range(1, UNROLL + 1):
        running = running + jnp.sum(jnp.maximum(lengths - unroll, 0)).astype(jnp.float32)
    return running


def high_halves(top, draft_index):
    members, draft_count = ZL * CORES, X * Y
    width = top.shape[1] // 2
    even = draft_index % 2 == 0
    left, right = top[:, :width], top[:, width:]
    first, second = [], []
    for t in range(members):
        for e in range(draft_count):
            target = e // 2 * draft_count + 2 * t
            first.append((t * draft_count + e, target + e % 2))
            second.append((t * draft_count + e, target + 1 - e % 2))
    axes = ("tp", "draft")
    one = lax.ppermute(jnp.where(even, left, right), axes, first)
    two = lax.ppermute(jnp.where(even, right, left), axes, second)
    return one, two


def high_rows(one, two, draft_index):
    even = draft_index % 2 == 0
    first = jnp.where(even, one, two)[:-TAIL]
    return jnp.concatenate([first, jnp.where(even, two, one)], axis=0)


def rows_ahead(top):
    return lax.ppermute(top[:TAIL], "draft", [(e, e - 1) for e in range(1, X * Y)])


def trade_columns(own):
    levels, rows, depth = own.shape
    quarters = own.reshape(levels, rows, ZH, depth // ZH).transpose(2, 0, 1, 3)
    return lax.all_to_all(quarters, "dp", split_axis=0, concat_axis=0, tiled=True)


def gather_grads(grad, features, zl, core):
    stack = lax.all_gather(grad, "dp", axis=0, tiled=False)
    above, below = from_z(stack, 1), from_z(stack, -1)
    far = jnp.concatenate([from_z(stack[:2], 2), from_z(stack[2:], -2)])
    other = from_other_core(stack)
    above, below, other, far = lax.optimization_barrier((above, below, other, far))
    swapped = [from_other_core(block) for block in (above, below, far)]

    def member(step, of_core):
        return (zl + step) % ZL * CORES + of_core

    near = [stack, other, above, below, far]
    owners = [member(0, core), member(0, 1 - core)] + [member(step, core) for step in (1, 3, 2)]
    before = weight_grad(near_kernel, "near", features, near, owners, (), jnp.float32)
    owners = [member(step, 1 - core) for step in (1, 3, 2)]
    return weight_grad(far_kernel, "far", features, swapped, owners, tuple(before), jnp.bfloat16)


def local(features, fc_weight, mix_gain, lengths):
    tp_index, zh = lax.axis_index("tp"), lax.axis_index("dp")
    draft_index = lax.axis_index("draft")
    zl, core = tp_index // CORES, tp_index % CORES
    x, y = draft_index // Y, draft_index % Y
    own_rows = features.shape[0]
    piece = own_rows * X * Y // (ZL * CORES)
    own = features.transpose(1, 0, 2)
    weight = fc_weight.transpose(1, 0, 2)

    traded = trade_columns(own)
    next_, last, across = (plane_move(step, True)(own) for step in (1, 3, 2))
    low, high = pair(own, next_), pair(across, last)
    up_low, down_high = plane_move(1, False)(low), plane_move(-1, False)(high)
    up_high, down_low = plane_move(1, False)(high), plane_move(-1, False)(low)
    zero = project([low, high], weight)
    ahead = rows_ahead(own[LEVELS - 1])
    up_low, down_high, zero, ahead, traded, later = lax.optimization_barrier(
        (up_low, down_high, zero, ahead, traded, own)
    )
    far_low, far_high = plane_move(1, False)(up_low), plane_move(-1, False)(down_high)
    halves = high_halves(jnp.concatenate([later[LEVELS - 1], ahead], axis=0), draft_index)
    sides = project([up_low, up_high, down_low, down_high], weight)
    far_low, far_high, halves, sides, turned = lax.optimization_barrier(
        (far_low, far_high, halves, sides, turn(traded))
    )
    every = lax.all_gather(turned, "draft", axis=0, tiled=False)
    keep, send = project_place([far_low, far_high], weight, zero, sides, core, x, y)
    mine, *away = join(keep, from_other_core(send), zl)
    parts = [mine] + [from_zl(block, step) for step, block in zip((1, 2, 3), away)]
    scale = LOSS_SCALE / valid_total(lengths)
    target = high_rows(*halves, draft_index)
    grad = chain(parts, target, mix_gain, tp_index * piece, lengths[zh], scale)
    fc_grad, mix_total = gather_grads(grad, every, zl, core)
    return (fc_grad.transpose(1, 0, 2), mix_total[0])


def solution(mesh):
    placed = (P(("dp", "draft"), None, "tp"), P("tp", None, "draft"), P("draft"), P())
    return jax.shard_map(
        local,
        mesh=mesh,
        in_specs=placed,
        out_specs=(P(("tp", "dp"), None, "draft"), P("draft")),
        check_vma=False,
    )
```

```python
import jax
import jax.numpy as jnp
from jax import lax
from jax.experimental import pallas as pl
from jax.experimental.pallas import tpu as pltpu
from jax.sharding import PartitionSpec as P

LEVELS = 3
UNROLL = 3
LOSS_SCALE = 64.0
HALO = 8
TAIL = 16
X, Y = 4, 4
ZL, CORES, ZH = 4, 2, 4
VMEM = pl.BlockSpec(memory_space=pltpu.VMEM)
SMEM = pl.BlockSpec(memory_space=pltpu.SMEM)


def params(mebibytes):
    return pltpu.CompilerParams(vmem_limit_bytes=mebibytes << 20)


def plane_move(step, first):
    pairs = []
    for t in range(ZL * CORES):
        for x in range(X):
            for y in range(Y):
                along_x = (t % CORES == 0) == first
                source = (x + step) % X * Y + y if along_x else x * Y + (y + step) % Y
                pairs.append((t * X * Y + source, t * X * Y + x * Y + y))
    return lambda block: lax.ppermute(block, ("tp", "draft"), pairs)


def from_other_core(block):
    return lax.ppermute(block, "tp", [(t ^ 1, t) for t in range(ZL * CORES)])


def from_zl(block, step):
    pairs = [((t // CORES + step) % ZL * CORES + t % CORES, t) for t in range(ZL * CORES)]
    return lax.ppermute(block, "tp", pairs)


def from_zh(block, step):
    return lax.ppermute(block, "dp", [((s + step) % ZH, s) for s in range(ZH)])


def from_z(block, step):
    pairs = []
    for t in range(ZL * CORES):
        for s in range(ZH):
            z = (s * ZL + t // CORES + step) % (ZL * ZH)
            pairs.append((((z % ZL) * CORES + t % CORES) * ZH + z // ZL, t * ZH + s))
    return lax.ppermute(block, ("tp", "dp"), pairs)


def pair_kernel(first_ref, second_ref, out_ref):
    out_ref[0] = first_ref[...]
    out_ref[1] = second_ref[...]


def pair(first, second):
    return pl.pallas_call(
        pair_kernel,
        out_shape=jax.ShapeDtypeStruct((2,) + first.shape, first.dtype),
        in_specs=[VMEM] * 2,
        out_specs=VMEM,
        compiler_params=params(4),
        cost_estimate=pl.CostEstimate(flops=0, bytes_accessed=8 * first.size, transcendentals=0),
        name="pair",
    )(first, second)


def rows_of(block_refs):
    return jnp.concatenate([r[...].reshape(-1, r.shape[-1]) for r in block_refs], axis=0)


def accumulate(total_ref, term):
    level = pl.program_id(0)

    @pl.when(level == 0)
    def _():
        total_ref[...] = term

    @pl.when(level > 0)
    def _():
        total_ref[...] += term


def project_kernel(*refs):
    *block_refs, weight_ref, out_ref, total_ref = refs
    accumulate(
        total_ref, jnp.dot(rows_of(block_refs), weight_ref[0], preferred_element_type=jnp.float32)
    )

    @pl.when(pl.program_id(0) == LEVELS - 1)
    def _():
        out_ref[...] = total_ref[...].astype(jnp.bfloat16).reshape(out_ref.shape)


def product_specs(blocks, weight):
    _, _, rows, depth = blocks[0].shape
    specs = [pl.BlockSpec((b.shape[0], 1, rows, depth), lambda l, *_: (0, l, 0, 0)) for b in blocks]
    return specs + [pl.BlockSpec((1, depth, weight.shape[2]), lambda l, *_: (l, 0, 0))]


def product_cost(blocks, weight):
    size = sum(b.size for b in blocks)
    return pl.CostEstimate(
        flops=2 * size * weight.shape[2], bytes_accessed=2 * (weight.size + size), transcendentals=0
    )


def project(blocks, weight):
    rows, width = blocks[0].shape[2], weight.shape[2]
    count = sum(b.shape[0] for b in blocks)
    return pl.pallas_call(
        project_kernel,
        grid=(LEVELS,),
        out_shape=jax.ShapeDtypeStruct((count, rows, width), jnp.bfloat16),
        in_specs=product_specs(blocks, weight),
        out_specs=pl.BlockSpec((count, rows, width), lambda l: (0, 0, 0)),
        scratch_shapes=[pltpu.VMEM((count * rows, width), jnp.float32)],
        compiler_params=params(14),
        cost_estimate=product_cost(blocks, weight),
        name="project",
    )(*blocks, weight)


def project_place_kernel(meta_ref, *refs):
    *block_refs, weight_ref, zero_ref, sides_ref, keep_ref, send_ref, total_ref, token_ref = refs
    accumulate(
        total_ref, jnp.dot(rows_of(block_refs), weight_ref[0], preferred_element_type=jnp.float32)
    )

    @pl.when(pl.program_id(0) == LEVELS - 1)
    def _():
        core, x, y = meta_ref[0], meta_ref[1], meta_ref[2]
        rows = zero_ref.shape[1]
        total = rows * X * Y
        edge = jnp.zeros((HALO, token_ref.shape[1]), jnp.float32)
        token_ref[pl.ds(0, HALO), :] = edge
        token_ref[pl.ds(HALO + total, HALO), :] = edge
        for second in range(4):
            for first in range(4):
                dx = jnp.where(core == 0, first, second)
                dy = jnp.where(core == 0, second, first)
                e = lax.rem(x + dx, X) * Y + lax.rem(y + dy, Y)
                at = pl.multiple_of(e * rows + HALO, 8)
                if second == 0:
                    block = zero_ref[first].astype(jnp.float32)
                elif second == 2:
                    block = total_ref[pl.ds(first * rows, rows), :]
                else:
                    block = sides_ref[second // 2 * 4 + first].astype(jnp.float32)
                token_ref[pl.ds(at, rows), :] = block
        piece = total // (ZL * CORES)
        for zl in range(ZL):
            for out_ref, whose in ((keep_ref, core), (send_ref, 1 - core)):
                at = pl.multiple_of((zl * CORES + whose) * piece, 8)
                out_ref[zl] = token_ref[pl.ds(at, piece + 2 * HALO), :].astype(jnp.bfloat16)


def project_place(blocks, weight, zero, sides, core, x, y):
    _, rows, width = zero.shape
    count = sum(b.shape[0] for b in blocks)
    total = rows * X * Y
    pieces = (ZL, total // (ZL * CORES) + 2 * HALO, width)
    whole = lambda shape: pl.BlockSpec(shape, lambda l, *_: (0, 0, 0))
    return pl.pallas_call(
        project_place_kernel,
        out_shape=(jax.ShapeDtypeStruct(pieces, jnp.bfloat16),) * 2,
        grid_spec=pltpu.PrefetchScalarGridSpec(
            num_scalar_prefetch=1,
            grid=(LEVELS,),
            in_specs=product_specs(blocks, weight) + [whole(zero.shape), whole(sides.shape)],
            out_specs=(whole(pieces),) * 2,
            scratch_shapes=[
                pltpu.VMEM((count * rows, width), jnp.float32),
                pltpu.VMEM((total + 2 * HALO, width), jnp.float32),
            ],
        ),
        compiler_params=params(18),
        cost_estimate=product_cost(blocks, weight),
        name="project_place",
    )(jnp.stack([core, x, y]), *blocks, weight, zero, sides)


def join_kernel(meta_ref, keep_ref, got_ref, own_ref, *away_refs):
    zl = meta_ref[0]

    def piece(index):
        return keep_ref[index].astype(jnp.float32) + got_ref[index].astype(jnp.float32)

    own_ref[...] = piece(zl).astype(jnp.bfloat16)
    for step, away_ref in zip((1, 2, 3), away_refs):
        away_ref[...] = piece(lax.rem(zl + ZL - step, ZL)).astype(jnp.bfloat16)


def join(keep, got, zl):
    count, rows, width = keep.shape
    whole = pl.BlockSpec(keep.shape, lambda i, m: (0, 0, 0))
    piece = pl.BlockSpec((rows, width), lambda i, m: (0, 0))
    return pl.pallas_call(
        join_kernel,
        out_shape=(jax.ShapeDtypeStruct((rows, width), jnp.bfloat16),) * count,
        grid_spec=pltpu.PrefetchScalarGridSpec(
            num_scalar_prefetch=1, grid=(1,), in_specs=[whole] * 2, out_specs=(piece,) * count
        ),
        compiler_params=params(8),
        cost_estimate=pl.CostEstimate(
            flops=keep.size, bytes_accessed=6 * keep.size, transcendentals=0
        ),
        name="join",
    )(zl.reshape(1), keep, got)


def sigmoid(v):
    return 1.0 / (1.0 + jnp.exp(-v))


def chain_kernel(meta_ref, scale_ref, *refs):
    *part_refs, high_ref, gain_ref, grad_ref = refs
    rows, width = part_refs[0].shape
    own = rows - 2 * HALO
    joined = part_refs[0][...].astype(jnp.float32)
    for part_ref in part_refs[1:]:
        joined = joined + part_ref[...].astype(jnp.float32)
    high = high_ref[...].astype(jnp.float32)
    gain = gain_ref[...]
    scale = scale_ref[0]
    start, length = meta_ref[0], meta_ref[1]
    position = start - HALO + lax.broadcasted_iota(jnp.int32, (rows, width), 0)

    def down(values):
        return jnp.concatenate([jnp.zeros((1, width), jnp.float32), values[:-1]], axis=0)

    def up(values):
        return jnp.concatenate([values[1:], jnp.zeros((1, width), jnp.float32)], axis=0)

    def target(step):
        lead = jnp.zeros((HALO - step, width), jnp.float32)
        return jnp.concatenate([lead, high[: rows - HALO + step]], axis=0)

    def state_and_slope(v):
        gate = sigmoid(v)
        return v * gate, gate * (1.0 + v * (1.0 - gate))

    def residual(state, step):
        return jnp.where(position + step < length, scale * (state - target(step)), 0.0)

    state_1, slope_1 = state_and_slope(joined)
    before_1 = down(state_1)
    state_2, slope_2 = state_and_slope(joined + gain * before_1)
    before_2 = down(state_2)
    state_3, slope_3 = state_and_slope(joined + gain * before_2)
    delta_3 = residual(state_3, 3) * slope_3
    delta_2 = (residual(state_2, 2) + up(gain * delta_3)) * slope_2
    delta_1 = (residual(state_1, 1) + up(gain * delta_2)) * slope_1
    total = delta_1 + delta_2 + delta_3
    mix = (delta_2 * before_1 + delta_3 * before_2)[HALO : HALO + own]
    rest = jnp.sum(mix, axis=0, keepdims=True)
    tail = []
    for _ in range(3):
        term = rest.astype(jnp.bfloat16).astype(jnp.float32)
        tail.append(term)
        rest = rest - term
    tail.append(jnp.zeros((TAIL - 3, width), jnp.float32))
    grad_ref[pl.ds(0, own), :] = total[HALO : HALO + own].astype(jnp.bfloat16)
    grad_ref[pl.ds(own, TAIL), :] = jnp.concatenate(tail, axis=0).astype(jnp.bfloat16)


def chain(parts, high, gain, start, length, scale):
    rows, width = parts[0].shape
    own = rows - 2 * HALO
    return pl.pallas_call(
        chain_kernel,
        out_shape=jax.ShapeDtypeStruct((own + TAIL, width), jnp.bfloat16),
        in_specs=[SMEM, SMEM] + [VMEM] * (len(parts) + 2),
        out_specs=VMEM,
        compiler_params=params(14),
        cost_estimate=pl.CostEstimate(
            flops=60 * rows * width, bytes_accessed=10 * rows * width, transcendentals=3 * rows * width
        ),
        name="chain",
    )(jnp.stack([start, length]), scale.reshape(1), *parts, high, gain.reshape(1, width))


def weight_grad_kernel(meta_ref, features_ref, *refs):
    *group_refs, out_ref, mix_ref, got_ref, grads_ref, held_ref, got_sem, held_sem = refs
    half = grads_ref.shape[1] // ZH
    width = grads_ref.shape[2]
    got = [
        pltpu.make_async_copy(group_ref, got_ref.at[at], got_sem.at[at])
        for at, group_ref in enumerate(group_refs)
    ]
    held = [
        pltpu.make_async_copy(features_ref.at[:, at], held_ref.at[at], held_sem.at[at])
        for at in range(LEVELS)
    ]
    for copy in got + held:
        copy.start()
    mix = jnp.zeros((TAIL, width), jnp.float32)
    for at, copy in enumerate(got):
        copy.wait()
        for part in range(2):
            slab = grads_ref.at[meta_ref[at] * 2 + part]
            for sequence in range(ZH):
                rows = got_ref[at, sequence, pl.ds(part * half, half), :]
                slab[pl.ds(sequence * half, half), :] = rows
        for sequence in range(ZH):
            mix = mix + got_ref[at, sequence, pl.ds(2 * half, TAIL), :].astype(jnp.float32)
    mix_ref[...] = jnp.sum(mix, axis=0, keepdims=True)
    blocks = held_ref.shape[1]
    for at, copy in enumerate(held):
        copy.wait()
        left = jnp.concatenate([held_ref[at, e] for e in range(blocks)], axis=1)
        right = grads_ref[...].reshape(-1, width)
        term = jnp.dot(left, right, preferred_element_type=jnp.float32)
        out_ref[at] = term.astype(jnp.bfloat16)


def weight_grad(features, groups, members):
    draft, _, columns, tokens = features.shape
    count, width = len(groups), groups[0].shape[2]
    hbm = pl.BlockSpec(memory_space=pltpu.HBM)
    return pl.pallas_call(
        weight_grad_kernel,
        out_shape=(
            jax.ShapeDtypeStruct((LEVELS, columns, width), jnp.bfloat16),
            jax.ShapeDtypeStruct((1, width), jnp.float32),
        ),
        in_specs=[SMEM] + [hbm] * (count + 1),
        out_specs=(VMEM, VMEM),
        scratch_shapes=[
            pltpu.VMEM((count,) + groups[0].shape, jnp.bfloat16),
            pltpu.VMEM((draft, tokens, width), jnp.bfloat16),
            pltpu.VMEM((LEVELS, draft, columns, tokens), jnp.bfloat16),
            pltpu.SemaphoreType.DMA((count,)),
            pltpu.SemaphoreType.DMA((LEVELS,)),
        ],
        compiler_params=params(58),
        cost_estimate=pl.CostEstimate(
            flops=2 * draft * LEVELS * columns * tokens * width,
            bytes_accessed=2 * features.size + 2 * draft * tokens * width,
            transcendentals=0,
        ),
        name="weight_grad",
    )(jnp.stack(members), features, *groups)


def turn_kernel(traded_ref, out_ref):
    rows = traded_ref[:, 0].reshape(-1, traded_ref.shape[3])
    out_ref[0] = rows.astype(jnp.float32).T.astype(jnp.bfloat16)


def turn(traded):
    sequences, levels, rows, columns = traded.shape
    return pl.pallas_call(
        turn_kernel,
        grid=(levels,),
        out_shape=jax.ShapeDtypeStruct((levels, columns, sequences * rows), jnp.bfloat16),
        in_specs=[pl.BlockSpec((sequences, 1, rows, columns), lambda l: (0, l, 0, 0))],
        out_specs=pl.BlockSpec((1, columns, sequences * rows), lambda l: (l, 0, 0)),
        compiler_params=params(8),
        cost_estimate=pl.CostEstimate(flops=0, bytes_accessed=4 * traded.size, transcendentals=0),
        name="turn",
    )(traded)


def valid_total(lengths):
    running = jnp.zeros((), jnp.float32)
    for unroll in range(1, UNROLL + 1):
        running = running + jnp.sum(jnp.maximum(lengths - unroll, 0)).astype(jnp.float32)
    return running


def send_high(top, draft_index):
    members, draft_count = ZL * CORES, X * Y
    width = top.shape[1] // 2
    even = draft_index % 2 == 0
    left, right = top[:, :width], top[:, width:]
    straight, crossed, after_left, after_right = [], [], [], []
    for t in range(members):
        for e in range(draft_count):
            source = t * draft_count + e
            target = e // 2 * draft_count + 2 * t
            straight.append((source, target + e % 2))
            crossed.append((source, target + 1 - e % 2))
            if e % 2 == 0 and e > 0:
                after_left.append((source, target - draft_count))
                after_right.append((source, target - draft_count + 1))
    axes = ("tp", "draft")
    return (
        lax.ppermute(jnp.where(even, left, right), axes, straight),
        lax.ppermute(jnp.where(even, right, left), axes, crossed),
        lax.ppermute(left[:TAIL], axes, after_left),
        lax.ppermute(right[:TAIL], axes, after_right),
    )


def high_rows(one, two, after_left, after_right, draft_index):
    even = draft_index % 2 == 0
    after = jnp.where(even, after_left, after_right)
    return jnp.concatenate([jnp.where(even, one, two), jnp.where(even, two, one), after], axis=0)


def trade_columns(own):
    levels, rows, depth = own.shape
    quarters = own.reshape(levels, rows, ZH, depth // ZH).transpose(2, 0, 1, 3)
    return lax.all_to_all(quarters, "dp", split_axis=0, concat_axis=0, tiled=True)


def gather_grads(grad, features, zl, core):
    stack = lax.all_gather(grad, "dp", axis=0, tiled=False)
    above, below = from_z(stack, 1), from_z(stack, -1)
    far = jnp.concatenate([from_z(stack[:2], 2), from_z(stack[2:], -2)])
    other = from_other_core(stack)
    above, below, other, far = lax.optimization_barrier((above, below, other, far))
    swapped = [from_other_core(block) for block in (above, below, far)]

    def member(step, of_core):
        return (zl + step) % ZL * CORES + of_core

    groups = [stack, other, above, below, far] + swapped
    members = [member(0, core), member(0, 1 - core)]
    members += [member(step, core) for step in (1, 3, 2)]
    members += [member(step, 1 - core) for step in (1, 3, 2)]
    return weight_grad(features, groups, members)


def local(features, fc_weight, mix_gain, lengths):
    tp_index, zh = lax.axis_index("tp"), lax.axis_index("dp")
    draft_index = lax.axis_index("draft")
    zl, core = tp_index // CORES, tp_index % CORES
    x, y = draft_index // Y, draft_index % Y
    own_rows = features.shape[0]
    piece = own_rows * X * Y // (ZL * CORES)
    own = features.transpose(1, 0, 2)
    weight = fc_weight.transpose(1, 0, 2)

    traded = trade_columns(own)
    next_, last, across = (plane_move(step, True)(own) for step in (1, 3, 2))
    low, high = pair(own, next_), pair(across, last)
    up_low, down_high = plane_move(1, False)(low), plane_move(-1, False)(high)
    up_high, down_low = plane_move(1, False)(high), plane_move(-1, False)(low)
    zero = project([low, high], weight)
    up_low, down_high, zero, traded, later = lax.optimization_barrier(
        (up_low, down_high, zero, traded, own)
    )
    far_low, far_high = plane_move(1, False)(up_low), plane_move(-1, False)(down_high)
    halves = send_high(later[LEVELS - 1], draft_index)
    sides = project([up_low, up_high, down_low, down_high], weight)
    far_low, far_high, halves, sides, turned = lax.optimization_barrier(
        (far_low, far_high, halves, sides, turn(traded))
    )
    keep, send = project_place([far_low, far_high], weight, zero, sides, core, x, y)
    keep, send, turned = lax.optimization_barrier((keep, send, turned))
    every = lax.all_gather(turned, "draft", axis=0, tiled=False)
    mine, *away = join(keep, from_other_core(send), zl)
    parts = [mine] + [from_zl(block, step) for step, block in zip((1, 2, 3), away)]
    scale = LOSS_SCALE / valid_total(lengths)
    target = high_rows(*halves, draft_index)
    grad = chain(parts, target, mix_gain, tp_index * piece, lengths[zh], scale)
    fc_grad, mix_total = gather_grads(grad, every, zl, core)
    return (fc_grad.transpose(1, 0, 2), mix_total[0])


def solution(mesh):
    placed = (P(("dp", "draft"), None, "tp"), P("tp", None, "draft"), P("draft"), P())
    return jax.shard_map(
        local,
        mesh=mesh,
        in_specs=placed,
        out_specs=(P(("tp", "dp"), None, "draft"), P("draft")),
        check_vma=False,
    )
```

```python
import jax
import jax.numpy as jnp
from jax import lax
from jax.experimental import pallas as pl
from jax.experimental.pallas import tpu as pltpu
from jax.sharding import PartitionSpec as P

LEVELS = 3
UNROLL = 3
LOSS_SCALE = 64.0
HALO = 8
TAIL = 16
X, Y = 4, 4
ZL, CORES, ZH = 4, 2, 4
VMEM = pl.BlockSpec(memory_space=pltpu.VMEM)
SMEM = pl.BlockSpec(memory_space=pltpu.SMEM)


def params(mebibytes):
    return pltpu.CompilerParams(vmem_limit_bytes=mebibytes << 20)


def plane_move(step, first):
    pairs = []
    for t in range(ZL * CORES):
        for x in range(X):
            for y in range(Y):
                along_x = (t % CORES == 0) == first
                source = (x + step) % X * Y + y if along_x else x * Y + (y + step) % Y
                pairs.append((t * X * Y + source, t * X * Y + x * Y + y))
    return lambda block: lax.ppermute(block, ("tp", "draft"), pairs)


def from_other_core(block):
    return lax.ppermute(block, "tp", [(t ^ 1, t) for t in range(ZL * CORES)])


def from_zl(block, step):
    pairs = [((t // CORES + step) % ZL * CORES + t % CORES, t) for t in range(ZL * CORES)]
    return lax.ppermute(block, "tp", pairs)


def from_zh(block, step):
    return lax.ppermute(block, "dp", [((s + step) % ZH, s) for s in range(ZH)])


def from_z(block, step):
    pairs = []
    for t in range(ZL * CORES):
        for s in range(ZH):
            z = (s * ZL + t // CORES + step) % (ZL * ZH)
            pairs.append((((z % ZL) * CORES + t % CORES) * ZH + z // ZL, t * ZH + s))
    return lax.ppermute(block, ("tp", "dp"), pairs)


def pair_kernel(first_ref, second_ref, out_ref):
    out_ref[0] = first_ref[...]
    out_ref[1] = second_ref[...]


def pair(first, second):
    return pl.pallas_call(
        pair_kernel,
        out_shape=jax.ShapeDtypeStruct((2,) + first.shape, first.dtype),
        in_specs=[VMEM] * 2,
        out_specs=VMEM,
        compiler_params=params(4),
        cost_estimate=pl.CostEstimate(flops=0, bytes_accessed=8 * first.size, transcendentals=0),
        name="pair",
    )(first, second)


def rows_of(block_refs):
    return jnp.concatenate([r[...].reshape(-1, r.shape[-1]) for r in block_refs], axis=0)


def accumulate(total_ref, term):
    level = pl.program_id(0)

    @pl.when(level == 0)
    def _():
        total_ref[...] = term

    @pl.when(level > 0)
    def _():
        total_ref[...] += term


def project_kernel(*refs):
    *block_refs, weight_ref, out_ref, total_ref = refs
    accumulate(
        total_ref, jnp.dot(rows_of(block_refs), weight_ref[0], preferred_element_type=jnp.float32)
    )

    @pl.when(pl.program_id(0) == LEVELS - 1)
    def _():
        out_ref[...] = total_ref[...].astype(jnp.bfloat16).reshape(out_ref.shape)


def product_specs(blocks, weight):
    _, _, rows, depth = blocks[0].shape
    specs = [pl.BlockSpec((b.shape[0], 1, rows, depth), lambda l, *_: (0, l, 0, 0)) for b in blocks]
    return specs + [pl.BlockSpec((1, depth, weight.shape[2]), lambda l, *_: (l, 0, 0))]


def product_cost(blocks, weight):
    size = sum(b.size for b in blocks)
    return pl.CostEstimate(flops=0, bytes_accessed=2 * size, transcendentals=0)


def project(blocks, weight):
    rows, width = blocks[0].shape[2], weight.shape[2]
    count = sum(b.shape[0] for b in blocks)
    return pl.pallas_call(
        project_kernel,
        grid=(LEVELS,),
        out_shape=jax.ShapeDtypeStruct((count, rows, width), jnp.bfloat16),
        in_specs=product_specs(blocks, weight),
        out_specs=pl.BlockSpec((count, rows, width), lambda l: (0, 0, 0)),
        scratch_shapes=[pltpu.VMEM((count * rows, width), jnp.float32)],
        compiler_params=params(14),
        cost_estimate=product_cost(blocks, weight),
        name="project",
    )(*blocks, weight)


def project_place_kernel(meta_ref, *refs):
    *block_refs, weight_ref, zero_ref, sides_ref, keep_ref, send_ref, total_ref, token_ref = refs
    accumulate(
        total_ref, jnp.dot(rows_of(block_refs), weight_ref[0], preferred_element_type=jnp.float32)
    )

    @pl.when(pl.program_id(0) == LEVELS - 1)
    def _():
        core, x, y = meta_ref[0], meta_ref[1], meta_ref[2]
        rows = zero_ref.shape[1]
        total = rows * X * Y
        edge = jnp.zeros((HALO, token_ref.shape[1]), jnp.float32)
        token_ref[pl.ds(0, HALO), :] = edge
        token_ref[pl.ds(HALO + total, HALO), :] = edge
        for second in range(4):
            for first in range(4):
                dx = jnp.where(core == 0, first, second)
                dy = jnp.where(core == 0, second, first)
                e = lax.rem(x + dx, X) * Y + lax.rem(y + dy, Y)
                at = pl.multiple_of(e * rows + HALO, 8)
                if second == 0:
                    block = zero_ref[first].astype(jnp.float32)
                elif second == 2:
                    block = total_ref[pl.ds(first * rows, rows), :]
                else:
                    block = sides_ref[second // 2 * 4 + first].astype(jnp.float32)
                token_ref[pl.ds(at, rows), :] = block
        piece = total // (ZL * CORES)
        for zl in range(ZL):
            for out_ref, whose in ((keep_ref, core), (send_ref, 1 - core)):
                at = pl.multiple_of((zl * CORES + whose) * piece, 8)
                out_ref[zl] = token_ref[pl.ds(at, piece + 2 * HALO), :].astype(jnp.bfloat16)


def project_place(blocks, weight, zero, sides, core, x, y):
    _, rows, width = zero.shape
    count = sum(b.shape[0] for b in blocks)
    total = rows * X * Y
    pieces = (ZL, total // (ZL * CORES) + 2 * HALO, width)
    whole = lambda shape: pl.BlockSpec(shape, lambda l, *_: (0, 0, 0))
    return pl.pallas_call(
        project_place_kernel,
        out_shape=(jax.ShapeDtypeStruct(pieces, jnp.bfloat16),) * 2,
        grid_spec=pltpu.PrefetchScalarGridSpec(
            num_scalar_prefetch=1,
            grid=(LEVELS,),
            in_specs=product_specs(blocks, weight) + [whole(zero.shape), whole(sides.shape)],
            out_specs=(whole(pieces),) * 2,
            scratch_shapes=[
                pltpu.VMEM((count * rows, width), jnp.float32),
                pltpu.VMEM((total + 2 * HALO, width), jnp.float32),
            ],
        ),
        compiler_params=params(18),
        cost_estimate=product_cost(blocks, weight),
        name="project_place",
    )(jnp.stack([core, x, y]), *blocks, weight, zero, sides)


def join_kernel(meta_ref, keep_ref, got_ref, own_ref, *away_refs):
    zl = meta_ref[0]

    def piece(index):
        return keep_ref[index].astype(jnp.float32) + got_ref[index].astype(jnp.float32)

    own_ref[...] = piece(zl).astype(jnp.bfloat16)
    for step, away_ref in zip((1, 2, 3), away_refs):
        away_ref[...] = piece(lax.rem(zl + ZL - step, ZL)).astype(jnp.bfloat16)


def join(keep, got, zl):
    count, rows, width = keep.shape
    whole = pl.BlockSpec(keep.shape, lambda i, m: (0, 0, 0))
    piece = pl.BlockSpec((rows, width), lambda i, m: (0, 0))
    return pl.pallas_call(
        join_kernel,
        out_shape=(jax.ShapeDtypeStruct((rows, width), jnp.bfloat16),) * count,
        grid_spec=pltpu.PrefetchScalarGridSpec(
            num_scalar_prefetch=1, grid=(1,), in_specs=[whole] * 2, out_specs=(piece,) * count
        ),
        compiler_params=params(8),
        cost_estimate=pl.CostEstimate(
            flops=keep.size, bytes_accessed=6 * keep.size, transcendentals=0
        ),
        name="join",
    )(zl.reshape(1), keep, got)


def sigmoid(v):
    return 1.0 / (1.0 + jnp.exp(-v))


def chain_kernel(meta_ref, scale_ref, *refs):
    *part_refs, high_ref, gain_ref, grad_ref = refs
    rows, width = part_refs[0].shape
    own = rows - 2 * HALO
    joined = part_refs[0][...].astype(jnp.float32)
    for part_ref in part_refs[1:]:
        joined = joined + part_ref[...].astype(jnp.float32)
    high = high_ref[...].astype(jnp.float32)
    gain = gain_ref[...]
    scale = scale_ref[0]
    start, length = meta_ref[0], meta_ref[1]
    position = start - HALO + lax.broadcasted_iota(jnp.int32, (rows, width), 0)

    def down(values):
        return jnp.concatenate([jnp.zeros((1, width), jnp.float32), values[:-1]], axis=0)

    def up(values):
        return jnp.concatenate([values[1:], jnp.zeros((1, width), jnp.float32)], axis=0)

    def target(step):
        lead = jnp.zeros((HALO - step, width), jnp.float32)
        return jnp.concatenate([lead, high[: rows - HALO + step]], axis=0)

    def state_and_slope(v):
        gate = sigmoid(v)
        return v * gate, gate * (1.0 + v * (1.0 - gate))

    def residual(state, step):
        return jnp.where(position + step < length, scale * (state - target(step)), 0.0)

    state_1, slope_1 = state_and_slope(joined)
    before_1 = down(state_1)
    state_2, slope_2 = state_and_slope(joined + gain * before_1)
    before_2 = down(state_2)
    state_3, slope_3 = state_and_slope(joined + gain * before_2)
    delta_3 = residual(state_3, 3) * slope_3
    delta_2 = (residual(state_2, 2) + up(gain * delta_3)) * slope_2
    delta_1 = (residual(state_1, 1) + up(gain * delta_2)) * slope_1
    total = delta_1 + delta_2 + delta_3
    mix = (delta_2 * before_1 + delta_3 * before_2)[HALO : HALO + own]
    rest = jnp.sum(mix, axis=0, keepdims=True)
    tail = []
    for _ in range(3):
        term = rest.astype(jnp.bfloat16).astype(jnp.float32)
        tail.append(term)
        rest = rest - term
    tail.append(jnp.zeros((TAIL - 3, width), jnp.float32))
    grad_ref[pl.ds(0, own), :] = total[HALO : HALO + own].astype(jnp.bfloat16)
    grad_ref[pl.ds(own, TAIL), :] = jnp.concatenate(tail, axis=0).astype(jnp.bfloat16)


def chain(parts, high, gain, start, length, scale):
    rows, width = parts[0].shape
    own = rows - 2 * HALO
    return pl.pallas_call(
        chain_kernel,
        out_shape=jax.ShapeDtypeStruct((own + TAIL, width), jnp.bfloat16),
        in_specs=[SMEM, SMEM] + [VMEM] * (len(parts) + 2),
        out_specs=VMEM,
        compiler_params=params(14),
        cost_estimate=pl.CostEstimate(
            flops=60 * rows * width, bytes_accessed=10 * rows * width, transcendentals=3 * rows * width
        ),
        name="chain",
    )(jnp.stack([start, length]), scale.reshape(1), *parts, high, gain.reshape(1, width))


def weight_grad_kernel(meta_ref, features_ref, *refs):
    *group_refs, out_ref, mix_ref, got_ref, grads_ref, held_ref, got_sem, held_sem = refs
    half = grads_ref.shape[1] // ZH
    width = grads_ref.shape[2]
    got = [
        pltpu.make_async_copy(group_ref, got_ref.at[at], got_sem.at[at])
        for at, group_ref in enumerate(group_refs)
    ]
    held = [
        pltpu.make_async_copy(features_ref.at[:, at], held_ref.at[at], held_sem.at[at])
        for at in range(LEVELS)
    ]
    for copy in got:
        copy.start()
    mix = jnp.zeros((TAIL, width), jnp.float32)
    for at, copy in enumerate(got):
        copy.wait()
        if at == len(got) // 2:
            for later in held:
                later.start()
        for part in range(2):
            slab = grads_ref.at[meta_ref[at] * 2 + part]
            for sequence in range(ZH):
                rows = got_ref[at, sequence, pl.ds(part * half, half), :]
                slab[pl.ds(sequence * half, half), :] = rows
        for sequence in range(ZH):
            mix = mix + got_ref[at, sequence, pl.ds(2 * half, TAIL), :].astype(jnp.float32)
    mix_ref[...] = jnp.sum(mix, axis=0, keepdims=True)
    blocks = held_ref.shape[1]
    for at, copy in enumerate(held):
        copy.wait()
        left = jnp.concatenate([held_ref[at, e] for e in range(blocks)], axis=1)
        right = grads_ref[...].reshape(-1, width)
        term = jnp.dot(left, right, preferred_element_type=jnp.float32)
        out_ref[at] = term.astype(jnp.bfloat16)


def weight_grad(features, groups, members):
    draft, _, columns, tokens = features.shape
    count, width = len(groups), groups[0].shape[2]
    hbm = pl.BlockSpec(memory_space=pltpu.HBM)
    return pl.pallas_call(
        weight_grad_kernel,
        out_shape=(
            jax.ShapeDtypeStruct((LEVELS, columns, width), jnp.bfloat16),
            jax.ShapeDtypeStruct((1, width), jnp.float32),
        ),
        in_specs=[SMEM] + [hbm] * (count + 1),
        out_specs=(VMEM, VMEM),
        scratch_shapes=[
            pltpu.VMEM((count,) + groups[0].shape, jnp.bfloat16),
            pltpu.VMEM((draft, tokens, width), jnp.bfloat16),
            pltpu.VMEM((LEVELS, draft, columns, tokens), jnp.bfloat16),
            pltpu.SemaphoreType.DMA((count,)),
            pltpu.SemaphoreType.DMA((LEVELS,)),
        ],
        compiler_params=params(58),
        cost_estimate=pl.CostEstimate(
            flops=2 * draft * LEVELS * columns * tokens * width,
            bytes_accessed=2 * features.size + 2 * draft * tokens * width,
            transcendentals=0,
        ),
        name="weight_grad",
    )(jnp.stack(members), features, *groups)


def turn_kernel(meta_ref, features_ref, out_ref):
    del meta_ref
    rows = features_ref[:, 0].reshape(-1, features_ref.shape[3])
    out_ref[0] = rows.astype(jnp.float32).T.astype(jnp.bfloat16)


def turn(sequences, zh):
    count, levels, rows, depth = sequences.shape
    part = depth // ZH
    return pl.pallas_call(
        turn_kernel,
        out_shape=jax.ShapeDtypeStruct((levels, part, count * rows), jnp.bfloat16),
        grid_spec=pltpu.PrefetchScalarGridSpec(
            num_scalar_prefetch=1,
            grid=(levels,),
            in_specs=[pl.BlockSpec((count, 1, rows, part), lambda l, m: (0, l, 0, m[0]))],
            out_specs=pl.BlockSpec((1, part, count * rows), lambda l, m: (l, 0, 0)),
        ),
        compiler_params=params(8),
        cost_estimate=pl.CostEstimate(flops=0, bytes_accessed=sequences.size, transcendentals=0),
        name="turn",
    )(zh.reshape(1), sequences)


def valid_total(lengths):
    running = jnp.zeros((), jnp.float32)
    for unroll in range(1, UNROLL + 1):
        running = running + jnp.sum(jnp.maximum(lengths - unroll, 0)).astype(jnp.float32)
    return running


def send_high(top, draft_index):
    members, draft_count = ZL * CORES, X * Y
    width = top.shape[1] // 2
    even = draft_index % 2 == 0
    left, right = top[:, :width], top[:, width:]
    straight, crossed, after_left, after_right = [], [], [], []
    for t in range(members):
        for e in range(draft_count):
            source = t * draft_count + e
            target = e // 2 * draft_count + 2 * t
            straight.append((source, target + e % 2))
            crossed.append((source, target + 1 - e % 2))
            if e % 2 == 0 and e > 0:
                after_left.append((source, target - draft_count))
                after_right.append((source, target - draft_count + 1))
    axes = ("tp", "draft")
    return (
        lax.ppermute(jnp.where(even, left, right), axes, straight),
        lax.ppermute(jnp.where(even, right, left), axes, crossed),
        lax.ppermute(left[:TAIL], axes, after_left),
        lax.ppermute(right[:TAIL], axes, after_right),
    )


def high_rows(one, two, after_left, after_right, draft_index):
    even = draft_index % 2 == 0
    after = jnp.where(even, after_left, after_right)
    return jnp.concatenate([jnp.where(even, one, two), jnp.where(even, two, one), after], axis=0)


def gather_grads(grad, features, zl, core):
    stack = lax.all_gather(grad, "dp", axis=0, tiled=False)
    above, below = from_z(stack, 1), from_z(stack, -1)
    far = jnp.concatenate([from_z(stack[:2], 2), from_z(stack[2:], -2)])
    other = from_other_core(stack)
    above, below, other, far = lax.optimization_barrier((above, below, other, far))
    swapped = [from_other_core(block) for block in (above, below, far)]

    def member(step, of_core):
        return (zl + step) % ZL * CORES + of_core

    groups = [stack, other, above, below, far] + swapped
    members = [member(0, core), member(0, 1 - core)]
    members += [member(step, core) for step in (1, 3, 2)]
    members += [member(step, 1 - core) for step in (1, 3, 2)]
    return weight_grad(features, groups, members)


def local(features, fc_weight, mix_gain, lengths):
    tp_index, zh = lax.axis_index("tp"), lax.axis_index("dp")
    draft_index = lax.axis_index("draft")
    zl, core = tp_index // CORES, tp_index % CORES
    x, y = draft_index // Y, draft_index % Y
    own_rows = features.shape[0]
    piece = own_rows * X * Y // (ZL * CORES)
    own = features.transpose(1, 0, 2)
    weight = fc_weight.transpose(1, 0, 2)

    sequences = lax.all_gather(own, "dp", axis=0, tiled=False)
    next_, last, across = (plane_move(step, True)(own) for step in (1, 3, 2))
    low, high = pair(own, next_), pair(across, last)
    up_low, down_high = plane_move(1, False)(low), plane_move(-1, False)(high)
    up_high, down_low = plane_move(1, False)(high), plane_move(-1, False)(low)
    zero = project([low, high], weight)
    up_low, down_high, zero, later = lax.optimization_barrier(
        (up_low, down_high, zero, own)
    )
    far_low, far_high = plane_move(1, False)(up_low), plane_move(-1, False)(down_high)
    halves = send_high(later[LEVELS - 1], draft_index)
    sides = project([up_low, up_high, down_low, down_high], weight)
    far_low, far_high, halves, sides = lax.optimization_barrier((far_low, far_high, halves, sides))
    keep, send = project_place([far_low, far_high], weight, zero, sides, core, x, y)
    mine, *away = join(keep, from_other_core(send), zl)
    parts = [mine] + [from_zl(block, step) for step, block in zip((1, 2, 3), away)]
    parts, sequences = lax.optimization_barrier((parts, sequences))
    every = lax.all_gather(turn(sequences, zh), "draft", axis=0, tiled=False)
    scale = LOSS_SCALE / valid_total(lengths)
    target = high_rows(*halves, draft_index)
    grad = chain(parts, target, mix_gain, tp_index * piece, lengths[zh], scale)
    fc_grad, mix_total = gather_grads(grad, every, zl, core)
    return (fc_grad.transpose(1, 0, 2), mix_total[0])


def solution(mesh):
    placed = (P(("dp", "draft"), None, "tp"), P("tp", None, "draft"), P("draft"), P())
    return jax.shard_map(
        local,
        mesh=mesh,
        in_specs=placed,
        out_specs=(P(("tp", "dp"), None, "draft"), P("draft")),
        check_vma=False,
    )
```

```python
import jax
import jax.numpy as jnp
from jax import lax
from jax.experimental import pallas as pl
from jax.experimental.pallas import tpu as pltpu
from jax.sharding import PartitionSpec as P

LEVELS = 3
UNROLL = 3
LOSS_SCALE = 64.0
HALO = 8
TAIL = 16
X, Y = 4, 4
ZL, CORES, ZH = 4, 2, 4
VMEM = pl.BlockSpec(memory_space=pltpu.VMEM)
SMEM = pl.BlockSpec(memory_space=pltpu.SMEM)


def params(mebibytes):
    return pltpu.CompilerParams(vmem_limit_bytes=mebibytes << 20)


def plane_move(step, first):
    pairs = []
    for t in range(ZL * CORES):
        for x in range(X):
            for y in range(Y):
                along_x = (t % CORES == 0) == first
                source = (x + step) % X * Y + y if along_x else x * Y + (y + step) % Y
                pairs.append((t * X * Y + source, t * X * Y + x * Y + y))
    return lambda block: lax.ppermute(block, ("tp", "draft"), pairs)


def from_other_core(block):
    return lax.ppermute(block, "tp", [(t ^ 1, t) for t in range(ZL * CORES)])


def from_zl(block, step):
    pairs = [((t // CORES + step) % ZL * CORES + t % CORES, t) for t in range(ZL * CORES)]
    return lax.ppermute(block, "tp", pairs)


def from_zh(block, step):
    return lax.ppermute(block, "dp", [((s + step) % ZH, s) for s in range(ZH)])


def from_z(block, step):
    pairs = []
    for t in range(ZL * CORES):
        for s in range(ZH):
            z = (s * ZL + t // CORES + step) % (ZL * ZH)
            pairs.append((((z % ZL) * CORES + t % CORES) * ZH + z // ZL, t * ZH + s))
    return lax.ppermute(block, ("tp", "dp"), pairs)


def pair_kernel(first_ref, second_ref, out_ref):
    out_ref[0] = first_ref[...]
    out_ref[1] = second_ref[...]


def pair(first, second):
    return pl.pallas_call(
        pair_kernel,
        out_shape=jax.ShapeDtypeStruct((2,) + first.shape, first.dtype),
        in_specs=[VMEM] * 2,
        out_specs=VMEM,
        compiler_params=params(4),
        cost_estimate=pl.CostEstimate(flops=0, bytes_accessed=8 * first.size, transcendentals=0),
        name="pair",
    )(first, second)


def rows_of(block_refs):
    return jnp.concatenate([r[...].reshape(-1, r.shape[-1]) for r in block_refs], axis=0)


def accumulate(total_ref, term):
    level = pl.program_id(0)

    @pl.when(level == 0)
    def _():
        total_ref[...] = term

    @pl.when(level > 0)
    def _():
        total_ref[...] += term


def project_kernel(*refs):
    *block_refs, weight_ref, out_ref, total_ref = refs
    accumulate(
        total_ref, jnp.dot(rows_of(block_refs), weight_ref[0], preferred_element_type=jnp.float32)
    )

    @pl.when(pl.program_id(0) == LEVELS - 1)
    def _():
        out_ref[...] = total_ref[...].astype(jnp.bfloat16).reshape(out_ref.shape)


def product_specs(blocks, weight):
    _, _, rows, depth = blocks[0].shape
    specs = [pl.BlockSpec((b.shape[0], 1, rows, depth), lambda l, *_: (0, l, 0, 0)) for b in blocks]
    return specs + [pl.BlockSpec((1, depth, weight.shape[2]), lambda l, *_: (l, 0, 0))]


def product_cost(blocks, weight):
    size = sum(b.size for b in blocks)
    return pl.CostEstimate(flops=0, bytes_accessed=2 * size, transcendentals=0)


def project(blocks, weight, mebibytes):
    rows, width = blocks[0].shape[2], weight.shape[2]
    count = sum(b.shape[0] for b in blocks)
    return pl.pallas_call(
        project_kernel,
        grid=(LEVELS,),
        out_shape=jax.ShapeDtypeStruct((count, rows, width), jnp.bfloat16),
        in_specs=product_specs(blocks, weight),
        out_specs=pl.BlockSpec((count, rows, width), lambda l: (0, 0, 0)),
        scratch_shapes=[pltpu.VMEM((count * rows, width), jnp.float32)],
        compiler_params=params(mebibytes),
        cost_estimate=product_cost(blocks, weight),
        name="project",
    )(*blocks, weight)


def project_place_kernel(meta_ref, *refs):
    *block_refs, weight_ref, zero_ref, sides_ref, keep_ref, send_ref, total_ref, token_ref = refs
    accumulate(
        total_ref, jnp.dot(rows_of(block_refs), weight_ref[0], preferred_element_type=jnp.float32)
    )

    @pl.when(pl.program_id(0) == LEVELS - 1)
    def _():
        core, x, y = meta_ref[0], meta_ref[1], meta_ref[2]
        rows = zero_ref.shape[1]
        total = rows * X * Y
        edge = jnp.zeros((HALO, token_ref.shape[1]), jnp.float32)
        token_ref[pl.ds(0, HALO), :] = edge
        token_ref[pl.ds(HALO + total, HALO), :] = edge
        for second in range(4):
            for first in range(4):
                dx = jnp.where(core == 0, first, second)
                dy = jnp.where(core == 0, second, first)
                e = lax.rem(x + dx, X) * Y + lax.rem(y + dy, Y)
                at = pl.multiple_of(e * rows + HALO, 8)
                if second == 0:
                    block = zero_ref[first].astype(jnp.float32)
                elif second == 2:
                    block = total_ref[pl.ds(first * rows, rows), :]
                else:
                    block = sides_ref[second // 2 * 4 + first].astype(jnp.float32)
                token_ref[pl.ds(at, rows), :] = block
        piece = total // (ZL * CORES)
        for zl in range(ZL):
            for out_ref, whose in ((keep_ref, core), (send_ref, 1 - core)):
                at = pl.multiple_of((zl * CORES + whose) * piece, 8)
                out_ref[zl] = token_ref[pl.ds(at, piece + 2 * HALO), :].astype(jnp.bfloat16)


def project_place(blocks, weight, zero, sides, core, x, y):
    _, rows, width = zero.shape
    count = sum(b.shape[0] for b in blocks)
    total = rows * X * Y
    pieces = (ZL, total // (ZL * CORES) + 2 * HALO, width)
    whole = lambda shape: pl.BlockSpec(shape, lambda l, *_: (0, 0, 0))
    return pl.pallas_call(
        project_place_kernel,
        out_shape=(jax.ShapeDtypeStruct(pieces, jnp.bfloat16),) * 2,
        grid_spec=pltpu.PrefetchScalarGridSpec(
            num_scalar_prefetch=1,
            grid=(LEVELS,),
            in_specs=product_specs(blocks, weight) + [whole(zero.shape), whole(sides.shape)],
            out_specs=(whole(pieces),) * 2,
            scratch_shapes=[
                pltpu.VMEM((count * rows, width), jnp.float32),
                pltpu.VMEM((total + 2 * HALO, width), jnp.float32),
            ],
        ),
        compiler_params=params(18),
        cost_estimate=product_cost(blocks, weight),
        name="project_place",
    )(jnp.stack([core, x, y]), *blocks, weight, zero, sides)


def join_kernel(meta_ref, keep_ref, got_ref, own_ref, *away_refs):
    zl = meta_ref[0]

    def piece(index):
        return keep_ref[index].astype(jnp.float32) + got_ref[index].astype(jnp.float32)

    own_ref[...] = piece(zl).astype(jnp.bfloat16)
    for step, away_ref in zip((1, 2, 3), away_refs):
        away_ref[...] = piece(lax.rem(zl + ZL - step, ZL)).astype(jnp.bfloat16)


def join(keep, got, zl):
    count, rows, width = keep.shape
    whole = pl.BlockSpec(keep.shape, lambda i, m: (0, 0, 0))
    piece = pl.BlockSpec((rows, width), lambda i, m: (0, 0))
    return pl.pallas_call(
        join_kernel,
        out_shape=(jax.ShapeDtypeStruct((rows, width), jnp.bfloat16),) * count,
        grid_spec=pltpu.PrefetchScalarGridSpec(
            num_scalar_prefetch=1, grid=(1,), in_specs=[whole] * 2, out_specs=(piece,) * count
        ),
        compiler_params=params(8),
        cost_estimate=pl.CostEstimate(
            flops=keep.size, bytes_accessed=6 * keep.size, transcendentals=0
        ),
        name="join",
    )(zl.reshape(1), keep, got)


def sigmoid(v):
    return 1.0 / (1.0 + jnp.exp(-v))


def chain_kernel(meta_ref, scale_ref, *refs):
    *part_refs, one_ref, two_ref, left_ref, right_ref, gain_ref, grad_ref = refs
    rows, width = part_refs[0].shape
    own = rows - 2 * HALO
    joined = part_refs[0][...].astype(jnp.float32)
    for part_ref in part_refs[1:]:
        joined = joined + part_ref[...].astype(jnp.float32)
    even = meta_ref[2] == 0
    pick = lambda a, b: jnp.where(even, a[...].astype(jnp.float32), b[...].astype(jnp.float32))
    high = jnp.concatenate(
        [pick(one_ref, two_ref), pick(two_ref, one_ref), pick(left_ref, right_ref)], axis=0
    )
    gain = gain_ref[...]
    scale = scale_ref[0]
    start, length = meta_ref[0], meta_ref[1]
    position = start - HALO + lax.broadcasted_iota(jnp.int32, (rows, width), 0)

    def down(values):
        return jnp.concatenate([jnp.zeros((1, width), jnp.float32), values[:-1]], axis=0)

    def up(values):
        return jnp.concatenate([values[1:], jnp.zeros((1, width), jnp.float32)], axis=0)

    def target(step):
        lead = jnp.zeros((HALO - step, width), jnp.float32)
        return jnp.concatenate([lead, high[: rows - HALO + step]], axis=0)

    def state_and_slope(v):
        gate = sigmoid(v)
        return v * gate, gate * (1.0 + v * (1.0 - gate))

    def residual(state, step):
        return jnp.where(position + step < length, scale * (state - target(step)), 0.0)

    state_1, slope_1 = state_and_slope(joined)
    before_1 = down(state_1)
    state_2, slope_2 = state_and_slope(joined + gain * before_1)
    before_2 = down(state_2)
    state_3, slope_3 = state_and_slope(joined + gain * before_2)
    delta_3 = residual(state_3, 3) * slope_3
    delta_2 = (residual(state_2, 2) + up(gain * delta_3)) * slope_2
    delta_1 = (residual(state_1, 1) + up(gain * delta_2)) * slope_1
    total = delta_1 + delta_2 + delta_3
    mix = (delta_2 * before_1 + delta_3 * before_2)[HALO : HALO + own]
    rest = jnp.sum(mix, axis=0, keepdims=True)
    tail = []
    for _ in range(3):
        term = rest.astype(jnp.bfloat16).astype(jnp.float32)
        tail.append(term)
        rest = rest - term
    tail.append(jnp.zeros((TAIL - 3, width), jnp.float32))
    grad_ref[pl.ds(0, own), :] = total[HALO : HALO + own].astype(jnp.bfloat16)
    grad_ref[pl.ds(own, TAIL), :] = jnp.concatenate(tail, axis=0).astype(jnp.bfloat16)


def chain(parts, halves, gain, start, length, odd, scale):
    rows, width = parts[0].shape
    own = rows - 2 * HALO
    return pl.pallas_call(
        chain_kernel,
        out_shape=jax.ShapeDtypeStruct((own + TAIL, width), jnp.bfloat16),
        in_specs=[SMEM, SMEM] + [VMEM] * (len(parts) + len(halves) + 1),
        out_specs=VMEM,
        compiler_params=params(14),
        cost_estimate=pl.CostEstimate(
            flops=60 * rows * width, bytes_accessed=10 * rows * width, transcendentals=3 * rows * width
        ),
        name="chain",
    )(jnp.stack([start, length, odd]), scale.reshape(1), *parts, *halves, gain.reshape(1, width))


def weight_grad_kernel(meta_ref, features_ref, *refs):
    *group_refs, out_ref, mix_ref, got_ref, grads_ref, held_ref, got_sem, held_sem = refs
    half = grads_ref.shape[1] // ZH
    width = grads_ref.shape[2]
    got = [
        pltpu.make_async_copy(group_ref, got_ref.at[at], got_sem.at[at])
        for at, group_ref in enumerate(group_refs)
    ]
    held = [
        pltpu.make_async_copy(features_ref.at[:, at], held_ref.at[at], held_sem.at[at])
        for at in range(LEVELS)
    ]
    for copy in got:
        copy.start()
    mix = jnp.zeros((TAIL, width), jnp.float32)
    for at, copy in enumerate(got):
        copy.wait()
        if at == len(got) // 2:
            for later in held:
                later.start()
        for part in range(2):
            slab = grads_ref.at[meta_ref[at] * 2 + part]
            for sequence in range(ZH):
                rows = got_ref[at, sequence, pl.ds(part * half, half), :]
                slab[pl.ds(sequence * half, half), :] = rows
        for sequence in range(ZH):
            mix = mix + got_ref[at, sequence, pl.ds(2 * half, TAIL), :].astype(jnp.float32)
    mix_ref[...] = jnp.sum(mix, axis=0, keepdims=True)
    blocks = held_ref.shape[1]
    for at, copy in enumerate(held):
        copy.wait()
        left = jnp.concatenate([held_ref[at, e] for e in range(blocks)], axis=1)
        right = grads_ref[...].reshape(-1, width)
        term = jnp.dot(left, right, preferred_element_type=jnp.float32)
        out_ref[at] = term.astype(jnp.bfloat16)


def weight_grad(features, groups, members):
    draft, _, columns, tokens = features.shape
    count, width = len(groups), groups[0].shape[2]
    hbm = pl.BlockSpec(memory_space=pltpu.HBM)
    return pl.pallas_call(
        weight_grad_kernel,
        out_shape=(
            jax.ShapeDtypeStruct((LEVELS, columns, width), jnp.bfloat16),
            jax.ShapeDtypeStruct((1, width), jnp.float32),
        ),
        in_specs=[SMEM] + [hbm] * (count + 1),
        out_specs=(VMEM, VMEM),
        scratch_shapes=[
            pltpu.VMEM((count,) + groups[0].shape, jnp.bfloat16),
            pltpu.VMEM((draft, tokens, width), jnp.bfloat16),
            pltpu.VMEM((LEVELS, draft, columns, tokens), jnp.bfloat16),
            pltpu.SemaphoreType.DMA((count,)),
            pltpu.SemaphoreType.DMA((LEVELS,)),
        ],
        compiler_params=params(58),
        cost_estimate=pl.CostEstimate(
            flops=2 * draft * LEVELS * columns * tokens * width,
            bytes_accessed=2 * features.size + 2 * draft * tokens * width,
            transcendentals=0,
        ),
        name="weight_grad",
    )(jnp.stack(members), features, *groups)


def turn_kernel(traded_ref, out_ref):
    rows = traded_ref[:, 0].reshape(-1, traded_ref.shape[3])
    out_ref[0] = rows.astype(jnp.float32).T.astype(jnp.bfloat16)


def turn(traded):
    sequences, levels, rows, columns = traded.shape
    return pl.pallas_call(
        turn_kernel,
        grid=(levels,),
        out_shape=jax.ShapeDtypeStruct((levels, columns, sequences * rows), jnp.bfloat16),
        in_specs=[pl.BlockSpec((sequences, 1, rows, columns), lambda l: (0, l, 0, 0))],
        out_specs=pl.BlockSpec((1, columns, sequences * rows), lambda l: (l, 0, 0)),
        compiler_params=params(8),
        cost_estimate=pl.CostEstimate(flops=0, bytes_accessed=4 * traded.size, transcendentals=0),
        name="turn",
    )(traded)


def valid_total(lengths):
    running = jnp.zeros((), jnp.float32)
    for unroll in range(1, UNROLL + 1):
        running = running + jnp.sum(jnp.maximum(lengths - unroll, 0)).astype(jnp.float32)
    return running


def send_high(top, draft_index):
    members, draft_count = ZL * CORES, X * Y
    width = top.shape[1] // 2
    even = draft_index % 2 == 0
    left, right = top[:, :width], top[:, width:]
    straight, crossed, after_left, after_right = [], [], [], []
    for t in range(members):
        for e in range(draft_count):
            source = t * draft_count + e
            target = e // 2 * draft_count + 2 * t
            straight.append((source, target + e % 2))
            crossed.append((source, target + 1 - e % 2))
            if e % 2 == 0 and e > 0:
                after_left.append((source, target - draft_count))
                after_right.append((source, target - draft_count + 1))
    axes = ("tp", "draft")
    return (
        lax.ppermute(jnp.where(even, left, right), axes, straight),
        lax.ppermute(jnp.where(even, right, left), axes, crossed),
        lax.ppermute(left[:TAIL], axes, after_left),
        lax.ppermute(right[:TAIL], axes, after_right),
    )


def trade_columns(own):
    levels, rows, depth = own.shape
    quarters = own.reshape(levels, rows, ZH, depth // ZH).transpose(2, 0, 1, 3)
    return lax.all_to_all(quarters, "dp", split_axis=0, concat_axis=0, tiled=True)


def gather_grads(grad, features, zl, core):
    stack = lax.all_gather(grad, "dp", axis=0, tiled=False)
    above, below = from_z(stack, 1), from_z(stack, -1)
    far = jnp.concatenate([from_z(stack[:2], 2), from_z(stack[2:], -2)])
    other = from_other_core(stack)
    above, below, other, far = lax.optimization_barrier((above, below, other, far))
    swapped = [from_other_core(block) for block in (above, below, far)]

    def member(step, of_core):
        return (zl + step) % ZL * CORES + of_core

    groups = [stack, other, above, below, far] + swapped
    members = [member(0, core), member(0, 1 - core)]
    members += [member(step, core) for step in (1, 3, 2)]
    members += [member(step, 1 - core) for step in (1, 3, 2)]
    return weight_grad(features, groups, members)


def local(features, fc_weight, mix_gain, lengths):
    tp_index, zh = lax.axis_index("tp"), lax.axis_index("dp")
    draft_index = lax.axis_index("draft")
    zl, core = tp_index // CORES, tp_index % CORES
    x, y = draft_index // Y, draft_index % Y
    own_rows = features.shape[0]
    piece = own_rows * X * Y // (ZL * CORES)
    own = features.transpose(1, 0, 2)
    weight = fc_weight.transpose(1, 0, 2)

    next_, last, across = (plane_move(step, True)(own) for step in (1, 3, 2))
    low, high = pair(own, next_), pair(across, last)
    up_low, down_high = plane_move(1, False)(low), plane_move(-1, False)(high)
    up_high, down_low = plane_move(1, False)(high), plane_move(-1, False)(low)
    zero = project([low, high], weight, 14)
    up_low, down_high, zero = lax.optimization_barrier((up_low, down_high, zero))
    far_low, far_high = plane_move(1, False)(up_low), plane_move(-1, False)(down_high)
    up_high, down_low, later = lax.optimization_barrier((up_high, down_low, own))
    traded = trade_columns(later)
    sides = project([up_low, up_high, down_low, down_high], weight, 58)
    far_low, far_high, sides = lax.optimization_barrier((far_low, far_high, sides))
    keep, send = project_place([far_low, far_high], weight, zero, sides, core, x, y)
    got, traded = lax.optimization_barrier((from_other_core(send), traded))
    every = lax.all_gather(turn(traded), "draft", axis=0, tiled=False)
    mine, *away = join(keep, got, zl)
    top, mine = lax.optimization_barrier((own[LEVELS - 1], mine))
    halves = send_high(top, draft_index)
    parts = [mine] + [from_zl(block, step) for step, block in zip((1, 2, 3), away)]
    scale = LOSS_SCALE / valid_total(lengths)
    odd = draft_index % 2
    grad = chain(parts, halves, mix_gain, tp_index * piece, lengths[zh], odd, scale)
    fc_grad, mix_total = gather_grads(grad, every, zl, core)
    return (fc_grad.transpose(1, 0, 2), mix_total[0])


def solution(mesh):
    placed = (P(("dp", "draft"), None, "tp"), P("tp", None, "draft"), P("draft"), P())
    return jax.shard_map(
        local,
        mesh=mesh,
        in_specs=placed,
        out_specs=(P(("tp", "dp"), None, "draft"), P("draft")),
        check_vma=False,
    )
```

```python
import jax
import jax.numpy as jnp
from jax import lax
from jax.experimental import pallas as pl
from jax.experimental.pallas import tpu as pltpu
from jax.sharding import PartitionSpec as P

LEVELS = 3
UNROLL = 3
LOSS_SCALE = 64.0
HALO = 8
TAIL = 16
X, Y = 4, 4
ZL, CORES, ZH = 4, 2, 4
VMEM = pl.BlockSpec(memory_space=pltpu.VMEM)
SMEM = pl.BlockSpec(memory_space=pltpu.SMEM)


def params(mebibytes):
    return pltpu.CompilerParams(vmem_limit_bytes=mebibytes << 20)


def plane_move(step, first):
    pairs = []
    for t in range(ZL * CORES):
        for x in range(X):
            for y in range(Y):
                along_x = (t % CORES == 0) == first
                source = (x + step) % X * Y + y if along_x else x * Y + (y + step) % Y
                pairs.append((t * X * Y + source, t * X * Y + x * Y + y))
    return lambda block: lax.ppermute(block, ("tp", "draft"), pairs)


def from_other_core(block):
    return lax.ppermute(block, "tp", [(t ^ 1, t) for t in range(ZL * CORES)])


def from_zl(block, step):
    pairs = [((t // CORES + step) % ZL * CORES + t % CORES, t) for t in range(ZL * CORES)]
    return lax.ppermute(block, "tp", pairs)


def from_zh(block, step):
    return lax.ppermute(block, "dp", [((s + step) % ZH, s) for s in range(ZH)])


def from_z(block, step):
    pairs = []
    for t in range(ZL * CORES):
        for s in range(ZH):
            z = (s * ZL + t // CORES + step) % (ZL * ZH)
            pairs.append((((z % ZL) * CORES + t % CORES) * ZH + z // ZL, t * ZH + s))
    return lax.ppermute(block, ("tp", "dp"), pairs)


def pair_kernel(first_ref, second_ref, out_ref):
    out_ref[0] = first_ref[...]
    out_ref[1] = second_ref[...]


def pair(first, second):
    return pl.pallas_call(
        pair_kernel,
        out_shape=jax.ShapeDtypeStruct((2,) + first.shape, first.dtype),
        in_specs=[VMEM] * 2,
        out_specs=VMEM,
        compiler_params=params(4),
        cost_estimate=pl.CostEstimate(flops=0, bytes_accessed=8 * first.size, transcendentals=0),
        name="pair",
    )(first, second)


def rows_of(block_refs):
    return jnp.concatenate([r[...].reshape(-1, r.shape[-1]) for r in block_refs], axis=0)


def accumulate(total_ref, term):
    level = pl.program_id(0)

    @pl.when(level == 0)
    def _():
        total_ref[...] = term

    @pl.when(level > 0)
    def _():
        total_ref[...] += term


def project_kernel(*refs):
    *block_refs, weight_ref, out_ref, total_ref = refs
    accumulate(
        total_ref, jnp.dot(rows_of(block_refs), weight_ref[0], preferred_element_type=jnp.float32)
    )

    @pl.when(pl.program_id(0) == LEVELS - 1)
    def _():
        out_ref[...] = total_ref[...].astype(jnp.bfloat16).reshape(out_ref.shape)


def product_specs(blocks, weight):
    _, _, rows, depth = blocks[0].shape
    specs = [pl.BlockSpec((b.shape[0], 1, rows, depth), lambda l, *_: (0, l, 0, 0)) for b in blocks]
    return specs + [pl.BlockSpec((1, depth, weight.shape[2]), lambda l, *_: (l, 0, 0))]


def product_cost(blocks, weight):
    size = sum(b.size for b in blocks)
    return pl.CostEstimate(flops=0, bytes_accessed=2 * size, transcendentals=0)


def project(blocks, weight, mebibytes):
    rows, width = blocks[0].shape[2], weight.shape[2]
    count = sum(b.shape[0] for b in blocks)
    return pl.pallas_call(
        project_kernel,
        grid=(LEVELS,),
        out_shape=jax.ShapeDtypeStruct((count, rows, width), jnp.bfloat16),
        in_specs=product_specs(blocks, weight),
        out_specs=pl.BlockSpec((count, rows, width), lambda l: (0, 0, 0)),
        scratch_shapes=[pltpu.VMEM((count * rows, width), jnp.float32)],
        compiler_params=params(mebibytes),
        cost_estimate=product_cost(blocks, weight),
        name="project",
    )(*blocks, weight)


def project_place_kernel(meta_ref, *refs):
    *block_refs, weight_ref, zero_ref, sides_ref, keep_ref, send_ref, total_ref, token_ref = refs
    accumulate(
        total_ref, jnp.dot(rows_of(block_refs), weight_ref[0], preferred_element_type=jnp.float32)
    )

    @pl.when(pl.program_id(0) == LEVELS - 1)
    def _():
        core, x, y = meta_ref[0], meta_ref[1], meta_ref[2]
        rows = zero_ref.shape[1]
        total = rows * X * Y
        edge = jnp.zeros((HALO, token_ref.shape[1]), jnp.float32)
        token_ref[pl.ds(0, HALO), :] = edge
        token_ref[pl.ds(HALO + total, HALO), :] = edge
        for second in range(4):
            for first in range(4):
                dx = jnp.where(core == 0, first, second)
                dy = jnp.where(core == 0, second, first)
                e = lax.rem(x + dx, X) * Y + lax.rem(y + dy, Y)
                at = pl.multiple_of(e * rows + HALO, 8)
                if second == 0:
                    block = zero_ref[first].astype(jnp.float32)
                elif second == 2:
                    block = total_ref[pl.ds(first * rows, rows), :]
                else:
                    block = sides_ref[second // 2 * 4 + first].astype(jnp.float32)
                token_ref[pl.ds(at, rows), :] = block
        piece = total // (ZL * CORES)
        for zl in range(ZL):
            for out_ref, whose in ((keep_ref, core), (send_ref, 1 - core)):
                at = pl.multiple_of((zl * CORES + whose) * piece, 8)
                out_ref[zl] = token_ref[pl.ds(at, piece + 2 * HALO), :].astype(jnp.bfloat16)


def project_place(blocks, weight, zero, sides, core, x, y):
    _, rows, width = zero.shape
    count = sum(b.shape[0] for b in blocks)
    total = rows * X * Y
    pieces = (ZL, total // (ZL * CORES) + 2 * HALO, width)
    whole = lambda shape: pl.BlockSpec(shape, lambda l, *_: (0, 0, 0))
    return pl.pallas_call(
        project_place_kernel,
        out_shape=(jax.ShapeDtypeStruct(pieces, jnp.bfloat16),) * 2,
        grid_spec=pltpu.PrefetchScalarGridSpec(
            num_scalar_prefetch=1,
            grid=(LEVELS,),
            in_specs=product_specs(blocks, weight) + [whole(zero.shape), whole(sides.shape)],
            out_specs=(whole(pieces),) * 2,
            scratch_shapes=[
                pltpu.VMEM((count * rows, width), jnp.float32),
                pltpu.VMEM((total + 2 * HALO, width), jnp.float32),
            ],
        ),
        compiler_params=params(18),
        cost_estimate=product_cost(blocks, weight),
        name="project_place",
    )(jnp.stack([core, x, y]), *blocks, weight, zero, sides)


def join_kernel(meta_ref, keep_ref, got_ref, own_ref, *away_refs):
    zl = meta_ref[0]

    def piece(index):
        return keep_ref[index].astype(jnp.float32) + got_ref[index].astype(jnp.float32)

    own_ref[...] = piece(zl).astype(jnp.bfloat16)
    for step, away_ref in zip((1, 2, 3), away_refs):
        away_ref[...] = piece(lax.rem(zl + ZL - step, ZL)).astype(jnp.bfloat16)


def join(keep, got, zl):
    count, rows, width = keep.shape
    whole = pl.BlockSpec(keep.shape, lambda i, m: (0, 0, 0))
    piece = pl.BlockSpec((rows, width), lambda i, m: (0, 0))
    return pl.pallas_call(
        join_kernel,
        out_shape=(jax.ShapeDtypeStruct((rows, width), jnp.bfloat16),) * count,
        grid_spec=pltpu.PrefetchScalarGridSpec(
            num_scalar_prefetch=1, grid=(1,), in_specs=[whole] * 2, out_specs=(piece,) * count
        ),
        compiler_params=params(8),
        cost_estimate=pl.CostEstimate(
            flops=keep.size, bytes_accessed=6 * keep.size, transcendentals=0
        ),
        name="join",
    )(zl.reshape(1), keep, got)


def sigmoid(v):
    return 1.0 / (1.0 + jnp.exp(-v))


def chain_kernel(meta_ref, scale_ref, *refs):
    *part_refs, one_ref, two_ref, left_ref, right_ref, gain_ref, grad_ref = refs
    rows, width = part_refs[0].shape
    own = rows - 2 * HALO
    joined = part_refs[0][...].astype(jnp.float32)
    for part_ref in part_refs[1:]:
        joined = joined + part_ref[...].astype(jnp.float32)
    even = meta_ref[2] == 0
    pick = lambda a, b: jnp.where(even, a[...].astype(jnp.float32), b[...].astype(jnp.float32))
    high = jnp.concatenate(
        [pick(one_ref, two_ref), pick(two_ref, one_ref), pick(left_ref, right_ref)], axis=0
    )
    gain = gain_ref[...]
    scale = scale_ref[0]
    start, length = meta_ref[0], meta_ref[1]
    position = start - HALO + lax.broadcasted_iota(jnp.int32, (rows, width), 0)

    def down(values):
        return jnp.concatenate([jnp.zeros((1, width), jnp.float32), values[:-1]], axis=0)

    def up(values):
        return jnp.concatenate([values[1:], jnp.zeros((1, width), jnp.float32)], axis=0)

    def target(step):
        lead = jnp.zeros((HALO - step, width), jnp.float32)
        return jnp.concatenate([lead, high[: rows - HALO + step]], axis=0)

    def state_and_slope(v):
        gate = sigmoid(v)
        return v * gate, gate * (1.0 + v * (1.0 - gate))

    def residual(state, step):
        return jnp.where(position + step < length, scale * (state - target(step)), 0.0)

    state_1, slope_1 = state_and_slope(joined)
    before_1 = down(state_1)
    state_2, slope_2 = state_and_slope(joined + gain * before_1)
    before_2 = down(state_2)
    state_3, slope_3 = state_and_slope(joined + gain * before_2)
    delta_3 = residual(state_3, 3) * slope_3
    delta_2 = (residual(state_2, 2) + up(gain * delta_3)) * slope_2
    delta_1 = (residual(state_1, 1) + up(gain * delta_2)) * slope_1
    total = delta_1 + delta_2 + delta_3
    mix = (delta_2 * before_1 + delta_3 * before_2)[HALO : HALO + own]
    rest = jnp.sum(mix, axis=0, keepdims=True)
    tail = []
    for _ in range(3):
        term = rest.astype(jnp.bfloat16).astype(jnp.float32)
        tail.append(term)
        rest = rest - term
    tail.append(jnp.zeros((TAIL - 3, width), jnp.float32))
    grad_ref[pl.ds(0, own), :] = total[HALO : HALO + own].astype(jnp.bfloat16)
    grad_ref[pl.ds(own, TAIL), :] = jnp.concatenate(tail, axis=0).astype(jnp.bfloat16)


def chain(parts, halves, gain, start, length, odd, scale):
    rows, width = parts[0].shape
    own = rows - 2 * HALO
    return pl.pallas_call(
        chain_kernel,
        out_shape=jax.ShapeDtypeStruct((own + TAIL, width), jnp.bfloat16),
        in_specs=[SMEM, SMEM] + [VMEM] * (len(parts) + len(halves) + 1),
        out_specs=VMEM,
        compiler_params=params(14),
        cost_estimate=pl.CostEstimate(
            flops=60 * rows * width, bytes_accessed=10 * rows * width, transcendentals=3 * rows * width
        ),
        name="chain",
    )(jnp.stack([start, length, odd]), scale.reshape(1), *parts, *halves, gain.reshape(1, width))


def weight_grad_kernel(meta_ref, features_ref, *refs):
    *group_refs, out_ref, mix_ref, grads_ref = refs
    half = grads_ref.shape[1] // ZH
    width = grads_ref.shape[2]
    mix = jnp.zeros((TAIL, width), jnp.float32)
    for at, group_ref in enumerate(group_refs):
        for part in range(2):
            slab = grads_ref.at[meta_ref[at] * 2 + part]
            for sequence in range(ZH):
                rows = group_ref[sequence, pl.ds(part * half, half), :]
                slab[pl.ds(sequence * half, half), :] = rows
        for sequence in range(ZH):
            mix = mix + group_ref[sequence, pl.ds(2 * half, TAIL), :].astype(jnp.float32)
    mix_ref[...] = jnp.sum(mix, axis=0, keepdims=True)
    blocks = features_ref.shape[0]
    for level in range(LEVELS):
        left = jnp.concatenate([features_ref[e, level] for e in range(blocks)], axis=1)
        right = grads_ref[...].reshape(-1, width)
        term = jnp.dot(left, right, preferred_element_type=jnp.float32)
        out_ref[level] = term.astype(jnp.bfloat16)


def weight_grad(features, groups, members):
    draft, _, columns, tokens = features.shape
    count, width = len(groups), groups[0].shape[2]
    return pl.pallas_call(
        weight_grad_kernel,
        out_shape=(
            jax.ShapeDtypeStruct((LEVELS, columns, width), jnp.bfloat16),
            jax.ShapeDtypeStruct((1, width), jnp.float32),
        ),
        in_specs=[SMEM] + [VMEM] * (count + 1),
        out_specs=(VMEM, VMEM),
        scratch_shapes=[pltpu.VMEM((draft, tokens, width), jnp.bfloat16)],
        compiler_params=params(28),
        cost_estimate=pl.CostEstimate(
            flops=2 * draft * LEVELS * columns * tokens * width,
            bytes_accessed=2 * features.size + 2 * draft * tokens * width,
            transcendentals=0,
        ),
        name="weight_grad",
    )(jnp.stack(members), features, *groups)


def turn_kernel(traded_ref, out_ref):
    rows = traded_ref[:, 0].reshape(-1, traded_ref.shape[3])
    out_ref[0] = rows.astype(jnp.float32).T.astype(jnp.bfloat16)


def turn(traded):
    sequences, levels, rows, columns = traded.shape
    return pl.pallas_call(
        turn_kernel,
        grid=(levels,),
        out_shape=jax.ShapeDtypeStruct((levels, columns, sequences * rows), jnp.bfloat16),
        in_specs=[pl.BlockSpec((sequences, 1, rows, columns), lambda l: (0, l, 0, 0))],
        out_specs=pl.BlockSpec((1, columns, sequences * rows), lambda l: (l, 0, 0)),
        compiler_params=params(8),
        cost_estimate=pl.CostEstimate(flops=0, bytes_accessed=4 * traded.size, transcendentals=0),
        name="turn",
    )(traded)


def valid_total(lengths):
    running = jnp.zeros((), jnp.float32)
    for unroll in range(1, UNROLL + 1):
        running = running + jnp.sum(jnp.maximum(lengths - unroll, 0)).astype(jnp.float32)
    return running


def send_high(top, draft_index):
    members, draft_count = ZL * CORES, X * Y
    width = top.shape[1] // 2
    even = draft_index % 2 == 0
    left, right = top[:, :width], top[:, width:]
    straight, crossed, after_left, after_right = [], [], [], []
    for t in range(members):
        for e in range(draft_count):
            source = t * draft_count + e
            target = e // 2 * draft_count + 2 * t
            straight.append((source, target + e % 2))
            crossed.append((source, target + 1 - e % 2))
            if e % 2 == 0 and e > 0:
                after_left.append((source, target - draft_count))
                after_right.append((source, target - draft_count + 1))
    axes = ("tp", "draft")
    return (
        lax.ppermute(jnp.where(even, left, right), axes, straight),
        lax.ppermute(jnp.where(even, right, left), axes, crossed),
        lax.ppermute(left[:TAIL], axes, after_left),
        lax.ppermute(right[:TAIL], axes, after_right),
    )


def trade_columns(own):
    levels, rows, depth = own.shape
    quarters = own.reshape(levels, rows, ZH, depth // ZH).transpose(2, 0, 1, 3)
    return lax.all_to_all(quarters, "dp", split_axis=0, concat_axis=0, tiled=True)


def gather_grads(grad, features, zl, core):
    stack = lax.all_gather(grad, "dp", axis=0, tiled=False)
    above, below = from_z(stack, 1), from_z(stack, -1)
    far = jnp.concatenate([from_z(stack[:2], 2), from_z(stack[2:], -2)])
    other = from_other_core(stack)
    above, below, other, far, features = lax.optimization_barrier(
        (above, below, other, far, features)
    )
    swapped = [from_other_core(block) for block in (above, below, far)]

    def member(step, of_core):
        return (zl + step) % ZL * CORES + of_core

    groups = [stack, other, above, below, far] + swapped
    members = [member(0, core), member(0, 1 - core)]
    members += [member(step, core) for step in (1, 3, 2)]
    members += [member(step, 1 - core) for step in (1, 3, 2)]
    return weight_grad(features, groups, members)


def local(features, fc_weight, mix_gain, lengths):
    tp_index, zh = lax.axis_index("tp"), lax.axis_index("dp")
    draft_index = lax.axis_index("draft")
    zl, core = tp_index // CORES, tp_index % CORES
    x, y = draft_index // Y, draft_index % Y
    own_rows = features.shape[0]
    piece = own_rows * X * Y // (ZL * CORES)
    own = features.transpose(1, 0, 2)
    weight = fc_weight.transpose(1, 0, 2)

    next_, last, across = (plane_move(step, True)(own) for step in (1, 3, 2))
    low, high = pair(own, next_), pair(across, last)
    up_low, down_high = plane_move(1, False)(low), plane_move(-1, False)(high)
    up_high, down_low = plane_move(1, False)(high), plane_move(-1, False)(low)
    zero = project([low, high], weight, 14)
    up_low, down_high, zero, later = lax.optimization_barrier((up_low, down_high, zero, own))
    traded = trade_columns(later)
    far_low, far_high = plane_move(1, False)(up_low), plane_move(-1, False)(down_high)
    halves = send_high(later[LEVELS - 1], draft_index)
    sides = project([up_low, up_high, down_low, down_high], weight, 58)
    far_low, far_high, halves, sides = lax.optimization_barrier((far_low, far_high, halves, sides))
    keep, send = project_place([far_low, far_high], weight, zero, sides, core, x, y)
    got, traded = lax.optimization_barrier((from_other_core(send), traded))
    every = lax.all_gather(turn(traded), "draft", axis=0, tiled=False)
    mine, *away = join(keep, got, zl)
    parts = [mine] + [from_zl(block, step) for step, block in zip((1, 2, 3), away)]
    scale = LOSS_SCALE / valid_total(lengths)
    odd = draft_index % 2
    grad = chain(parts, halves, mix_gain, tp_index * piece, lengths[zh], odd, scale)
    fc_grad, mix_total = gather_grads(grad, every, zl, core)
    return (fc_grad.transpose(1, 0, 2), mix_total[0])


def solution(mesh):
    placed = (P(("dp", "draft"), None, "tp"), P("tp", None, "draft"), P("draft"), P())
    return jax.shard_map(
        local,
        mesh=mesh,
        in_specs=placed,
        out_specs=(P(("tp", "dp"), None, "draft"), P("draft")),
        check_vma=False,
    )
```

```python
import jax
import jax.numpy as jnp
from jax import lax
from jax.experimental import pallas as pl
from jax.experimental.pallas import tpu as pltpu
from jax.sharding import PartitionSpec as P

LEVELS = 3
UNROLL = 3
LOSS_SCALE = 64.0
HALO = 8
TAIL = 16
X, Y = 4, 4
ZL, CORES, ZH = 4, 2, 4
VMEM = pl.BlockSpec(memory_space=pltpu.VMEM)
SMEM = pl.BlockSpec(memory_space=pltpu.SMEM)


def params(mebibytes):
    return pltpu.CompilerParams(vmem_limit_bytes=mebibytes << 20)


def plane_move(step, first):
    pairs = []
    for t in range(ZL * CORES):
        for x in range(X):
            for y in range(Y):
                along_x = (t % CORES == 0) == first
                source = (x + step) % X * Y + y if along_x else x * Y + (y + step) % Y
                pairs.append((t * X * Y + source, t * X * Y + x * Y + y))
    return lambda block: lax.ppermute(block, ("tp", "draft"), pairs)


def from_other_core(block):
    return lax.ppermute(block, "tp", [(t ^ 1, t) for t in range(ZL * CORES)])


def from_zl(block, step):
    pairs = [((t // CORES + step) % ZL * CORES + t % CORES, t) for t in range(ZL * CORES)]
    return lax.ppermute(block, "tp", pairs)


def from_zh(block, step):
    return lax.ppermute(block, "dp", [((s + step) % ZH, s) for s in range(ZH)])


def from_z(block, step):
    pairs = []
    for t in range(ZL * CORES):
        for s in range(ZH):
            z = (s * ZL + t // CORES + step) % (ZL * ZH)
            pairs.append((((z % ZL) * CORES + t % CORES) * ZH + z // ZL, t * ZH + s))
    return lax.ppermute(block, ("tp", "dp"), pairs)


def pair_kernel(first_ref, second_ref, out_ref):
    out_ref[0] = first_ref[...]
    out_ref[1] = second_ref[...]


def pair(first, second):
    return pl.pallas_call(
        pair_kernel,
        out_shape=jax.ShapeDtypeStruct((2,) + first.shape, first.dtype),
        in_specs=[VMEM] * 2,
        out_specs=VMEM,
        compiler_params=params(4),
        cost_estimate=pl.CostEstimate(flops=0, bytes_accessed=8 * first.size, transcendentals=0),
        name="pair",
    )(first, second)


def rows_of(block_refs):
    return jnp.concatenate([r[...].reshape(-1, r.shape[-1]) for r in block_refs], axis=0)


def accumulate(total_ref, term):
    level = pl.program_id(0)

    @pl.when(level == 0)
    def _():
        total_ref[...] = term

    @pl.when(level > 0)
    def _():
        total_ref[...] += term


def project_kernel(*refs):
    *block_refs, weight_ref, out_ref, total_ref = refs
    accumulate(
        total_ref, jnp.dot(rows_of(block_refs), weight_ref[0], preferred_element_type=jnp.float32)
    )

    @pl.when(pl.program_id(0) == LEVELS - 1)
    def _():
        out_ref[...] = total_ref[...].astype(jnp.bfloat16).reshape(out_ref.shape)


def product_specs(blocks, weight):
    _, _, rows, depth = blocks[0].shape
    specs = [pl.BlockSpec((b.shape[0], 1, rows, depth), lambda l, *_: (0, l, 0, 0)) for b in blocks]
    return specs + [pl.BlockSpec((1, depth, weight.shape[2]), lambda l, *_: (l, 0, 0))]


def product_cost(blocks, weight):
    size = sum(b.size for b in blocks)
    return pl.CostEstimate(flops=0, bytes_accessed=2 * size, transcendentals=0)


def project(blocks, weight, mebibytes):
    rows, width = blocks[0].shape[2], weight.shape[2]
    count = sum(b.shape[0] for b in blocks)
    return pl.pallas_call(
        project_kernel,
        grid=(LEVELS,),
        out_shape=jax.ShapeDtypeStruct((count, rows, width), jnp.bfloat16),
        in_specs=product_specs(blocks, weight),
        out_specs=pl.BlockSpec((count, rows, width), lambda l: (0, 0, 0)),
        scratch_shapes=[pltpu.VMEM((count * rows, width), jnp.float32)],
        compiler_params=params(mebibytes),
        cost_estimate=product_cost(blocks, weight),
        name="project",
    )(*blocks, weight)


def project_place_kernel(meta_ref, *refs):
    *block_refs, weight_ref, zero_ref, sides_ref, keep_ref, send_ref, total_ref, token_ref = refs
    accumulate(
        total_ref, jnp.dot(rows_of(block_refs), weight_ref[0], preferred_element_type=jnp.float32)
    )

    @pl.when(pl.program_id(0) == LEVELS - 1)
    def _():
        core, x, y = meta_ref[0], meta_ref[1], meta_ref[2]
        rows = zero_ref.shape[1]
        total = rows * X * Y
        edge = jnp.zeros((HALO, token_ref.shape[1]), jnp.float32)
        token_ref[pl.ds(0, HALO), :] = edge
        token_ref[pl.ds(HALO + total, HALO), :] = edge
        for second in range(4):
            for first in range(4):
                dx = jnp.where(core == 0, first, second)
                dy = jnp.where(core == 0, second, first)
                e = lax.rem(x + dx, X) * Y + lax.rem(y + dy, Y)
                at = pl.multiple_of(e * rows + HALO, 8)
                if second == 0:
                    block = zero_ref[first].astype(jnp.float32)
                elif second == 2:
                    block = total_ref[pl.ds(first * rows, rows), :]
                else:
                    block = sides_ref[second // 2 * 4 + first].astype(jnp.float32)
                token_ref[pl.ds(at, rows), :] = block
        piece = total // (ZL * CORES)
        for zl in range(ZL):
            for out_ref, whose in ((keep_ref, core), (send_ref, 1 - core)):
                at = pl.multiple_of((zl * CORES + whose) * piece, 8)
                out_ref[zl] = token_ref[pl.ds(at, piece + 2 * HALO), :].astype(jnp.bfloat16)


def project_place(blocks, weight, zero, sides, core, x, y):
    _, rows, width = zero.shape
    count = sum(b.shape[0] for b in blocks)
    total = rows * X * Y
    pieces = (ZL, total // (ZL * CORES) + 2 * HALO, width)
    whole = lambda shape: pl.BlockSpec(shape, lambda l, *_: (0, 0, 0))
    return pl.pallas_call(
        project_place_kernel,
        out_shape=(jax.ShapeDtypeStruct(pieces, jnp.bfloat16),) * 2,
        grid_spec=pltpu.PrefetchScalarGridSpec(
            num_scalar_prefetch=1,
            grid=(LEVELS,),
            in_specs=product_specs(blocks, weight) + [whole(zero.shape), whole(sides.shape)],
            out_specs=(whole(pieces),) * 2,
            scratch_shapes=[
                pltpu.VMEM((count * rows, width), jnp.float32),
                pltpu.VMEM((total + 2 * HALO, width), jnp.float32),
            ],
        ),
        compiler_params=params(18),
        cost_estimate=product_cost(blocks, weight),
        name="project_place",
    )(jnp.stack([core, x, y]), *blocks, weight, zero, sides)


def join_kernel(meta_ref, keep_ref, got_ref, own_ref, *away_refs):
    zl = meta_ref[0]

    def piece(index):
        return keep_ref[index].astype(jnp.float32) + got_ref[index].astype(jnp.float32)

    own_ref[...] = piece(zl).astype(jnp.bfloat16)
    for step, away_ref in zip((1, 2, 3), away_refs):
        away_ref[...] = piece(lax.rem(zl + ZL - step, ZL)).astype(jnp.bfloat16)


def join(keep, got, zl):
    count, rows, width = keep.shape
    whole = pl.BlockSpec(keep.shape, lambda i, m: (0, 0, 0))
    piece = pl.BlockSpec((rows, width), lambda i, m: (0, 0))
    return pl.pallas_call(
        join_kernel,
        out_shape=(jax.ShapeDtypeStruct((rows, width), jnp.bfloat16),) * count,
        grid_spec=pltpu.PrefetchScalarGridSpec(
            num_scalar_prefetch=1, grid=(1,), in_specs=[whole] * 2, out_specs=(piece,) * count
        ),
        compiler_params=params(8),
        cost_estimate=pl.CostEstimate(
            flops=keep.size, bytes_accessed=6 * keep.size, transcendentals=0
        ),
        name="join",
    )(zl.reshape(1), keep, got)


def sigmoid(v):
    return 1.0 / (1.0 + jnp.exp(-v))


def chain_kernel(meta_ref, scale_ref, *refs):
    *part_refs, one_ref, two_ref, left_ref, right_ref, gain_ref, grad_ref = refs
    rows, width = part_refs[0].shape
    own = rows - 2 * HALO
    joined = part_refs[0][...].astype(jnp.float32)
    for part_ref in part_refs[1:]:
        joined = joined + part_ref[...].astype(jnp.float32)
    even = meta_ref[2] == 0
    pick = lambda a, b: jnp.where(even, a[...].astype(jnp.float32), b[...].astype(jnp.float32))
    high = jnp.concatenate(
        [pick(one_ref, two_ref), pick(two_ref, one_ref), pick(left_ref, right_ref)], axis=0
    )
    gain = gain_ref[...]
    scale = scale_ref[0]
    start, length = meta_ref[0], meta_ref[1]
    position = start - HALO + lax.broadcasted_iota(jnp.int32, (rows, width), 0)

    def down(values):
        return jnp.concatenate([jnp.zeros((1, width), jnp.float32), values[:-1]], axis=0)

    def up(values):
        return jnp.concatenate([values[1:], jnp.zeros((1, width), jnp.float32)], axis=0)

    def target(step):
        lead = jnp.zeros((HALO - step, width), jnp.float32)
        return jnp.concatenate([lead, high[: rows - HALO + step]], axis=0)

    def state_and_slope(v):
        gate = sigmoid(v)
        return v * gate, gate * (1.0 + v * (1.0 - gate))

    def residual(state, step):
        return jnp.where(position + step < length, scale * (state - target(step)), 0.0)

    state_1, slope_1 = state_and_slope(joined)
    before_1 = down(state_1)
    state_2, slope_2 = state_and_slope(joined + gain * before_1)
    before_2 = down(state_2)
    state_3, slope_3 = state_and_slope(joined + gain * before_2)
    delta_3 = residual(state_3, 3) * slope_3
    delta_2 = (residual(state_2, 2) + up(gain * delta_3)) * slope_2
    delta_1 = (residual(state_1, 1) + up(gain * delta_2)) * slope_1
    total = delta_1 + delta_2 + delta_3
    mix = (delta_2 * before_1 + delta_3 * before_2)[HALO : HALO + own]
    rest = jnp.sum(mix, axis=0, keepdims=True)
    tail = []
    for _ in range(3):
        term = rest.astype(jnp.bfloat16).astype(jnp.float32)
        tail.append(term)
        rest = rest - term
    tail.append(jnp.zeros((TAIL - 3, width), jnp.float32))
    grad_ref[pl.ds(0, own), :] = total[HALO : HALO + own].astype(jnp.bfloat16)
    grad_ref[pl.ds(own, TAIL), :] = jnp.concatenate(tail, axis=0).astype(jnp.bfloat16)


def chain(parts, halves, gain, start, length, odd, scale):
    rows, width = parts[0].shape
    own = rows - 2 * HALO
    return pl.pallas_call(
        chain_kernel,
        out_shape=jax.ShapeDtypeStruct((own + TAIL, width), jnp.bfloat16),
        in_specs=[SMEM, SMEM] + [VMEM] * (len(parts) + len(halves) + 1),
        out_specs=VMEM,
        compiler_params=params(14),
        cost_estimate=pl.CostEstimate(
            flops=60 * rows * width, bytes_accessed=10 * rows * width, transcendentals=3 * rows * width
        ),
        name="chain",
    )(jnp.stack([start, length, odd]), scale.reshape(1), *parts, *halves, gain.reshape(1, width))


def weight_grad_kernel(meta_ref, features_ref, *refs):
    *group_refs, out_ref, mix_ref, grads_ref = refs
    half = grads_ref.shape[1] // ZH
    width = grads_ref.shape[2]
    mix = jnp.zeros((TAIL, width), jnp.float32)
    for at, group_ref in enumerate(group_refs):
        for part in range(2):
            slab = grads_ref.at[meta_ref[at] * 2 + part]
            for sequence in range(ZH):
                rows = group_ref[sequence, pl.ds(part * half, half), :]
                slab[pl.ds(sequence * half, half), :] = rows
        for sequence in range(ZH):
            mix = mix + group_ref[sequence, pl.ds(2 * half, TAIL), :].astype(jnp.float32)
    mix_ref[...] = jnp.sum(mix, axis=0, keepdims=True)
    blocks = features_ref.shape[0]
    for level in range(LEVELS):
        left = jnp.concatenate([features_ref[e, level] for e in range(blocks)], axis=1)
        right = grads_ref[...].reshape(-1, width)
        term = jnp.dot(left, right, preferred_element_type=jnp.float32)
        out_ref[level] = term.astype(jnp.bfloat16)


def weight_grad(features, groups, members):
    draft, _, columns, tokens = features.shape
    count, width = len(groups), groups[0].shape[2]
    return pl.pallas_call(
        weight_grad_kernel,
        out_shape=(
            jax.ShapeDtypeStruct((LEVELS, columns, width), jnp.bfloat16),
            jax.ShapeDtypeStruct((1, width), jnp.float32),
        ),
        in_specs=[SMEM] + [VMEM] * (count + 1),
        out_specs=(VMEM, VMEM),
        scratch_shapes=[pltpu.VMEM((draft, tokens, width), jnp.bfloat16)],
        compiler_params=params(28),
        cost_estimate=pl.CostEstimate(
            flops=2 * draft * LEVELS * columns * tokens * width,
            bytes_accessed=2 * features.size + 2 * draft * tokens * width,
            transcendentals=0,
        ),
        name="weight_grad",
    )(jnp.stack(members), features, *groups)


def turn_kernel(traded_ref, out_ref):
    rows = traded_ref[:, 0].reshape(-1, traded_ref.shape[3])
    out_ref[0] = rows.astype(jnp.float32).T.astype(jnp.bfloat16)


def turn(traded):
    sequences, levels, rows, columns = traded.shape
    return pl.pallas_call(
        turn_kernel,
        grid=(levels,),
        out_shape=jax.ShapeDtypeStruct((levels, columns, sequences * rows), jnp.bfloat16),
        in_specs=[pl.BlockSpec((sequences, 1, rows, columns), lambda l: (0, l, 0, 0))],
        out_specs=pl.BlockSpec((1, columns, sequences * rows), lambda l: (l, 0, 0)),
        compiler_params=params(8),
        cost_estimate=pl.CostEstimate(flops=0, bytes_accessed=4 * traded.size, transcendentals=0),
        name="turn",
    )(traded)


def valid_total(lengths):
    running = jnp.zeros((), jnp.float32)
    for unroll in range(1, UNROLL + 1):
        running = running + jnp.sum(jnp.maximum(lengths - unroll, 0)).astype(jnp.float32)
    return running


def send_high(top, draft_index):
    members, draft_count = ZL * CORES, X * Y
    width = top.shape[1] // 2
    even = draft_index % 2 == 0
    left, right = top[:, :width], top[:, width:]
    straight, crossed, after_left, after_right = [], [], [], []
    for t in range(members):
        for e in range(draft_count):
            source = t * draft_count + e
            target = e // 2 * draft_count + 2 * t
            straight.append((source, target + e % 2))
            crossed.append((source, target + 1 - e % 2))
            if e % 2 == 0 and e > 0:
                after_left.append((source, target - draft_count))
                after_right.append((source, target - draft_count + 1))
    axes = ("tp", "draft")
    return (
        lax.ppermute(jnp.where(even, left, right), axes, straight),
        lax.ppermute(jnp.where(even, right, left), axes, crossed),
        lax.ppermute(left[:TAIL], axes, after_left),
        lax.ppermute(right[:TAIL], axes, after_right),
    )


def trade_columns(own):
    levels, rows, depth = own.shape
    quarters = own.reshape(levels, rows, ZH, depth // ZH).transpose(2, 0, 1, 3)
    return lax.all_to_all(quarters, "dp", split_axis=0, concat_axis=0, tiled=True)


def gather_grads(grad, features, zl, core):
    stack = lax.all_gather(grad, "dp", axis=0, tiled=False)
    above, below = from_z(stack, 1), from_z(stack, -1)
    far = jnp.concatenate([from_z(stack[:2], 2), from_z(stack[2:], -2)])
    other = from_other_core(stack)
    above, below, other, far, features = lax.optimization_barrier(
        (above, below, other, far, features)
    )
    swapped = [from_other_core(block) for block in (above, below, far)]

    def member(step, of_core):
        return (zl + step) % ZL * CORES + of_core

    groups = [stack, other, above, below, far] + swapped
    members = [member(0, core), member(0, 1 - core)]
    members += [member(step, core) for step in (1, 3, 2)]
    members += [member(step, 1 - core) for step in (1, 3, 2)]
    return weight_grad(features, groups, members)


def local(features, fc_weight, mix_gain, lengths):
    tp_index, zh = lax.axis_index("tp"), lax.axis_index("dp")
    draft_index = lax.axis_index("draft")
    zl, core = tp_index // CORES, tp_index % CORES
    x, y = draft_index // Y, draft_index % Y
    own_rows = features.shape[0]
    piece = own_rows * X * Y // (ZL * CORES)
    own = features.transpose(1, 0, 2)
    weight = fc_weight.transpose(1, 0, 2)

    next_, last, across = (plane_move(step, True)(own) for step in (1, 3, 2))
    halves = send_high(own[LEVELS - 1], draft_index)
    last, across, halves = lax.optimization_barrier((last, across, halves))
    low, high = pair(own, next_), pair(across, last)
    up_low, down_high = plane_move(1, False)(low), plane_move(-1, False)(high)
    up_high, down_low = plane_move(1, False)(high), plane_move(-1, False)(low)
    zero = project([low, high], weight, 14)
    up_low, down_high, zero, later = lax.optimization_barrier((up_low, down_high, zero, own))
    traded = trade_columns(later)
    far_low, far_high = plane_move(1, False)(up_low), plane_move(-1, False)(down_high)
    sides = project([up_low, up_high, down_low, down_high], weight, 58)
    far_low, far_high, sides = lax.optimization_barrier((far_low, far_high, sides))
    keep, send = project_place([far_low, far_high], weight, zero, sides, core, x, y)
    got, traded = lax.optimization_barrier((from_other_core(send), traded))
    every = lax.all_gather(turn(traded), "draft", axis=0, tiled=False)
    mine, *away = join(keep, got, zl)
    parts = [mine] + [from_zl(block, step) for step, block in zip((1, 2, 3), away)]
    scale = LOSS_SCALE / valid_total(lengths)
    odd = draft_index % 2
    grad = chain(parts, halves, mix_gain, tp_index * piece, lengths[zh], odd, scale)
    fc_grad, mix_total = gather_grads(grad, every, zl, core)
    return (fc_grad.transpose(1, 0, 2), mix_total[0])


def solution(mesh):
    placed = (P(("dp", "draft"), None, "tp"), P("tp", None, "draft"), P("draft"), P())
    return jax.shard_map(
        local,
        mesh=mesh,
        in_specs=placed,
        out_specs=(P(("tp", "dp"), None, "draft"), P("draft")),
        check_vma=False,
    )
```

```python
import jax
import jax.numpy as jnp
from jax import lax
from jax.experimental import pallas as pl
from jax.experimental.pallas import tpu as pltpu
from jax.sharding import PartitionSpec as P

LEVELS = 3
UNROLL = 3
LOSS_SCALE = 64.0
HALO = 8
TAIL = 16
X, Y = 4, 4
ZL, CORES, ZH = 4, 2, 4
VMEM = pl.BlockSpec(memory_space=pltpu.VMEM)
SMEM = pl.BlockSpec(memory_space=pltpu.SMEM)


def params(mebibytes):
    return pltpu.CompilerParams(vmem_limit_bytes=mebibytes << 20)


def plane_move(step, first):
    pairs = []
    for t in range(ZL * CORES):
        for x in range(X):
            for y in range(Y):
                along_x = (t % CORES == 0) == first
                source = (x + step) % X * Y + y if along_x else x * Y + (y + step) % Y
                pairs.append((t * X * Y + source, t * X * Y + x * Y + y))
    return lambda block: lax.ppermute(block, ("tp", "draft"), pairs)


def from_other_core(block):
    return lax.ppermute(block, "tp", [(t ^ 1, t) for t in range(ZL * CORES)])


def from_zl(block, step):
    pairs = [((t // CORES + step) % ZL * CORES + t % CORES, t) for t in range(ZL * CORES)]
    return lax.ppermute(block, "tp", pairs)


def from_zh(block, step):
    return lax.ppermute(block, "dp", [((s + step) % ZH, s) for s in range(ZH)])


def from_z(block, step):
    pairs = []
    for t in range(ZL * CORES):
        for s in range(ZH):
            z = (s * ZL + t // CORES + step) % (ZL * ZH)
            pairs.append((((z % ZL) * CORES + t % CORES) * ZH + z // ZL, t * ZH + s))
    return lax.ppermute(block, ("tp", "dp"), pairs)


def pair_kernel(first_ref, second_ref, out_ref):
    out_ref[0] = first_ref[...]
    out_ref[1] = second_ref[...]


def pair(first, second):
    return pl.pallas_call(
        pair_kernel,
        out_shape=jax.ShapeDtypeStruct((2,) + first.shape, first.dtype),
        in_specs=[VMEM] * 2,
        out_specs=VMEM,
        compiler_params=params(4),
        cost_estimate=pl.CostEstimate(flops=0, bytes_accessed=8 * first.size, transcendentals=0),
        name="pair",
    )(first, second)


def rows_of(block_refs):
    return jnp.concatenate([r[...].reshape(-1, r.shape[-1]) for r in block_refs], axis=0)


def accumulate(total_ref, term):
    level = pl.program_id(0)

    @pl.when(level == 0)
    def _():
        total_ref[...] = term

    @pl.when(level > 0)
    def _():
        total_ref[...] += term


def project_kernel(*refs):
    *block_refs, weight_ref, out_ref, total_ref = refs
    accumulate(
        total_ref, jnp.dot(rows_of(block_refs), weight_ref[0], preferred_element_type=jnp.float32)
    )

    @pl.when(pl.program_id(0) == LEVELS - 1)
    def _():
        out_ref[...] = total_ref[...].astype(jnp.bfloat16).reshape(out_ref.shape)


def product_specs(blocks, weight):
    _, _, rows, depth = blocks[0].shape
    specs = [pl.BlockSpec((b.shape[0], 1, rows, depth), lambda l, *_: (0, l, 0, 0)) for b in blocks]
    return specs + [pl.BlockSpec((1, depth, weight.shape[2]), lambda l, *_: (l, 0, 0))]


def product_cost(blocks, weight):
    size = sum(b.size for b in blocks)
    return pl.CostEstimate(flops=0, bytes_accessed=2 * size, transcendentals=0)


def project(blocks, weight, mebibytes):
    rows, width = blocks[0].shape[2], weight.shape[2]
    count = sum(b.shape[0] for b in blocks)
    return pl.pallas_call(
        project_kernel,
        grid=(LEVELS,),
        out_shape=jax.ShapeDtypeStruct((count, rows, width), jnp.bfloat16),
        in_specs=product_specs(blocks, weight),
        out_specs=pl.BlockSpec((count, rows, width), lambda l: (0, 0, 0)),
        scratch_shapes=[pltpu.VMEM((count * rows, width), jnp.float32)],
        compiler_params=params(mebibytes),
        cost_estimate=product_cost(blocks, weight),
        name="project",
    )(*blocks, weight)


def project_place_kernel(meta_ref, *refs):
    *block_refs, weight_ref, zero_ref, sides_ref, keep_ref, send_ref, total_ref, token_ref = refs
    accumulate(
        total_ref, jnp.dot(rows_of(block_refs), weight_ref[0], preferred_element_type=jnp.float32)
    )

    @pl.when(pl.program_id(0) == LEVELS - 1)
    def _():
        core, x, y = meta_ref[0], meta_ref[1], meta_ref[2]
        rows = zero_ref.shape[1]
        total = rows * X * Y
        edge = jnp.zeros((HALO, token_ref.shape[1]), jnp.float32)
        token_ref[pl.ds(0, HALO), :] = edge
        token_ref[pl.ds(HALO + total, HALO), :] = edge
        for second in range(4):
            for first in range(4):
                dx = jnp.where(core == 0, first, second)
                dy = jnp.where(core == 0, second, first)
                e = lax.rem(x + dx, X) * Y + lax.rem(y + dy, Y)
                at = pl.multiple_of(e * rows + HALO, 8)
                if second == 0:
                    block = zero_ref[first].astype(jnp.float32)
                elif second == 2:
                    block = total_ref[pl.ds(first * rows, rows), :]
                else:
                    block = sides_ref[second // 2 * 4 + first].astype(jnp.float32)
                token_ref[pl.ds(at, rows), :] = block
        piece = total // (ZL * CORES)
        for zl in range(ZL):
            for out_ref, whose in ((keep_ref, core), (send_ref, 1 - core)):
                at = pl.multiple_of((zl * CORES + whose) * piece, 8)
                out_ref[zl] = token_ref[pl.ds(at, piece + 2 * HALO), :].astype(jnp.bfloat16)


def project_place(blocks, weight, zero, sides, core, x, y):
    _, rows, width = zero.shape
    count = sum(b.shape[0] for b in blocks)
    total = rows * X * Y
    pieces = (ZL, total // (ZL * CORES) + 2 * HALO, width)
    whole = lambda shape: pl.BlockSpec(shape, lambda l, *_: (0, 0, 0))
    return pl.pallas_call(
        project_place_kernel,
        out_shape=(jax.ShapeDtypeStruct(pieces, jnp.bfloat16),) * 2,
        grid_spec=pltpu.PrefetchScalarGridSpec(
            num_scalar_prefetch=1,
            grid=(LEVELS,),
            in_specs=product_specs(blocks, weight) + [whole(zero.shape), whole(sides.shape)],
            out_specs=(whole(pieces),) * 2,
            scratch_shapes=[
                pltpu.VMEM((count * rows, width), jnp.float32),
                pltpu.VMEM((total + 2 * HALO, width), jnp.float32),
            ],
        ),
        compiler_params=params(18),
        cost_estimate=product_cost(blocks, weight),
        name="project_place",
    )(jnp.stack([core, x, y]), *blocks, weight, zero, sides)


def join_kernel(meta_ref, keep_ref, got_ref, own_ref, *away_refs):
    zl = meta_ref[0]

    def piece(index):
        return keep_ref[index].astype(jnp.float32) + got_ref[index].astype(jnp.float32)

    own_ref[...] = piece(zl).astype(jnp.bfloat16)
    for step, away_ref in zip((1, 2, 3), away_refs):
        away_ref[...] = piece(lax.rem(zl + ZL - step, ZL)).astype(jnp.bfloat16)


def join(keep, got, zl):
    count, rows, width = keep.shape
    whole = pl.BlockSpec(keep.shape, lambda i, m: (0, 0, 0))
    piece = pl.BlockSpec((rows, width), lambda i, m: (0, 0))
    return pl.pallas_call(
        join_kernel,
        out_shape=(jax.ShapeDtypeStruct((rows, width), jnp.bfloat16),) * count,
        grid_spec=pltpu.PrefetchScalarGridSpec(
            num_scalar_prefetch=1, grid=(1,), in_specs=[whole] * 2, out_specs=(piece,) * count
        ),
        compiler_params=params(8),
        cost_estimate=pl.CostEstimate(
            flops=keep.size, bytes_accessed=6 * keep.size, transcendentals=0
        ),
        name="join",
    )(zl.reshape(1), keep, got)


def sigmoid(v):
    return 1.0 / (1.0 + jnp.exp(-v))


def chain_kernel(meta_ref, scale_ref, *refs):
    *part_refs, one_ref, two_ref, left_ref, right_ref, gain_ref, grad_ref = refs
    rows, width = part_refs[0].shape
    own = rows - 2 * HALO
    joined = part_refs[0][...].astype(jnp.float32)
    for part_ref in part_refs[1:]:
        joined = joined + part_ref[...].astype(jnp.float32)
    even = meta_ref[2] == 0
    pick = lambda a, b: jnp.where(even, a[...].astype(jnp.float32), b[...].astype(jnp.float32))
    high = jnp.concatenate(
        [pick(one_ref, two_ref), pick(two_ref, one_ref), pick(left_ref, right_ref)], axis=0
    )
    gain = gain_ref[...]
    scale = scale_ref[0]
    start, length = meta_ref[0], meta_ref[1]
    position = start - HALO + lax.broadcasted_iota(jnp.int32, (rows, width), 0)

    def down(values):
        return jnp.concatenate([jnp.zeros((1, width), jnp.float32), values[:-1]], axis=0)

    def up(values):
        return jnp.concatenate([values[1:], jnp.zeros((1, width), jnp.float32)], axis=0)

    def target(step):
        lead = jnp.zeros((HALO - step, width), jnp.float32)
        return jnp.concatenate([lead, high[: rows - HALO + step]], axis=0)

    def state_and_slope(v):
        gate = sigmoid(v)
        return v * gate, gate * (1.0 + v * (1.0 - gate))

    def residual(state, step):
        return jnp.where(position + step < length, scale * (state - target(step)), 0.0)

    state_1, slope_1 = state_and_slope(joined)
    before_1 = down(state_1)
    state_2, slope_2 = state_and_slope(joined + gain * before_1)
    before_2 = down(state_2)
    state_3, slope_3 = state_and_slope(joined + gain * before_2)
    delta_3 = residual(state_3, 3) * slope_3
    delta_2 = (residual(state_2, 2) + up(gain * delta_3)) * slope_2
    delta_1 = (residual(state_1, 1) + up(gain * delta_2)) * slope_1
    total = delta_1 + delta_2 + delta_3
    mix = (delta_2 * before_1 + delta_3 * before_2)[HALO : HALO + own]
    rest = jnp.sum(mix, axis=0, keepdims=True)
    tail = []
    for _ in range(3):
        term = rest.astype(jnp.bfloat16).astype(jnp.float32)
        tail.append(term)
        rest = rest - term
    tail.append(jnp.zeros((TAIL - 3, width), jnp.float32))
    grad_ref[pl.ds(0, own), :] = total[HALO : HALO + own].astype(jnp.bfloat16)
    grad_ref[pl.ds(own, TAIL), :] = jnp.concatenate(tail, axis=0).astype(jnp.bfloat16)


def chain(parts, halves, gain, start, length, odd, scale):
    rows, width = parts[0].shape
    own = rows - 2 * HALO
    return pl.pallas_call(
        chain_kernel,
        out_shape=jax.ShapeDtypeStruct((own + TAIL, width), jnp.bfloat16),
        in_specs=[SMEM, SMEM] + [VMEM] * (len(parts) + len(halves) + 1),
        out_specs=VMEM,
        compiler_params=params(14),
        cost_estimate=pl.CostEstimate(
            flops=60 * rows * width, bytes_accessed=10 * rows * width, transcendentals=3 * rows * width
        ),
        name="chain",
    )(jnp.stack([start, length, odd]), scale.reshape(1), *parts, *halves, gain.reshape(1, width))


def weight_grad_kernel(meta_ref, features_ref, *refs):
    *group_refs, out_ref, mix_ref, grads_ref = refs
    half = grads_ref.shape[1] // ZH
    width = grads_ref.shape[2]
    mix = jnp.zeros((TAIL, width), jnp.float32)
    for at, group_ref in enumerate(group_refs):
        for part in range(2):
            slab = grads_ref.at[meta_ref[at] * 2 + part]
            for sequence in range(ZH):
                rows = group_ref[sequence, pl.ds(part * half, half), :]
                slab[pl.ds(sequence * half, half), :] = rows
        for sequence in range(ZH):
            mix = mix + group_ref[sequence, pl.ds(2 * half, TAIL), :].astype(jnp.float32)
    mix_ref[...] = jnp.sum(mix, axis=0, keepdims=True)
    blocks = features_ref.shape[0]
    for level in range(LEVELS):
        left = jnp.concatenate([features_ref[e, level] for e in range(blocks)], axis=1)
        right = grads_ref[...].reshape(-1, width)
        term = jnp.dot(left, right, preferred_element_type=jnp.float32)
        out_ref[level] = term.astype(jnp.bfloat16)


def weight_grad(features, groups, members):
    draft, _, columns, tokens = features.shape
    count, width = len(groups), groups[0].shape[2]
    return pl.pallas_call(
        weight_grad_kernel,
        out_shape=(
            jax.ShapeDtypeStruct((LEVELS, columns, width), jnp.bfloat16),
            jax.ShapeDtypeStruct((1, width), jnp.float32),
        ),
        in_specs=[SMEM] + [VMEM] * (count + 1),
        out_specs=(VMEM, VMEM),
        scratch_shapes=[pltpu.VMEM((draft, tokens, width), jnp.bfloat16)],
        compiler_params=params(28),
        cost_estimate=pl.CostEstimate(
            flops=2 * draft * LEVELS * columns * tokens * width,
            bytes_accessed=2 * features.size + 2 * draft * tokens * width,
            transcendentals=0,
        ),
        name="weight_grad",
    )(jnp.stack(members), features, *groups)


def turn_kernel(traded_ref, out_ref):
    rows = traded_ref[:, 0].reshape(-1, traded_ref.shape[3])
    out_ref[0] = rows.astype(jnp.float32).T.astype(jnp.bfloat16)


def turn(traded):
    sequences, levels, rows, columns = traded.shape
    return pl.pallas_call(
        turn_kernel,
        grid=(levels,),
        out_shape=jax.ShapeDtypeStruct((levels, columns, sequences * rows), jnp.bfloat16),
        in_specs=[pl.BlockSpec((sequences, 1, rows, columns), lambda l: (0, l, 0, 0))],
        out_specs=pl.BlockSpec((1, columns, sequences * rows), lambda l: (l, 0, 0)),
        compiler_params=params(8),
        cost_estimate=pl.CostEstimate(flops=0, bytes_accessed=4 * traded.size, transcendentals=0),
        name="turn",
    )(traded)


def valid_total(lengths):
    running = jnp.zeros((), jnp.float32)
    for unroll in range(1, UNROLL + 1):
        running = running + jnp.sum(jnp.maximum(lengths - unroll, 0)).astype(jnp.float32)
    return running


def send_high(top, draft_index):
    members, draft_count = ZL * CORES, X * Y
    width = top.shape[1] // 2
    even = draft_index % 2 == 0
    left, right = top[:, :width], top[:, width:]
    straight, crossed, after_left, after_right = [], [], [], []
    for t in range(members):
        for e in range(draft_count):
            source = t * draft_count + e
            target = e // 2 * draft_count + 2 * t
            straight.append((source, target + e % 2))
            crossed.append((source, target + 1 - e % 2))
            if e % 2 == 0 and e > 0:
                after_left.append((source, target - draft_count))
                after_right.append((source, target - draft_count + 1))
    axes = ("tp", "draft")
    return (
        lax.ppermute(jnp.where(even, left, right), axes, straight),
        lax.ppermute(jnp.where(even, right, left), axes, crossed),
        lax.ppermute(left[:TAIL], axes, after_left),
        lax.ppermute(right[:TAIL], axes, after_right),
    )


def trade_columns(own):
    levels, rows, depth = own.shape
    quarters = own.reshape(levels, rows, ZH, depth // ZH).transpose(2, 0, 1, 3)
    return lax.all_to_all(quarters, "dp", split_axis=0, concat_axis=0, tiled=True)


def gather_grads(grad, features, zl, core):
    stack = lax.all_gather(grad, "dp", axis=0, tiled=False)
    above, below = from_z(stack, 1), from_z(stack, -1)
    far = jnp.concatenate([from_z(stack[:2], 2), from_z(stack[2:], -2)])
    other = from_other_core(stack)
    above, below, other, far, features = lax.optimization_barrier(
        (above, below, other, far, features)
    )
    swapped = [from_other_core(block) for block in (above, below, far)]

    def member(step, of_core):
        return (zl + step) % ZL * CORES + of_core

    groups = [stack, other, above, below, far] + swapped
    members = [member(0, core), member(0, 1 - core)]
    members += [member(step, core) for step in (1, 3, 2)]
    members += [member(step, 1 - core) for step in (1, 3, 2)]
    return weight_grad(features, groups, members)


def local(features, fc_weight, mix_gain, lengths):
    tp_index, zh = lax.axis_index("tp"), lax.axis_index("dp")
    draft_index = lax.axis_index("draft")
    zl, core = tp_index // CORES, tp_index % CORES
    x, y = draft_index // Y, draft_index % Y
    own_rows = features.shape[0]
    piece = own_rows * X * Y // (ZL * CORES)
    own = features.transpose(1, 0, 2)
    weight = fc_weight.transpose(1, 0, 2)

    next_, last, across = (plane_move(step, True)(own) for step in (1, 3, 2))
    low, high = pair(own, next_), pair(across, last)
    up_low, down_high = plane_move(1, False)(low), plane_move(-1, False)(high)
    up_high, down_low = plane_move(1, False)(high), plane_move(-1, False)(low)
    zero = project([low, high], weight, 14)
    up_low, down_high, zero, later = lax.optimization_barrier((up_low, down_high, zero, own))
    traded = trade_columns(later)
    far_low, far_high = plane_move(1, False)(up_low), plane_move(-1, False)(down_high)
    sides = project([up_low, up_high, down_low, down_high], weight, 58)
    far_low, far_high, sides = lax.optimization_barrier((far_low, far_high, sides))
    keep, send = project_place([far_low, far_high], weight, zero, sides, core, x, y)
    mine, *away = join(keep, from_other_core(send), zl)
    top, mine, traded = lax.optimization_barrier((own[LEVELS - 1], mine, traded))
    halves = send_high(top, draft_index)
    every = lax.all_gather(turn(traded), "draft", axis=0, tiled=False)
    parts = [mine] + [from_zl(block, step) for step, block in zip((1, 2, 3), away)]
    scale = LOSS_SCALE / valid_total(lengths)
    odd = draft_index % 2
    grad = chain(parts, halves, mix_gain, tp_index * piece, lengths[zh], odd, scale)
    fc_grad, mix_total = gather_grads(grad, every, zl, core)
    return (fc_grad.transpose(1, 0, 2), mix_total[0])


def solution(mesh):
    placed = (P(("dp", "draft"), None, "tp"), P("tp", None, "draft"), P("draft"), P())
    return jax.shard_map(
        local,
        mesh=mesh,
        in_specs=placed,
        out_specs=(P(("tp", "dp"), None, "draft"), P("draft")),
        check_vma=False,
    )
```

```python
import jax
import jax.numpy as jnp
from jax import lax
from jax.experimental import pallas as pl
from jax.experimental.pallas import tpu as pltpu
from jax.sharding import PartitionSpec as P

LEVELS = 3
UNROLL = 3
LOSS_SCALE = 64.0
HALO = 8
TAIL = 16
X, Y = 4, 4
ZL, CORES, ZH = 4, 2, 4
VMEM = pl.BlockSpec(memory_space=pltpu.VMEM)
SMEM = pl.BlockSpec(memory_space=pltpu.SMEM)


def params(mebibytes):
    return pltpu.CompilerParams(vmem_limit_bytes=mebibytes << 20)


def plane_move(step, first):
    pairs = []
    for t in range(ZL * CORES):
        for x in range(X):
            for y in range(Y):
                along_x = (t % CORES == 0) == first
                source = (x + step) % X * Y + y if along_x else x * Y + (y + step) % Y
                pairs.append((t * X * Y + source, t * X * Y + x * Y + y))
    return lambda block: lax.ppermute(block, ("tp", "draft"), pairs)


def from_other_core(block):
    return lax.ppermute(block, "tp", [(t ^ 1, t) for t in range(ZL * CORES)])


def from_zl(block, step):
    pairs = [((t // CORES + step) % ZL * CORES + t % CORES, t) for t in range(ZL * CORES)]
    return lax.ppermute(block, "tp", pairs)


def from_zh(block, step):
    return lax.ppermute(block, "dp", [((s + step) % ZH, s) for s in range(ZH)])


def from_z(block, step):
    pairs = []
    for t in range(ZL * CORES):
        for s in range(ZH):
            z = (s * ZL + t // CORES + step) % (ZL * ZH)
            pairs.append((((z % ZL) * CORES + t % CORES) * ZH + z // ZL, t * ZH + s))
    return lax.ppermute(block, ("tp", "dp"), pairs)


def pair_kernel(first_ref, second_ref, out_ref):
    out_ref[0] = first_ref[...]
    out_ref[1] = second_ref[...]


def pair(first, second):
    return pl.pallas_call(
        pair_kernel,
        out_shape=jax.ShapeDtypeStruct((2,) + first.shape, first.dtype),
        in_specs=[VMEM] * 2,
        out_specs=VMEM,
        compiler_params=params(4),
        cost_estimate=pl.CostEstimate(flops=0, bytes_accessed=8 * first.size, transcendentals=0),
        name="pair",
    )(first, second)


def rows_of(block_refs):
    return jnp.concatenate([r[...].reshape(-1, r.shape[-1]) for r in block_refs], axis=0)


def accumulate(total_ref, term):
    level = pl.program_id(0)

    @pl.when(level == 0)
    def _():
        total_ref[...] = term

    @pl.when(level > 0)
    def _():
        total_ref[...] += term


def project_kernel(*refs):
    *block_refs, weight_ref, out_ref, total_ref = refs
    accumulate(
        total_ref, jnp.dot(rows_of(block_refs), weight_ref[0], preferred_element_type=jnp.float32)
    )

    @pl.when(pl.program_id(0) == LEVELS - 1)
    def _():
        out_ref[...] = total_ref[...].astype(jnp.bfloat16).reshape(out_ref.shape)


def product_specs(blocks, weight):
    _, _, rows, depth = blocks[0].shape
    specs = [pl.BlockSpec((b.shape[0], 1, rows, depth), lambda l, *_: (0, l, 0, 0)) for b in blocks]
    return specs + [pl.BlockSpec((1, depth, weight.shape[2]), lambda l, *_: (l, 0, 0))]


def product_cost(blocks, weight):
    size = sum(b.size for b in blocks)
    return pl.CostEstimate(flops=0, bytes_accessed=2 * size, transcendentals=0)


def project(blocks, weight, mebibytes):
    rows, width = blocks[0].shape[2], weight.shape[2]
    count = sum(b.shape[0] for b in blocks)
    return pl.pallas_call(
        project_kernel,
        grid=(LEVELS,),
        out_shape=jax.ShapeDtypeStruct((count, rows, width), jnp.bfloat16),
        in_specs=product_specs(blocks, weight),
        out_specs=pl.BlockSpec((count, rows, width), lambda l: (0, 0, 0)),
        scratch_shapes=[pltpu.VMEM((count * rows, width), jnp.float32)],
        compiler_params=params(mebibytes),
        cost_estimate=product_cost(blocks, weight),
        name="project",
    )(*blocks, weight)


def project_place_kernel(meta_ref, *refs):
    *block_refs, weight_ref, near_ref, keep_ref, send_ref, total_ref, token_ref = refs
    accumulate(
        total_ref, jnp.dot(rows_of(block_refs), weight_ref[0], preferred_element_type=jnp.float32)
    )

    @pl.when(pl.program_id(0) == LEVELS - 1)
    def _():
        core, x, y = meta_ref[0], meta_ref[1], meta_ref[2]
        rows = near_ref.shape[1]
        total = rows * X * Y
        edge = jnp.zeros((HALO, token_ref.shape[1]), jnp.float32)
        token_ref[pl.ds(0, HALO), :] = edge
        token_ref[pl.ds(HALO + total, HALO), :] = edge
        for second in range(4):
            for first in range(4):
                dx = jnp.where(core == 0, first, second)
                dy = jnp.where(core == 0, second, first)
                e = lax.rem(x + dx, X) * Y + lax.rem(y + dy, Y)
                at = pl.multiple_of(e * rows + HALO, 8)
                if second == 2:
                    block = total_ref[pl.ds(first * rows, rows), :]
                else:
                    block = near_ref[(0, 4, 0, 8)[second] + first].astype(jnp.float32)
                token_ref[pl.ds(at, rows), :] = block
        piece = total // (ZL * CORES)
        for zl in range(ZL):
            for out_ref, whose in ((keep_ref, core), (send_ref, 1 - core)):
                at = pl.multiple_of((zl * CORES + whose) * piece, 8)
                out_ref[zl] = token_ref[pl.ds(at, piece + 2 * HALO), :].astype(jnp.bfloat16)


def project_place(blocks, weight, near, core, x, y):
    _, rows, width = near.shape
    count = sum(b.shape[0] for b in blocks)
    total = rows * X * Y
    pieces = (ZL, total // (ZL * CORES) + 2 * HALO, width)
    whole = lambda shape: pl.BlockSpec(shape, lambda l, *_: (0, 0, 0))
    return pl.pallas_call(
        project_place_kernel,
        out_shape=(jax.ShapeDtypeStruct(pieces, jnp.bfloat16),) * 2,
        grid_spec=pltpu.PrefetchScalarGridSpec(
            num_scalar_prefetch=1,
            grid=(LEVELS,),
            in_specs=product_specs(blocks, weight) + [whole(near.shape)],
            out_specs=(whole(pieces),) * 2,
            scratch_shapes=[
                pltpu.VMEM((count * rows, width), jnp.float32),
                pltpu.VMEM((total + 2 * HALO, width), jnp.float32),
            ],
        ),
        compiler_params=params(18),
        cost_estimate=product_cost(blocks, weight),
        name="project_place",
    )(jnp.stack([core, x, y]), *blocks, weight, near)


def join_kernel(meta_ref, keep_ref, got_ref, own_ref, *away_refs):
    zl = meta_ref[0]

    def piece(index):
        return keep_ref[index].astype(jnp.float32) + got_ref[index].astype(jnp.float32)

    own_ref[...] = piece(zl).astype(jnp.bfloat16)
    for step, away_ref in zip((1, 2, 3), away_refs):
        away_ref[...] = piece(lax.rem(zl + ZL - step, ZL)).astype(jnp.bfloat16)


def join(keep, got, zl):
    count, rows, width = keep.shape
    whole = pl.BlockSpec(keep.shape, lambda i, m: (0, 0, 0))
    piece = pl.BlockSpec((rows, width), lambda i, m: (0, 0))
    return pl.pallas_call(
        join_kernel,
        out_shape=(jax.ShapeDtypeStruct((rows, width), jnp.bfloat16),) * count,
        grid_spec=pltpu.PrefetchScalarGridSpec(
            num_scalar_prefetch=1, grid=(1,), in_specs=[whole] * 2, out_specs=(piece,) * count
        ),
        compiler_params=params(8),
        cost_estimate=pl.CostEstimate(
            flops=keep.size, bytes_accessed=6 * keep.size, transcendentals=0
        ),
        name="join",
    )(zl.reshape(1), keep, got)


def sigmoid(v):
    return 1.0 / (1.0 + jnp.exp(-v))


def chain_kernel(meta_ref, scale_ref, *refs):
    *part_refs, one_ref, two_ref, left_ref, right_ref, gain_ref, grad_ref = refs
    rows, width = part_refs[0].shape
    own = rows - 2 * HALO
    joined = part_refs[0][...].astype(jnp.float32)
    for part_ref in part_refs[1:]:
        joined = joined + part_ref[...].astype(jnp.float32)
    even = meta_ref[2] == 0
    pick = lambda a, b: jnp.where(even, a[...].astype(jnp.float32), b[...].astype(jnp.float32))
    high = jnp.concatenate(
        [pick(one_ref, two_ref), pick(two_ref, one_ref), pick(left_ref, right_ref)], axis=0
    )
    gain = gain_ref[...]
    scale = scale_ref[0]
    start, length = meta_ref[0], meta_ref[1]
    position = start - HALO + lax.broadcasted_iota(jnp.int32, (rows, width), 0)

    def down(values):
        return jnp.concatenate([jnp.zeros((1, width), jnp.float32), values[:-1]], axis=0)

    def up(values):
        return jnp.concatenate([values[1:], jnp.zeros((1, width), jnp.float32)], axis=0)

    def target(step):
        lead = jnp.zeros((HALO - step, width), jnp.float32)
        return jnp.concatenate([lead, high[: rows - HALO + step]], axis=0)

    def state_and_slope(v):
        gate = sigmoid(v)
        return v * gate, gate * (1.0 + v * (1.0 - gate))

    def residual(state, step):
        return jnp.where(position + step < length, scale * (state - target(step)), 0.0)

    state_1, slope_1 = state_and_slope(joined)
    before_1 = down(state_1)
    state_2, slope_2 = state_and_slope(joined + gain * before_1)
    before_2 = down(state_2)
    state_3, slope_3 = state_and_slope(joined + gain * before_2)
    delta_3 = residual(state_3, 3) * slope_3
    delta_2 = (residual(state_2, 2) + up(gain * delta_3)) * slope_2
    delta_1 = (residual(state_1, 1) + up(gain * delta_2)) * slope_1
    total = delta_1 + delta_2 + delta_3
    mix = (delta_2 * before_1 + delta_3 * before_2)[HALO : HALO + own]
    rest = jnp.sum(mix, axis=0, keepdims=True)
    tail = []
    for _ in range(3):
        term = rest.astype(jnp.bfloat16).astype(jnp.float32)
        tail.append(term)
        rest = rest - term
    tail.append(jnp.zeros((TAIL - 3, width), jnp.float32))
    grad_ref[pl.ds(0, own), :] = total[HALO : HALO + own].astype(jnp.bfloat16)
    grad_ref[pl.ds(own, TAIL), :] = jnp.concatenate(tail, axis=0).astype(jnp.bfloat16)


def chain(parts, halves, gain, start, length, odd, scale):
    rows, width = parts[0].shape
    own = rows - 2 * HALO
    return pl.pallas_call(
        chain_kernel,
        out_shape=jax.ShapeDtypeStruct((own + TAIL, width), jnp.bfloat16),
        in_specs=[SMEM, SMEM] + [VMEM] * (len(parts) + len(halves) + 1),
        out_specs=VMEM,
        compiler_params=params(14),
        cost_estimate=pl.CostEstimate(
            flops=60 * rows * width, bytes_accessed=10 * rows * width, transcendentals=3 * rows * width
        ),
        name="chain",
    )(jnp.stack([start, length, odd]), scale.reshape(1), *parts, *halves, gain.reshape(1, width))


def weight_grad_kernel(meta_ref, features_ref, *refs):
    *group_refs, out_ref, mix_ref, grads_ref, held_ref, sem = refs
    half = grads_ref.shape[1] // ZH
    width = grads_ref.shape[2]
    held = [
        pltpu.make_async_copy(features_ref.at[:, at], held_ref.at[at], sem.at[at])
        for at in range(LEVELS)
    ]
    for copy in held:
        copy.start()
    mix = jnp.zeros((TAIL, width), jnp.float32)
    for at, group_ref in enumerate(group_refs):
        for part in range(2):
            slab = grads_ref.at[meta_ref[at] * 2 + part]
            for sequence in range(ZH):
                rows = group_ref[sequence, pl.ds(part * half, half), :]
                slab[pl.ds(sequence * half, half), :] = rows
        for sequence in range(ZH):
            mix = mix + group_ref[sequence, pl.ds(2 * half, TAIL), :].astype(jnp.float32)
    mix_ref[...] = jnp.sum(mix, axis=0, keepdims=True)
    blocks = held_ref.shape[1]
    for level, copy in enumerate(held):
        copy.wait()
        left = jnp.concatenate([held_ref[level, e] for e in range(blocks)], axis=1)
        right = grads_ref[...].reshape(-1, width)
        term = jnp.dot(left, right, preferred_element_type=jnp.float32)
        out_ref[level] = term.astype(jnp.bfloat16)


def weight_grad(features, groups, members):
    draft, _, columns, tokens = features.shape
    count, width = len(groups), groups[0].shape[2]
    return pl.pallas_call(
        weight_grad_kernel,
        out_shape=(
            jax.ShapeDtypeStruct((LEVELS, columns, width), jnp.bfloat16),
            jax.ShapeDtypeStruct((1, width), jnp.float32),
        ),
        in_specs=[SMEM, pl.BlockSpec(memory_space=pltpu.HBM)] + [VMEM] * count,
        out_specs=(VMEM, VMEM),
        scratch_shapes=[
            pltpu.VMEM((draft, tokens, width), jnp.bfloat16),
            pltpu.VMEM((LEVELS, draft, columns, tokens), jnp.bfloat16),
            pltpu.SemaphoreType.DMA((LEVELS,)),
        ],
        compiler_params=params(46),
        cost_estimate=pl.CostEstimate(
            flops=2 * draft * LEVELS * columns * tokens * width,
            bytes_accessed=2 * features.size + 2 * draft * tokens * width,
            transcendentals=0,
        ),
        name="weight_grad",
    )(jnp.stack(members), features, *groups)


def turn_kernel(traded_ref, out_ref):
    rows = traded_ref[:, 0].reshape(-1, traded_ref.shape[3])
    out_ref[0] = rows.astype(jnp.float32).T.astype(jnp.bfloat16)


def turn(traded):
    sequences, levels, rows, columns = traded.shape
    return pl.pallas_call(
        turn_kernel,
        grid=(levels,),
        out_shape=jax.ShapeDtypeStruct((levels, columns, sequences * rows), jnp.bfloat16),
        in_specs=[pl.BlockSpec((sequences, 1, rows, columns), lambda l: (0, l, 0, 0))],
        out_specs=pl.BlockSpec((1, columns, sequences * rows), lambda l: (l, 0, 0)),
        compiler_params=params(8),
        cost_estimate=pl.CostEstimate(flops=0, bytes_accessed=4 * traded.size, transcendentals=0),
        name="turn",
    )(traded)


def valid_total(lengths):
    running = jnp.zeros((), jnp.float32)
    for unroll in range(1, UNROLL + 1):
        running = running + jnp.sum(jnp.maximum(lengths - unroll, 0)).astype(jnp.float32)
    return running


def send_high(top, draft_index):
    members, draft_count = ZL * CORES, X * Y
    width = top.shape[1] // 2
    even = draft_index % 2 == 0
    left, right = top[:, :width], top[:, width:]
    straight, crossed, after_left, after_right = [], [], [], []
    for t in range(members):
        for e in range(draft_count):
            source = t * draft_count + e
            target = e // 2 * draft_count + 2 * t
            straight.append((source, target + e % 2))
            crossed.append((source, target + 1 - e % 2))
            if e % 2 == 0 and e > 0:
                after_left.append((source, target - draft_count))
                after_right.append((source, target - draft_count + 1))
    axes = ("tp", "draft")
    return (
        lax.ppermute(jnp.where(even, left, right), axes, straight),
        lax.ppermute(jnp.where(even, right, left), axes, crossed),
        lax.ppermute(left[:TAIL], axes, after_left),
        lax.ppermute(right[:TAIL], axes, after_right),
    )


def trade_columns(own):
    levels, rows, depth = own.shape
    quarters = own.reshape(levels, rows, ZH, depth // ZH).transpose(2, 0, 1, 3)
    return lax.all_to_all(quarters, "dp", split_axis=0, concat_axis=0, tiled=True)


def gather_grads(grad, features, zl, core):
    stack = lax.all_gather(grad, "dp", axis=0, tiled=False)
    above, below = from_z(stack, 1), from_z(stack, -1)
    far = jnp.concatenate([from_z(stack[:2], 2), from_z(stack[2:], -2)])
    other = from_other_core(stack)
    above, below, other, far, features = lax.optimization_barrier(
        (above, below, other, far, features)
    )
    swapped = [from_other_core(block) for block in (above, below, far)]

    def member(step, of_core):
        return (zl + step) % ZL * CORES + of_core

    groups = [stack, other, above, below, far] + swapped
    members = [member(0, core), member(0, 1 - core)]
    members += [member(step, core) for step in (1, 3, 2)]
    members += [member(step, 1 - core) for step in (1, 3, 2)]
    return weight_grad(features, groups, members)


def local(features, fc_weight, mix_gain, lengths):
    tp_index, zh = lax.axis_index("tp"), lax.axis_index("dp")
    draft_index = lax.axis_index("draft")
    zl, core = tp_index // CORES, tp_index % CORES
    x, y = draft_index // Y, draft_index % Y
    own_rows = features.shape[0]
    piece = own_rows * X * Y // (ZL * CORES)
    own = features.transpose(1, 0, 2)
    weight = fc_weight.transpose(1, 0, 2)

    next_, last, across = (plane_move(step, True)(own) for step in (1, 3, 2))
    low, high = pair(own, next_), pair(across, last)
    up_low, down_high = plane_move(1, False)(low), plane_move(-1, False)(high)
    up_high, down_low = plane_move(1, False)(high), plane_move(-1, False)(low)
    up_low, down_high, later = lax.optimization_barrier((up_low, down_high, own))
    traded = trade_columns(later)
    far_low, far_high = plane_move(1, False)(up_low), plane_move(-1, False)(down_high)
    near = project([low, high, up_low, up_high, down_low, down_high], weight, 58)
    far_low, far_high, near = lax.optimization_barrier((far_low, far_high, near))
    keep, send = project_place([far_low, far_high], weight, near, core, x, y)
    mine, *away = join(keep, from_other_core(send), zl)
    top, mine, traded = lax.optimization_barrier((own[LEVELS - 1], mine, traded))
    halves = send_high(top, draft_index)
    every = lax.all_gather(turn(traded), "draft", axis=0, tiled=False)
    parts = [mine] + [from_zl(block, step) for step, block in zip((1, 2, 3), away)]
    scale = LOSS_SCALE / valid_total(lengths)
    odd = draft_index % 2
    grad = chain(parts, halves, mix_gain, tp_index * piece, lengths[zh], odd, scale)
    fc_grad, mix_total = gather_grads(grad, every, zl, core)
    return (fc_grad.transpose(1, 0, 2), mix_total[0])


def solution(mesh):
    placed = (P(("dp", "draft"), None, "tp"), P("tp", None, "draft"), P("draft"), P())
    return jax.shard_map(
        local,
        mesh=mesh,
        in_specs=placed,
        out_specs=(P(("tp", "dp"), None, "draft"), P("draft")),
        check_vma=False,
    )
```

```python
import jax
import jax.numpy as jnp
from jax import lax
from jax.experimental import pallas as pl
from jax.experimental.pallas import tpu as pltpu
from jax.sharding import PartitionSpec as P

LEVELS = 3
UNROLL = 3
LOSS_SCALE = 64.0
HALO = 8
TAIL = 16
X, Y = 4, 4
ZL, CORES, ZH = 4, 2, 4
VMEM = pl.BlockSpec(memory_space=pltpu.VMEM)
SMEM = pl.BlockSpec(memory_space=pltpu.SMEM)


def params(mebibytes):
    return pltpu.CompilerParams(vmem_limit_bytes=mebibytes << 20)


def plane_move(step, first):
    pairs = []
    for t in range(ZL * CORES):
        for x in range(X):
            for y in range(Y):
                along_x = (t % CORES == 0) == first
                source = (x + step) % X * Y + y if along_x else x * Y + (y + step) % Y
                pairs.append((t * X * Y + source, t * X * Y + x * Y + y))
    return lambda block: lax.ppermute(block, ("tp", "draft"), pairs)


def from_other_core(block):
    return lax.ppermute(block, "tp", [(t ^ 1, t) for t in range(ZL * CORES)])


def from_zl(block, step):
    pairs = [((t // CORES + step) % ZL * CORES + t % CORES, t) for t in range(ZL * CORES)]
    return lax.ppermute(block, "tp", pairs)


def from_zh(block, step):
    return lax.ppermute(block, "dp", [((s + step) % ZH, s) for s in range(ZH)])


def from_z(block, step):
    pairs = []
    for t in range(ZL * CORES):
        for s in range(ZH):
            z = (s * ZL + t // CORES + step) % (ZL * ZH)
            pairs.append((((z % ZL) * CORES + t % CORES) * ZH + z // ZL, t * ZH + s))
    return lax.ppermute(block, ("tp", "dp"), pairs)


def pair_kernel(first_ref, second_ref, out_ref):
    out_ref[0] = first_ref[...]
    out_ref[1] = second_ref[...]


def pair(first, second):
    return pl.pallas_call(
        pair_kernel,
        out_shape=jax.ShapeDtypeStruct((2,) + first.shape, first.dtype),
        in_specs=[VMEM] * 2,
        out_specs=VMEM,
        compiler_params=params(4),
        cost_estimate=pl.CostEstimate(flops=0, bytes_accessed=8 * first.size, transcendentals=0),
        name="pair",
    )(first, second)


def rows_of(block_refs):
    return jnp.concatenate([r[...].reshape(-1, r.shape[-1]) for r in block_refs], axis=0)


def accumulate(total_ref, term):
    level = pl.program_id(0)

    @pl.when(level == 0)
    def _():
        total_ref[...] = term

    @pl.when(level > 0)
    def _():
        total_ref[...] += term


def project_kernel(*refs):
    *block_refs, weight_ref, out_ref, total_ref = refs
    accumulate(
        total_ref, jnp.dot(rows_of(block_refs), weight_ref[0], preferred_element_type=jnp.float32)
    )

    @pl.when(pl.program_id(0) == LEVELS - 1)
    def _():
        out_ref[...] = total_ref[...].astype(jnp.bfloat16).reshape(out_ref.shape)


def product_specs(blocks, weight):
    _, _, rows, depth = blocks[0].shape
    specs = [pl.BlockSpec((b.shape[0], 1, rows, depth), lambda l, *_: (0, l, 0, 0)) for b in blocks]
    return specs + [pl.BlockSpec((1, depth, weight.shape[2]), lambda l, *_: (l, 0, 0))]


def product_cost(blocks, weight):
    size = sum(b.size for b in blocks)
    return pl.CostEstimate(flops=0, bytes_accessed=2 * size, transcendentals=0)


def project(blocks, weight, mebibytes):
    rows, width = blocks[0].shape[2], weight.shape[2]
    count = sum(b.shape[0] for b in blocks)
    return pl.pallas_call(
        project_kernel,
        grid=(LEVELS,),
        out_shape=jax.ShapeDtypeStruct((count, rows, width), jnp.bfloat16),
        in_specs=product_specs(blocks, weight),
        out_specs=pl.BlockSpec((count, rows, width), lambda l: (0, 0, 0)),
        scratch_shapes=[pltpu.VMEM((count * rows, width), jnp.float32)],
        compiler_params=params(mebibytes),
        cost_estimate=product_cost(blocks, weight),
        name="project",
    )(*blocks, weight)


def project_place_kernel(meta_ref, *refs):
    *block_refs, weight_ref, near_ref, keep_ref, send_ref, total_ref, token_ref = refs
    accumulate(
        total_ref, jnp.dot(rows_of(block_refs), weight_ref[0], preferred_element_type=jnp.float32)
    )

    @pl.when(pl.program_id(0) == LEVELS - 1)
    def _():
        core, x, y = meta_ref[0], meta_ref[1], meta_ref[2]
        rows = near_ref.shape[1]
        total = rows * X * Y
        edge = jnp.zeros((HALO, token_ref.shape[1]), jnp.float32)
        token_ref[pl.ds(0, HALO), :] = edge
        token_ref[pl.ds(HALO + total, HALO), :] = edge
        for second in range(4):
            for first in range(4):
                dx = jnp.where(core == 0, first, second)
                dy = jnp.where(core == 0, second, first)
                e = lax.rem(x + dx, X) * Y + lax.rem(y + dy, Y)
                at = pl.multiple_of(e * rows + HALO, 8)
                if second == 2:
                    block = total_ref[pl.ds(first * rows, rows), :]
                else:
                    block = near_ref[(0, 4, 0, 8)[second] + first].astype(jnp.float32)
                token_ref[pl.ds(at, rows), :] = block
        piece = total // (ZL * CORES)
        for zl in range(ZL):
            for out_ref, whose in ((keep_ref, core), (send_ref, 1 - core)):
                at = pl.multiple_of((zl * CORES + whose) * piece, 8)
                out_ref[zl] = token_ref[pl.ds(at, piece + 2 * HALO), :].astype(jnp.bfloat16)


def project_place(blocks, weight, near, core, x, y):
    _, rows, width = near.shape
    count = sum(b.shape[0] for b in blocks)
    total = rows * X * Y
    pieces = (ZL, total // (ZL * CORES) + 2 * HALO, width)
    whole = lambda shape: pl.BlockSpec(shape, lambda l, *_: (0, 0, 0))
    return pl.pallas_call(
        project_place_kernel,
        out_shape=(jax.ShapeDtypeStruct(pieces, jnp.bfloat16),) * 2,
        grid_spec=pltpu.PrefetchScalarGridSpec(
            num_scalar_prefetch=1,
            grid=(LEVELS,),
            in_specs=product_specs(blocks, weight) + [whole(near.shape)],
            out_specs=(whole(pieces),) * 2,
            scratch_shapes=[
                pltpu.VMEM((count * rows, width), jnp.float32),
                pltpu.VMEM((total + 2 * HALO, width), jnp.float32),
            ],
        ),
        compiler_params=params(18),
        cost_estimate=product_cost(blocks, weight),
        name="project_place",
    )(jnp.stack([core, x, y]), *blocks, weight, near)


def join_kernel(meta_ref, keep_ref, got_ref, own_ref, *away_refs):
    zl = meta_ref[0]

    def piece(index):
        return keep_ref[index].astype(jnp.float32) + got_ref[index].astype(jnp.float32)

    own_ref[...] = piece(zl).astype(jnp.bfloat16)
    for step, away_ref in zip((1, 2, 3), away_refs):
        away_ref[...] = piece(lax.rem(zl + ZL - step, ZL)).astype(jnp.bfloat16)


def join(keep, got, zl):
    count, rows, width = keep.shape
    whole = pl.BlockSpec(keep.shape, lambda i, m: (0, 0, 0))
    piece = pl.BlockSpec((rows, width), lambda i, m: (0, 0))
    return pl.pallas_call(
        join_kernel,
        out_shape=(jax.ShapeDtypeStruct((rows, width), jnp.bfloat16),) * count,
        grid_spec=pltpu.PrefetchScalarGridSpec(
            num_scalar_prefetch=1, grid=(1,), in_specs=[whole] * 2, out_specs=(piece,) * count
        ),
        compiler_params=params(8),
        cost_estimate=pl.CostEstimate(
            flops=keep.size, bytes_accessed=6 * keep.size, transcendentals=0
        ),
        name="join",
    )(zl.reshape(1), keep, got)


def sigmoid(v):
    return 1.0 / (1.0 + jnp.exp(-v))


def chain_kernel(meta_ref, scale_ref, *refs):
    *part_refs, one_ref, two_ref, left_ref, right_ref, gain_ref, grad_ref = refs
    rows, width = part_refs[0].shape
    own = rows - 2 * HALO
    joined = part_refs[0][...].astype(jnp.float32)
    for part_ref in part_refs[1:]:
        joined = joined + part_ref[...].astype(jnp.float32)
    even = meta_ref[2] == 0
    pick = lambda a, b: jnp.where(even, a[...].astype(jnp.float32), b[...].astype(jnp.float32))
    high = jnp.concatenate(
        [pick(one_ref, two_ref), pick(two_ref, one_ref), pick(left_ref, right_ref)], axis=0
    )
    gain = gain_ref[...]
    scale = scale_ref[0]
    start, length = meta_ref[0], meta_ref[1]
    position = start - HALO + lax.broadcasted_iota(jnp.int32, (rows, width), 0)

    def down(values):
        return jnp.concatenate([jnp.zeros((1, width), jnp.float32), values[:-1]], axis=0)

    def up(values):
        return jnp.concatenate([values[1:], jnp.zeros((1, width), jnp.float32)], axis=0)

    def target(step):
        lead = jnp.zeros((HALO - step, width), jnp.float32)
        return jnp.concatenate([lead, high[: rows - HALO + step]], axis=0)

    def state_and_slope(v):
        gate = sigmoid(v)
        return v * gate, gate * (1.0 + v * (1.0 - gate))

    def residual(state, step):
        return jnp.where(position + step < length, scale * (state - target(step)), 0.0)

    state_1, slope_1 = state_and_slope(joined)
    before_1 = down(state_1)
    state_2, slope_2 = state_and_slope(joined + gain * before_1)
    before_2 = down(state_2)
    state_3, slope_3 = state_and_slope(joined + gain * before_2)
    delta_3 = residual(state_3, 3) * slope_3
    delta_2 = (residual(state_2, 2) + up(gain * delta_3)) * slope_2
    delta_1 = (residual(state_1, 1) + up(gain * delta_2)) * slope_1
    total = delta_1 + delta_2 + delta_3
    mix = (delta_2 * before_1 + delta_3 * before_2)[HALO : HALO + own]
    rest = jnp.sum(mix, axis=0, keepdims=True)
    tail = []
    for _ in range(3):
        term = rest.astype(jnp.bfloat16).astype(jnp.float32)
        tail.append(term)
        rest = rest - term
    tail.append(jnp.zeros((TAIL - 3, width), jnp.float32))
    grad_ref[pl.ds(0, own), :] = total[HALO : HALO + own].astype(jnp.bfloat16)
    grad_ref[pl.ds(own, TAIL), :] = jnp.concatenate(tail, axis=0).astype(jnp.bfloat16)


def chain(parts, halves, gain, start, length, odd, scale):
    rows, width = parts[0].shape
    own = rows - 2 * HALO
    return pl.pallas_call(
        chain_kernel,
        out_shape=jax.ShapeDtypeStruct((own + TAIL, width), jnp.bfloat16),
        in_specs=[SMEM, SMEM] + [VMEM] * (len(parts) + len(halves) + 1),
        out_specs=VMEM,
        compiler_params=params(14),
        cost_estimate=pl.CostEstimate(
            flops=60 * rows * width, bytes_accessed=10 * rows * width, transcendentals=3 * rows * width
        ),
        name="chain",
    )(jnp.stack([start, length, odd]), scale.reshape(1), *parts, *halves, gain.reshape(1, width))


def weight_grad_kernel(meta_ref, features_ref, *refs):
    *group_refs, out_ref, mix_ref, grads_ref, held_ref, sem = refs
    half = grads_ref.shape[1] // ZH
    width = grads_ref.shape[2]
    held = [
        pltpu.make_async_copy(features_ref.at[:, at], held_ref.at[at], sem.at[at])
        for at in range(LEVELS)
    ]
    for copy in held:
        copy.start()
    mix = jnp.zeros((TAIL, width), jnp.float32)
    for at, group_ref in enumerate(group_refs):
        for part in range(2):
            slab = grads_ref.at[meta_ref[at] * 2 + part]
            for sequence in range(ZH):
                rows = group_ref[sequence, pl.ds(part * half, half), :]
                slab[pl.ds(sequence * half, half), :] = rows
        for sequence in range(ZH):
            mix = mix + group_ref[sequence, pl.ds(2 * half, TAIL), :].astype(jnp.float32)
    mix_ref[...] = jnp.sum(mix, axis=0, keepdims=True)
    blocks = held_ref.shape[1]
    for level, copy in enumerate(held):
        copy.wait()
        left = jnp.concatenate([held_ref[level, e] for e in range(blocks)], axis=1)
        right = grads_ref[...].reshape(-1, width)
        term = jnp.dot(left, right, preferred_element_type=jnp.float32)
        out_ref[level] = term.astype(jnp.bfloat16)


def weight_grad(features, groups, members):
    draft, _, columns, tokens = features.shape
    count, width = len(groups), groups[0].shape[2]
    return pl.pallas_call(
        weight_grad_kernel,
        out_shape=(
            jax.ShapeDtypeStruct((LEVELS, columns, width), jnp.bfloat16),
            jax.ShapeDtypeStruct((1, width), jnp.float32),
        ),
        in_specs=[SMEM, pl.BlockSpec(memory_space=pltpu.HBM)] + [VMEM] * count,
        out_specs=(VMEM, VMEM),
        scratch_shapes=[
            pltpu.VMEM((draft, tokens, width), jnp.bfloat16),
            pltpu.VMEM((LEVELS, draft, columns, tokens), jnp.bfloat16),
            pltpu.SemaphoreType.DMA((LEVELS,)),
        ],
        compiler_params=params(46),
        cost_estimate=pl.CostEstimate(
            flops=2 * draft * LEVELS * columns * tokens * width,
            bytes_accessed=2 * features.size + 2 * draft * tokens * width,
            transcendentals=0,
        ),
        name="weight_grad",
    )(jnp.stack(members), features, *groups)


def turn_kernel(traded_ref, out_ref):
    rows = traded_ref[:, 0].reshape(-1, traded_ref.shape[3])
    out_ref[0] = rows.astype(jnp.float32).T.astype(jnp.bfloat16)


def turn(traded):
    sequences, levels, rows, columns = traded.shape
    return pl.pallas_call(
        turn_kernel,
        grid=(levels,),
        out_shape=jax.ShapeDtypeStruct((levels, columns, sequences * rows), jnp.bfloat16),
        in_specs=[pl.BlockSpec((sequences, 1, rows, columns), lambda l: (0, l, 0, 0))],
        out_specs=pl.BlockSpec((1, columns, sequences * rows), lambda l: (l, 0, 0)),
        compiler_params=params(8),
        cost_estimate=pl.CostEstimate(flops=0, bytes_accessed=4 * traded.size, transcendentals=0),
        name="turn",
    )(traded)


def valid_total(lengths):
    running = jnp.zeros((), jnp.float32)
    for unroll in range(1, UNROLL + 1):
        running = running + jnp.sum(jnp.maximum(lengths - unroll, 0)).astype(jnp.float32)
    return running


def send_high(top, draft_index):
    members, draft_count = ZL * CORES, X * Y
    width = top.shape[1] // 2
    even = draft_index % 2 == 0
    left, right = top[:, :width], top[:, width:]
    straight, crossed, after_left, after_right = [], [], [], []
    for t in range(members):
        for e in range(draft_count):
            source = t * draft_count + e
            target = e // 2 * draft_count + 2 * t
            straight.append((source, target + e % 2))
            crossed.append((source, target + 1 - e % 2))
            if e % 2 == 0 and e > 0:
                after_left.append((source, target - draft_count))
                after_right.append((source, target - draft_count + 1))
    axes = ("tp", "draft")
    return (
        lax.ppermute(jnp.where(even, left, right), axes, straight),
        lax.ppermute(jnp.where(even, right, left), axes, crossed),
        lax.ppermute(left[:TAIL], axes, after_left),
        lax.ppermute(right[:TAIL], axes, after_right),
    )


def trade_columns(own):
    levels, rows, depth = own.shape
    quarters = own.reshape(levels, rows, ZH, depth // ZH).transpose(2, 0, 1, 3)
    return lax.all_to_all(quarters, "dp", split_axis=0, concat_axis=0, tiled=True)


def gather_grads(grad, features, zl, core):
    stack = lax.all_gather(grad, "dp", axis=0, tiled=False)
    above, below = from_z(stack, 1), from_z(stack, -1)
    far = jnp.concatenate([from_z(stack[:2], 2), from_z(stack[2:], -2)])
    other = from_other_core(stack)
    above, below, other, far, features = lax.optimization_barrier(
        (above, below, other, far, features)
    )
    swapped = [from_other_core(block) for block in (above, below, far)]

    def member(step, of_core):
        return (zl + step) % ZL * CORES + of_core

    groups = [stack, other, above, below, far] + swapped
    members = [member(0, core), member(0, 1 - core)]
    members += [member(step, core) for step in (1, 3, 2)]
    members += [member(step, 1 - core) for step in (1, 3, 2)]
    return weight_grad(features, groups, members)


def local(features, fc_weight, mix_gain, lengths):
    tp_index, zh = lax.axis_index("tp"), lax.axis_index("dp")
    draft_index = lax.axis_index("draft")
    zl, core = tp_index // CORES, tp_index % CORES
    x, y = draft_index // Y, draft_index % Y
    own_rows = features.shape[0]
    piece = own_rows * X * Y // (ZL * CORES)
    own = features.transpose(1, 0, 2)
    weight = fc_weight.transpose(1, 0, 2)

    next_, last, across = (plane_move(step, True)(own) for step in (1, 3, 2))
    low, high = pair(own, next_), pair(across, last)
    high, later = lax.optimization_barrier((high, own))
    traded = trade_columns(later)
    up_low, down_high = plane_move(1, False)(low), plane_move(-1, False)(high)
    up_high, down_low = plane_move(1, False)(high), plane_move(-1, False)(low)
    far_low, far_high = plane_move(1, False)(up_low), plane_move(-1, False)(down_high)
    near = project([low, high, up_low, up_high, down_low, down_high], weight, 58)
    far_low, far_high, near, traded = lax.optimization_barrier((far_low, far_high, near, traded))
    keep, send = project_place([far_low, far_high], weight, near, core, x, y)
    mine, *away = join(keep, from_other_core(send), zl)
    top, mine, traded = lax.optimization_barrier((own[LEVELS - 1], mine, traded))
    halves = send_high(top, draft_index)
    every = lax.all_gather(turn(traded), "draft", axis=0, tiled=False)
    parts = [mine] + [from_zl(block, step) for step, block in zip((1, 2, 3), away)]
    scale = LOSS_SCALE / valid_total(lengths)
    odd = draft_index % 2
    grad = chain(parts, halves, mix_gain, tp_index * piece, lengths[zh], odd, scale)
    fc_grad, mix_total = gather_grads(grad, every, zl, core)
    return (fc_grad.transpose(1, 0, 2), mix_total[0])


def solution(mesh):
    placed = (P(("dp", "draft"), None, "tp"), P("tp", None, "draft"), P("draft"), P())
    return jax.shard_map(
        local,
        mesh=mesh,
        in_specs=placed,
        out_specs=(P(("tp", "dp"), None, "draft"), P("draft")),
        check_vma=False,
    )
```

```python
import jax
import jax.numpy as jnp
from jax import lax
from jax.experimental import pallas as pl
from jax.experimental.pallas import tpu as pltpu
from jax.sharding import PartitionSpec as P

LEVELS = 3
UNROLL = 3
LOSS_SCALE = 64.0
HALO = 8
TAIL = 16
X, Y = 4, 4
ZL, CORES, ZH = 4, 2, 4
VMEM = pl.BlockSpec(memory_space=pltpu.VMEM)
SMEM = pl.BlockSpec(memory_space=pltpu.SMEM)


def params(mebibytes):
    return pltpu.CompilerParams(vmem_limit_bytes=mebibytes << 20)


def plane_move(step, first):
    pairs = []
    for t in range(ZL * CORES):
        for x in range(X):
            for y in range(Y):
                along_x = (t % CORES == 0) == first
                source = (x + step) % X * Y + y if along_x else x * Y + (y + step) % Y
                pairs.append((t * X * Y + source, t * X * Y + x * Y + y))
    return lambda block: lax.ppermute(block, ("tp", "draft"), pairs)


def from_other_core(block):
    return lax.ppermute(block, "tp", [(t ^ 1, t) for t in range(ZL * CORES)])


def from_zl(block, step):
    pairs = [((t // CORES + step) % ZL * CORES + t % CORES, t) for t in range(ZL * CORES)]
    return lax.ppermute(block, "tp", pairs)


def from_zh(block, step):
    return lax.ppermute(block, "dp", [((s + step) % ZH, s) for s in range(ZH)])


def from_z(block, step):
    pairs = []
    for t in range(ZL * CORES):
        for s in range(ZH):
            z = (s * ZL + t // CORES + step) % (ZL * ZH)
            pairs.append((((z % ZL) * CORES + t % CORES) * ZH + z // ZL, t * ZH + s))
    return lax.ppermute(block, ("tp", "dp"), pairs)


def pair_kernel(first_ref, second_ref, out_ref):
    out_ref[0] = first_ref[...]
    out_ref[1] = second_ref[...]


def pair(first, second):
    return pl.pallas_call(
        pair_kernel,
        out_shape=jax.ShapeDtypeStruct((2,) + first.shape, first.dtype),
        in_specs=[VMEM] * 2,
        out_specs=VMEM,
        compiler_params=params(4),
        cost_estimate=pl.CostEstimate(flops=0, bytes_accessed=8 * first.size, transcendentals=0),
        name="pair",
    )(first, second)


def rows_of(block_refs):
    return jnp.concatenate([r[...].reshape(-1, r.shape[-1]) for r in block_refs], axis=0)


def accumulate(total_ref, term):
    level = pl.program_id(0)

    @pl.when(level == 0)
    def _():
        total_ref[...] = term

    @pl.when(level > 0)
    def _():
        total_ref[...] += term


def project_kernel(*refs):
    *block_refs, weight_ref, out_ref, total_ref = refs
    accumulate(
        total_ref, jnp.dot(rows_of(block_refs), weight_ref[0], preferred_element_type=jnp.float32)
    )

    @pl.when(pl.program_id(0) == LEVELS - 1)
    def _():
        out_ref[...] = total_ref[...].astype(jnp.bfloat16).reshape(out_ref.shape)


def product_specs(blocks, weight):
    _, _, rows, depth = blocks[0].shape
    specs = [pl.BlockSpec((b.shape[0], 1, rows, depth), lambda l, *_: (0, l, 0, 0)) for b in blocks]
    return specs + [pl.BlockSpec((1, depth, weight.shape[2]), lambda l, *_: (l, 0, 0))]


def product_cost(blocks, weight):
    size = sum(b.size for b in blocks)
    return pl.CostEstimate(flops=0, bytes_accessed=2 * size, transcendentals=0)


def project(blocks, weight, mebibytes):
    rows, width = blocks[0].shape[2], weight.shape[2]
    count = sum(b.shape[0] for b in blocks)
    return pl.pallas_call(
        project_kernel,
        grid=(LEVELS,),
        out_shape=jax.ShapeDtypeStruct((count, rows, width), jnp.bfloat16),
        in_specs=product_specs(blocks, weight),
        out_specs=pl.BlockSpec((count, rows, width), lambda l: (0, 0, 0)),
        scratch_shapes=[pltpu.VMEM((count * rows, width), jnp.float32)],
        compiler_params=params(mebibytes),
        cost_estimate=product_cost(blocks, weight),
        name="project",
    )(*blocks, weight)


def project_place_kernel(meta_ref, *refs):
    *block_refs, weight_ref, near_ref, keep_ref, send_ref, total_ref, token_ref = refs
    accumulate(
        total_ref, jnp.dot(rows_of(block_refs), weight_ref[0], preferred_element_type=jnp.float32)
    )

    @pl.when(pl.program_id(0) == LEVELS - 1)
    def _():
        core, x, y = meta_ref[0], meta_ref[1], meta_ref[2]
        rows = near_ref.shape[1]
        total = rows * X * Y
        edge = jnp.zeros((HALO, token_ref.shape[1]), jnp.float32)
        token_ref[pl.ds(0, HALO), :] = edge
        token_ref[pl.ds(HALO + total, HALO), :] = edge
        for second in range(4):
            for first in range(4):
                dx = jnp.where(core == 0, first, second)
                dy = jnp.where(core == 0, second, first)
                e = lax.rem(x + dx, X) * Y + lax.rem(y + dy, Y)
                at = pl.multiple_of(e * rows + HALO, 8)
                if second == 2:
                    block = total_ref[pl.ds(first * rows, rows), :]
                else:
                    block = near_ref[(0, 4, 0, 8)[second] + first].astype(jnp.float32)
                token_ref[pl.ds(at, rows), :] = block
        piece = total // (ZL * CORES)
        for zl in range(ZL):
            for out_ref, whose in ((keep_ref, core), (send_ref, 1 - core)):
                at = pl.multiple_of((zl * CORES + whose) * piece, 8)
                out_ref[zl] = token_ref[pl.ds(at, piece + 2 * HALO), :].astype(jnp.bfloat16)


def project_place(blocks, weight, near, core, x, y):
    _, rows, width = near.shape
    count = sum(b.shape[0] for b in blocks)
    total = rows * X * Y
    pieces = (ZL, total // (ZL * CORES) + 2 * HALO, width)
    whole = lambda shape: pl.BlockSpec(shape, lambda l, *_: (0, 0, 0))
    return pl.pallas_call(
        project_place_kernel,
        out_shape=(jax.ShapeDtypeStruct(pieces, jnp.bfloat16),) * 2,
        grid_spec=pltpu.PrefetchScalarGridSpec(
            num_scalar_prefetch=1,
            grid=(LEVELS,),
            in_specs=product_specs(blocks, weight) + [whole(near.shape)],
            out_specs=(whole(pieces),) * 2,
            scratch_shapes=[
                pltpu.VMEM((count * rows, width), jnp.float32),
                pltpu.VMEM((total + 2 * HALO, width), jnp.float32),
            ],
        ),
        compiler_params=params(18),
        cost_estimate=product_cost(blocks, weight),
        name="project_place",
    )(jnp.stack([core, x, y]), *blocks, weight, near)


def join_kernel(meta_ref, keep_ref, got_ref, own_ref, *away_refs):
    zl = meta_ref[0]

    def piece(index):
        return keep_ref[index].astype(jnp.float32) + got_ref[index].astype(jnp.float32)

    own_ref[...] = piece(zl).astype(jnp.bfloat16)
    for step, away_ref in zip((1, 2, 3), away_refs):
        away_ref[...] = piece(lax.rem(zl + ZL - step, ZL)).astype(jnp.bfloat16)


def join(keep, got, zl):
    count, rows, width = keep.shape
    whole = pl.BlockSpec(keep.shape, lambda i, m: (0, 0, 0))
    piece = pl.BlockSpec((rows, width), lambda i, m: (0, 0))
    return pl.pallas_call(
        join_kernel,
        out_shape=(jax.ShapeDtypeStruct((rows, width), jnp.bfloat16),) * count,
        grid_spec=pltpu.PrefetchScalarGridSpec(
            num_scalar_prefetch=1, grid=(1,), in_specs=[whole] * 2, out_specs=(piece,) * count
        ),
        compiler_params=params(8),
        cost_estimate=pl.CostEstimate(
            flops=keep.size, bytes_accessed=6 * keep.size, transcendentals=0
        ),
        name="join",
    )(zl.reshape(1), keep, got)


def sigmoid(v):
    return 1.0 / (1.0 + jnp.exp(-v))


def chain_kernel(meta_ref, scale_ref, *refs):
    *part_refs, one_ref, two_ref, left_ref, right_ref, gain_ref, grad_ref = refs
    rows, width = part_refs[0].shape
    own = rows - 2 * HALO
    joined = part_refs[0][...].astype(jnp.float32)
    for part_ref in part_refs[1:]:
        joined = joined + part_ref[...].astype(jnp.float32)
    even = meta_ref[2] == 0
    pick = lambda a, b: jnp.where(even, a[...].astype(jnp.float32), b[...].astype(jnp.float32))
    high = jnp.concatenate(
        [pick(one_ref, two_ref), pick(two_ref, one_ref), pick(left_ref, right_ref)], axis=0
    )
    gain = gain_ref[...]
    scale = scale_ref[0]
    start, length = meta_ref[0], meta_ref[1]
    position = start - HALO + lax.broadcasted_iota(jnp.int32, (rows, width), 0)

    def down(values):
        return jnp.concatenate([jnp.zeros((1, width), jnp.float32), values[:-1]], axis=0)

    def up(values):
        return jnp.concatenate([values[1:], jnp.zeros((1, width), jnp.float32)], axis=0)

    def target(step):
        lead = jnp.zeros((HALO - step, width), jnp.float32)
        return jnp.concatenate([lead, high[: rows - HALO + step]], axis=0)

    def state_and_slope(v):
        gate = sigmoid(v)
        return v * gate, gate * (1.0 + v * (1.0 - gate))

    def residual(state, step):
        return jnp.where(position + step < length, scale * (state - target(step)), 0.0)

    state_1, slope_1 = state_and_slope(joined)
    before_1 = down(state_1)
    state_2, slope_2 = state_and_slope(joined + gain * before_1)
    before_2 = down(state_2)
    state_3, slope_3 = state_and_slope(joined + gain * before_2)
    delta_3 = residual(state_3, 3) * slope_3
    delta_2 = (residual(state_2, 2) + up(gain * delta_3)) * slope_2
    delta_1 = (residual(state_1, 1) + up(gain * delta_2)) * slope_1
    total = delta_1 + delta_2 + delta_3
    mix = (delta_2 * before_1 + delta_3 * before_2)[HALO : HALO + own]
    rest = jnp.sum(mix, axis=0, keepdims=True)
    tail = []
    for _ in range(3):
        term = rest.astype(jnp.bfloat16).astype(jnp.float32)
        tail.append(term)
        rest = rest - term
    tail.append(jnp.zeros((TAIL - 3, width), jnp.float32))
    grad_ref[pl.ds(0, own), :] = total[HALO : HALO + own].astype(jnp.bfloat16)
    grad_ref[pl.ds(own, TAIL), :] = jnp.concatenate(tail, axis=0).astype(jnp.bfloat16)


def chain(parts, halves, gain, start, length, odd, scale):
    rows, width = parts[0].shape
    own = rows - 2 * HALO
    return pl.pallas_call(
        chain_kernel,
        out_shape=jax.ShapeDtypeStruct((own + TAIL, width), jnp.bfloat16),
        in_specs=[SMEM, SMEM] + [VMEM] * (len(parts) + len(halves) + 1),
        out_specs=VMEM,
        compiler_params=params(14),
        cost_estimate=pl.CostEstimate(
            flops=60 * rows * width, bytes_accessed=10 * rows * width, transcendentals=3 * rows * width
        ),
        name="chain",
    )(jnp.stack([start, length, odd]), scale.reshape(1), *parts, *halves, gain.reshape(1, width))


def weight_grad_kernel(meta_ref, features_ref, *refs):
    *group_refs, out_ref, mix_ref, grads_ref, held_ref, sem = refs
    half = grads_ref.shape[1] // ZH
    width = grads_ref.shape[2]
    held = [
        pltpu.make_async_copy(features_ref.at[:, at], held_ref.at[at], sem.at[at])
        for at in range(LEVELS)
    ]
    for copy in held:
        copy.start()
    mix = jnp.zeros((TAIL, width), jnp.float32)
    for at, group_ref in enumerate(group_refs):
        for part in range(2):
            slab = grads_ref.at[meta_ref[at] * 2 + part]
            for sequence in range(ZH):
                rows = group_ref[sequence, pl.ds(part * half, half), :]
                slab[pl.ds(sequence * half, half), :] = rows
        for sequence in range(ZH):
            mix = mix + group_ref[sequence, pl.ds(2 * half, TAIL), :].astype(jnp.float32)
    mix_ref[...] = jnp.sum(mix, axis=0, keepdims=True)
    blocks = held_ref.shape[1]
    for level, copy in enumerate(held):
        copy.wait()
        left = jnp.concatenate([held_ref[level, e] for e in range(blocks)], axis=1)
        right = grads_ref[...].reshape(-1, width)
        term = jnp.dot(left, right, preferred_element_type=jnp.float32)
        out_ref[level] = term.astype(jnp.bfloat16)


def weight_grad(features, groups, members):
    draft, _, columns, tokens = features.shape
    count, width = len(groups), groups[0].shape[2]
    return pl.pallas_call(
        weight_grad_kernel,
        out_shape=(
            jax.ShapeDtypeStruct((LEVELS, columns, width), jnp.bfloat16),
            jax.ShapeDtypeStruct((1, width), jnp.float32),
        ),
        in_specs=[SMEM, pl.BlockSpec(memory_space=pltpu.HBM)] + [VMEM] * count,
        out_specs=(VMEM, VMEM),
        scratch_shapes=[
            pltpu.VMEM((draft, tokens, width), jnp.bfloat16),
            pltpu.VMEM((LEVELS, draft, columns, tokens), jnp.bfloat16),
            pltpu.SemaphoreType.DMA((LEVELS,)),
        ],
        compiler_params=params(46),
        cost_estimate=pl.CostEstimate(
            flops=2 * draft * LEVELS * columns * tokens * width,
            bytes_accessed=2 * features.size + 2 * draft * tokens * width,
            transcendentals=0,
        ),
        name="weight_grad",
    )(jnp.stack(members), features, *groups)


def turn_kernel(traded_ref, out_ref):
    rows = traded_ref[:, 0].reshape(-1, traded_ref.shape[3])
    out_ref[0] = rows.astype(jnp.float32).T.astype(jnp.bfloat16)


def turn(traded):
    sequences, levels, rows, columns = traded.shape
    return pl.pallas_call(
        turn_kernel,
        grid=(levels,),
        out_shape=jax.ShapeDtypeStruct((levels, columns, sequences * rows), jnp.bfloat16),
        in_specs=[pl.BlockSpec((sequences, 1, rows, columns), lambda l: (0, l, 0, 0))],
        out_specs=pl.BlockSpec((1, columns, sequences * rows), lambda l: (l, 0, 0)),
        compiler_params=params(8),
        cost_estimate=pl.CostEstimate(flops=0, bytes_accessed=4 * traded.size, transcendentals=0),
        name="turn",
    )(traded)


def valid_total(lengths):
    running = jnp.zeros((), jnp.float32)
    for unroll in range(1, UNROLL + 1):
        running = running + jnp.sum(jnp.maximum(lengths - unroll, 0)).astype(jnp.float32)
    return running


def send_high(top, draft_index):
    members, draft_count = ZL * CORES, X * Y
    width = top.shape[1] // 2
    even = draft_index % 2 == 0
    left, right = top[:, :width], top[:, width:]
    straight, crossed, after_left, after_right = [], [], [], []
    for t in range(members):
        for e in range(draft_count):
            source = t * draft_count + e
            target = e // 2 * draft_count + 2 * t
            straight.append((source, target + e % 2))
            crossed.append((source, target + 1 - e % 2))
            if e % 2 == 0 and e > 0:
                after_left.append((source, target - draft_count))
                after_right.append((source, target - draft_count + 1))
    axes = ("tp", "draft")
    return (
        lax.ppermute(jnp.where(even, left, right), axes, straight),
        lax.ppermute(jnp.where(even, right, left), axes, crossed),
        lax.ppermute(left[:TAIL], axes, after_left),
        lax.ppermute(right[:TAIL], axes, after_right),
    )


def trade_columns(own):
    levels, rows, depth = own.shape
    quarters = own.reshape(levels, rows, ZH, depth // ZH).transpose(2, 0, 1, 3)
    return lax.all_to_all(quarters, "dp", split_axis=0, concat_axis=0, tiled=True)


def gather_grads(grad, features, zl, core):
    stack = lax.all_gather(grad, "dp", axis=0, tiled=False)
    above, below = from_z(stack, 1), from_z(stack, -1)
    far = jnp.concatenate([from_z(stack[:2], 2), from_z(stack[2:], -2)])
    other = from_other_core(stack)
    above, below, other, far, features = lax.optimization_barrier(
        (above, below, other, far, features)
    )
    swapped = [from_other_core(block) for block in (above, below, far)]

    def member(step, of_core):
        return (zl + step) % ZL * CORES + of_core

    groups = [stack, other, above, below, far] + swapped
    members = [member(0, core), member(0, 1 - core)]
    members += [member(step, core) for step in (1, 3, 2)]
    members += [member(step, 1 - core) for step in (1, 3, 2)]
    return weight_grad(features, groups, members)


def local(features, fc_weight, mix_gain, lengths):
    tp_index, zh = lax.axis_index("tp"), lax.axis_index("dp")
    draft_index = lax.axis_index("draft")
    zl, core = tp_index // CORES, tp_index % CORES
    x, y = draft_index // Y, draft_index % Y
    own_rows = features.shape[0]
    piece = own_rows * X * Y // (ZL * CORES)
    own = features.transpose(1, 0, 2)
    weight = fc_weight.transpose(1, 0, 2)

    next_, last, across = (plane_move(step, True)(own) for step in (1, 3, 2))
    low, high = pair(own, next_), pair(across, last)
    up_low, down_high = plane_move(1, False)(low), plane_move(-1, False)(high)
    up_high, down_low = plane_move(1, False)(high), plane_move(-1, False)(low)
    up_low, later = lax.optimization_barrier((up_low, own))
    traded = trade_columns(later)
    far_low, far_high = plane_move(1, False)(up_low), plane_move(-1, False)(down_high)
    near = project([low, high, up_low, up_high, down_low, down_high], weight, 58)
    far_low, far_high, near = lax.optimization_barrier((far_low, far_high, near))
    keep, send = project_place([far_low, far_high], weight, near, core, x, y)
    mine, *away = join(keep, from_other_core(send), zl)
    top, mine, traded = lax.optimization_barrier((own[LEVELS - 1], mine, traded))
    halves = send_high(top, draft_index)
    every = lax.all_gather(turn(traded), "draft", axis=0, tiled=False)
    parts = [mine] + [from_zl(block, step) for step, block in zip((1, 2, 3), away)]
    scale = LOSS_SCALE / valid_total(lengths)
    odd = draft_index % 2
    grad = chain(parts, halves, mix_gain, tp_index * piece, lengths[zh], odd, scale)
    fc_grad, mix_total = gather_grads(grad, every, zl, core)
    return (fc_grad.transpose(1, 0, 2), mix_total[0])


def solution(mesh):
    placed = (P(("dp", "draft"), None, "tp"), P("tp", None, "draft"), P("draft"), P())
    return jax.shard_map(
        local,
        mesh=mesh,
        in_specs=placed,
        out_specs=(P(("tp", "dp"), None, "draft"), P("draft")),
        check_vma=False,
    )
```

```python
import jax
import jax.numpy as jnp
from jax import lax
from jax.experimental import pallas as pl
from jax.experimental.pallas import tpu as pltpu
from jax.sharding import PartitionSpec as P

LEVELS = 3
UNROLL = 3
LOSS_SCALE = 64.0
HALO = 8
TAIL = 16
X, Y = 4, 4
ZL, CORES, ZH = 4, 2, 4
VMEM = pl.BlockSpec(memory_space=pltpu.VMEM)
SMEM = pl.BlockSpec(memory_space=pltpu.SMEM)


def params(mebibytes):
    return pltpu.CompilerParams(vmem_limit_bytes=mebibytes << 20)


def plane_move(step, first):
    pairs = []
    for t in range(ZL * CORES):
        for x in range(X):
            for y in range(Y):
                along_x = (t % CORES == 0) == first
                source = (x + step) % X * Y + y if along_x else x * Y + (y + step) % Y
                pairs.append((t * X * Y + source, t * X * Y + x * Y + y))
    return lambda block: lax.ppermute(block, ("tp", "draft"), pairs)


def from_other_core(block):
    return lax.ppermute(block, "tp", [(t ^ 1, t) for t in range(ZL * CORES)])


def from_zl(block, step):
    pairs = [((t // CORES + step) % ZL * CORES + t % CORES, t) for t in range(ZL * CORES)]
    return lax.ppermute(block, "tp", pairs)


def from_zh(block, step):
    return lax.ppermute(block, "dp", [((s + step) % ZH, s) for s in range(ZH)])


def from_z(block, step):
    pairs = []
    for t in range(ZL * CORES):
        for s in range(ZH):
            z = (s * ZL + t // CORES + step) % (ZL * ZH)
            pairs.append((((z % ZL) * CORES + t % CORES) * ZH + z // ZL, t * ZH + s))
    return lax.ppermute(block, ("tp", "dp"), pairs)


def pair_kernel(first_ref, second_ref, out_ref):
    out_ref[0] = first_ref[...]
    out_ref[1] = second_ref[...]


def pair(first, second):
    return pl.pallas_call(
        pair_kernel,
        out_shape=jax.ShapeDtypeStruct((2,) + first.shape, first.dtype),
        in_specs=[VMEM] * 2,
        out_specs=VMEM,
        compiler_params=params(4),
        cost_estimate=pl.CostEstimate(flops=0, bytes_accessed=8 * first.size, transcendentals=0),
        name="pair",
    )(first, second)


def rows_of(block_refs):
    return jnp.concatenate([r[...].reshape(-1, r.shape[-1]) for r in block_refs], axis=0)


def accumulate(total_ref, term):
    level = pl.program_id(0)

    @pl.when(level == 0)
    def _():
        total_ref[...] = term

    @pl.when(level > 0)
    def _():
        total_ref[...] += term


def project_kernel(*refs):
    *block_refs, weight_ref, out_ref, total_ref = refs
    accumulate(
        total_ref, jnp.dot(rows_of(block_refs), weight_ref[0], preferred_element_type=jnp.float32)
    )

    @pl.when(pl.program_id(0) == LEVELS - 1)
    def _():
        out_ref[...] = total_ref[...].astype(jnp.bfloat16).reshape(out_ref.shape)


def product_specs(blocks, weight):
    _, _, rows, depth = blocks[0].shape
    specs = [pl.BlockSpec((b.shape[0], 1, rows, depth), lambda l, *_: (0, l, 0, 0)) for b in blocks]
    return specs + [pl.BlockSpec((1, depth, weight.shape[2]), lambda l, *_: (l, 0, 0))]


def product_cost(blocks, weight):
    size = sum(b.size for b in blocks)
    return pl.CostEstimate(flops=0, bytes_accessed=2 * size, transcendentals=0)


def project(blocks, weight, mebibytes):
    rows, width = blocks[0].shape[2], weight.shape[2]
    count = sum(b.shape[0] for b in blocks)
    return pl.pallas_call(
        project_kernel,
        grid=(LEVELS,),
        out_shape=jax.ShapeDtypeStruct((count, rows, width), jnp.bfloat16),
        in_specs=product_specs(blocks, weight),
        out_specs=pl.BlockSpec((count, rows, width), lambda l: (0, 0, 0)),
        scratch_shapes=[pltpu.VMEM((count * rows, width), jnp.float32)],
        compiler_params=params(mebibytes),
        cost_estimate=product_cost(blocks, weight),
        name="project",
    )(*blocks, weight)


def project_place_kernel(meta_ref, *refs):
    *block_refs, weight_ref, near_ref, keep_ref, send_ref, total_ref, token_ref = refs
    accumulate(
        total_ref, jnp.dot(rows_of(block_refs), weight_ref[0], preferred_element_type=jnp.float32)
    )

    @pl.when(pl.program_id(0) == LEVELS - 1)
    def _():
        core, x, y = meta_ref[0], meta_ref[1], meta_ref[2]
        rows = near_ref.shape[1]
        total = rows * X * Y
        edge = jnp.zeros((HALO, token_ref.shape[1]), jnp.float32)
        token_ref[pl.ds(0, HALO), :] = edge
        token_ref[pl.ds(HALO + total, HALO), :] = edge
        for second in range(4):
            for first in range(4):
                dx = jnp.where(core == 0, first, second)
                dy = jnp.where(core == 0, second, first)
                e = lax.rem(x + dx, X) * Y + lax.rem(y + dy, Y)
                at = pl.multiple_of(e * rows + HALO, 8)
                if second == 2:
                    block = total_ref[pl.ds(first * rows, rows), :]
                else:
                    block = near_ref[(0, 4, 0, 8)[second] + first].astype(jnp.float32)
                token_ref[pl.ds(at, rows), :] = block
        piece = total // (ZL * CORES)
        for zl in range(ZL):
            for out_ref, whose in ((keep_ref, core), (send_ref, 1 - core)):
                at = pl.multiple_of((zl * CORES + whose) * piece, 8)
                out_ref[zl] = token_ref[pl.ds(at, piece + 2 * HALO), :].astype(jnp.bfloat16)


def project_place(blocks, weight, near, core, x, y):
    _, rows, width = near.shape
    count = sum(b.shape[0] for b in blocks)
    total = rows * X * Y
    pieces = (ZL, total // (ZL * CORES) + 2 * HALO, width)
    whole = lambda shape: pl.BlockSpec(shape, lambda l, *_: (0, 0, 0))
    return pl.pallas_call(
        project_place_kernel,
        out_shape=(jax.ShapeDtypeStruct(pieces, jnp.bfloat16),) * 2,
        grid_spec=pltpu.PrefetchScalarGridSpec(
            num_scalar_prefetch=1,
            grid=(LEVELS,),
            in_specs=product_specs(blocks, weight) + [whole(near.shape)],
            out_specs=(whole(pieces),) * 2,
            scratch_shapes=[
                pltpu.VMEM((count * rows, width), jnp.float32),
                pltpu.VMEM((total + 2 * HALO, width), jnp.float32),
            ],
        ),
        compiler_params=params(18),
        cost_estimate=product_cost(blocks, weight),
        name="project_place",
    )(jnp.stack([core, x, y]), *blocks, weight, near)


def join_kernel(meta_ref, keep_ref, got_ref, own_ref, *away_refs):
    zl = meta_ref[0]

    def piece(index):
        return keep_ref[index].astype(jnp.float32) + got_ref[index].astype(jnp.float32)

    own_ref[...] = piece(zl).astype(jnp.bfloat16)
    for step, away_ref in zip((1, 2, 3), away_refs):
        away_ref[...] = piece(lax.rem(zl + ZL - step, ZL)).astype(jnp.bfloat16)


def join(keep, got, zl):
    count, rows, width = keep.shape
    whole = pl.BlockSpec(keep.shape, lambda i, m: (0, 0, 0))
    piece = pl.BlockSpec((rows, width), lambda i, m: (0, 0))
    return pl.pallas_call(
        join_kernel,
        out_shape=(jax.ShapeDtypeStruct((rows, width), jnp.bfloat16),) * count,
        grid_spec=pltpu.PrefetchScalarGridSpec(
            num_scalar_prefetch=1, grid=(1,), in_specs=[whole] * 2, out_specs=(piece,) * count
        ),
        compiler_params=params(8),
        cost_estimate=pl.CostEstimate(
            flops=keep.size, bytes_accessed=6 * keep.size, transcendentals=0
        ),
        name="join",
    )(zl.reshape(1), keep, got)


def sigmoid(v):
    return 1.0 / (1.0 + jnp.exp(-v))


def chain_kernel(meta_ref, lengths_ref, *refs):
    *part_refs, one_ref, two_ref, left_ref, right_ref, gain_ref, grad_ref = refs
    rows, width = part_refs[0].shape
    own = rows - 2 * HALO
    joined = part_refs[0][...].astype(jnp.float32)
    for part_ref in part_refs[1:]:
        joined = joined + part_ref[...].astype(jnp.float32)
    even = meta_ref[2] == 0
    pick = lambda a, b: jnp.where(even, a[...].astype(jnp.float32), b[...].astype(jnp.float32))
    high = jnp.concatenate(
        [pick(one_ref, two_ref), pick(two_ref, one_ref), pick(left_ref, right_ref)], axis=0
    )
    gain = gain_ref[...]
    start, length = meta_ref[0], lengths_ref[meta_ref[1]]
    valid = jnp.int32(0)
    for step in range(1, UNROLL + 1):
        for sequence in range(lengths_ref.shape[0]):
            valid = valid + jnp.maximum(lengths_ref[sequence] - step, 0)
    scale = LOSS_SCALE / jnp.full((1, width), valid, jnp.int32).astype(jnp.float32)
    position = start - HALO + lax.broadcasted_iota(jnp.int32, (rows, width), 0)

    def down(values):
        return jnp.concatenate([jnp.zeros((1, width), jnp.float32), values[:-1]], axis=0)

    def up(values):
        return jnp.concatenate([values[1:], jnp.zeros((1, width), jnp.float32)], axis=0)

    def target(step):
        lead = jnp.zeros((HALO - step, width), jnp.float32)
        return jnp.concatenate([lead, high[: rows - HALO + step]], axis=0)

    def state_and_slope(v):
        gate = sigmoid(v)
        return v * gate, gate * (1.0 + v * (1.0 - gate))

    def residual(state, step):
        return jnp.where(position + step < length, scale * (state - target(step)), 0.0)

    state_1, slope_1 = state_and_slope(joined)
    before_1 = down(state_1)
    state_2, slope_2 = state_and_slope(joined + gain * before_1)
    before_2 = down(state_2)
    state_3, slope_3 = state_and_slope(joined + gain * before_2)
    delta_3 = residual(state_3, 3) * slope_3
    delta_2 = (residual(state_2, 2) + up(gain * delta_3)) * slope_2
    delta_1 = (residual(state_1, 1) + up(gain * delta_2)) * slope_1
    total = delta_1 + delta_2 + delta_3
    mix = (delta_2 * before_1 + delta_3 * before_2)[HALO : HALO + own]
    rest = jnp.sum(mix, axis=0, keepdims=True)
    tail = []
    for _ in range(3):
        term = rest.astype(jnp.bfloat16).astype(jnp.float32)
        tail.append(term)
        rest = rest - term
    tail.append(jnp.zeros((TAIL - 3, width), jnp.float32))
    grad_ref[pl.ds(0, own), :] = total[HALO : HALO + own].astype(jnp.bfloat16)
    grad_ref[pl.ds(own, TAIL), :] = jnp.concatenate(tail, axis=0).astype(jnp.bfloat16)


def chain(parts, halves, gain, start, zh, odd, lengths):
    rows, width = parts[0].shape
    own = rows - 2 * HALO
    return pl.pallas_call(
        chain_kernel,
        out_shape=jax.ShapeDtypeStruct((own + TAIL, width), jnp.bfloat16),
        in_specs=[SMEM, SMEM] + [VMEM] * (len(parts) + len(halves) + 1),
        out_specs=VMEM,
        compiler_params=params(14),
        cost_estimate=pl.CostEstimate(
            flops=60 * rows * width, bytes_accessed=10 * rows * width, transcendentals=3 * rows * width
        ),
        name="chain",
    )(jnp.stack([start, zh, odd]), lengths, *parts, *halves, gain.reshape(1, width))


def weight_grad_kernel(meta_ref, features_ref, *refs):
    *group_refs, out_ref, mix_ref, grads_ref, held_ref, sem = refs
    half = grads_ref.shape[1] // ZH
    width = grads_ref.shape[2]
    held = [
        pltpu.make_async_copy(features_ref.at[:, at], held_ref.at[at], sem.at[at])
        for at in range(LEVELS)
    ]
    for copy in held:
        copy.start()
    mix = jnp.zeros((TAIL, width), jnp.float32)
    for at, group_ref in enumerate(group_refs):
        for part in range(2):
            slab = grads_ref.at[meta_ref[at] * 2 + part]
            for sequence in range(ZH):
                rows = group_ref[sequence, pl.ds(part * half, half), :]
                slab[pl.ds(sequence * half, half), :] = rows
        for sequence in range(ZH):
            mix = mix + group_ref[sequence, pl.ds(2 * half, TAIL), :].astype(jnp.float32)
    mix_ref[...] = jnp.sum(mix, axis=0, keepdims=True)
    blocks = held_ref.shape[1]
    for level, copy in enumerate(held):
        copy.wait()
        left = jnp.concatenate([held_ref[level, e] for e in range(blocks)], axis=1)
        right = grads_ref[...].reshape(-1, width)
        term = jnp.dot(left, right, preferred_element_type=jnp.float32)
        out_ref[level] = term.astype(jnp.bfloat16)


def weight_grad(features, groups, members):
    draft, _, columns, tokens = features.shape
    count, width = len(groups), groups[0].shape[2]
    return pl.pallas_call(
        weight_grad_kernel,
        out_shape=(
            jax.ShapeDtypeStruct((LEVELS, columns, width), jnp.bfloat16),
            jax.ShapeDtypeStruct((1, width), jnp.float32),
        ),
        in_specs=[SMEM, pl.BlockSpec(memory_space=pltpu.HBM)] + [VMEM] * count,
        out_specs=(VMEM, VMEM),
        scratch_shapes=[
            pltpu.VMEM((draft, tokens, width), jnp.bfloat16),
            pltpu.VMEM((LEVELS, draft, columns, tokens), jnp.bfloat16),
            pltpu.SemaphoreType.DMA((LEVELS,)),
        ],
        compiler_params=params(46),
        cost_estimate=pl.CostEstimate(
            flops=2 * draft * LEVELS * columns * tokens * width,
            bytes_accessed=2 * features.size + 2 * draft * tokens * width,
            transcendentals=0,
        ),
        name="weight_grad",
    )(jnp.stack(members), features, *groups)


def turn_kernel(traded_ref, out_ref):
    rows = traded_ref[:, 0].reshape(-1, traded_ref.shape[3])
    out_ref[0] = rows.astype(jnp.float32).T.astype(jnp.bfloat16)


def turn(traded):
    sequences, levels, rows, columns = traded.shape
    return pl.pallas_call(
        turn_kernel,
        grid=(levels,),
        out_shape=jax.ShapeDtypeStruct((levels, columns, sequences * rows), jnp.bfloat16),
        in_specs=[pl.BlockSpec((sequences, 1, rows, columns), lambda l: (0, l, 0, 0))],
        out_specs=pl.BlockSpec((1, columns, sequences * rows), lambda l: (l, 0, 0)),
        compiler_params=params(8),
        cost_estimate=pl.CostEstimate(flops=0, bytes_accessed=4 * traded.size, transcendentals=0),
        name="turn",
    )(traded)


def send_high(top, draft_index):
    members, draft_count = ZL * CORES, X * Y
    width = top.shape[1] // 2
    even = draft_index % 2 == 0
    left, right = top[:, :width], top[:, width:]
    straight, crossed, after_left, after_right = [], [], [], []
    for t in range(members):
        for e in range(draft_count):
            source = t * draft_count + e
            target = e // 2 * draft_count + 2 * t
            straight.append((source, target + e % 2))
            crossed.append((source, target + 1 - e % 2))
            if e % 2 == 0 and e > 0:
                after_left.append((source, target - draft_count))
                after_right.append((source, target - draft_count + 1))
    axes = ("tp", "draft")
    return (
        lax.ppermute(jnp.where(even, left, right), axes, straight),
        lax.ppermute(jnp.where(even, right, left), axes, crossed),
        lax.ppermute(left[:TAIL], axes, after_left),
        lax.ppermute(right[:TAIL], axes, after_right),
    )


def trade_columns(own):
    levels, rows, depth = own.shape
    quarters = own.reshape(levels, rows, ZH, depth // ZH).transpose(2, 0, 1, 3)
    return lax.all_to_all(quarters, "dp", split_axis=0, concat_axis=0, tiled=True)


def gather_grads(grad, features, zl, core):
    stack = lax.all_gather(grad, "dp", axis=0, tiled=False)
    above, below = from_z(stack, 1), from_z(stack, -1)
    far = jnp.concatenate([from_z(stack[:2], 2), from_z(stack[2:], -2)])
    other = from_other_core(stack)
    above, below, other, far, features = lax.optimization_barrier(
        (above, below, other, far, features)
    )
    swapped = [from_other_core(block) for block in (above, below, far)]

    def member(step, of_core):
        return (zl + step) % ZL * CORES + of_core

    groups = [stack, other, above, below, far] + swapped
    members = [member(0, core), member(0, 1 - core)]
    members += [member(step, core) for step in (1, 3, 2)]
    members += [member(step, 1 - core) for step in (1, 3, 2)]
    return weight_grad(features, groups, members)


def local(features, fc_weight, mix_gain, lengths):
    tp_index, zh = lax.axis_index("tp"), lax.axis_index("dp")
    draft_index = lax.axis_index("draft")
    zl, core = tp_index // CORES, tp_index % CORES
    x, y = draft_index // Y, draft_index % Y
    own_rows = features.shape[0]
    piece = own_rows * X * Y // (ZL * CORES)
    own = features.transpose(1, 0, 2)
    weight = fc_weight.transpose(1, 0, 2)

    next_, last, across = (plane_move(step, True)(own) for step in (1, 3, 2))
    low, high = pair(own, next_), pair(across, last)
    up_low, down_high = plane_move(1, False)(low), plane_move(-1, False)(high)
    up_high, down_low = plane_move(1, False)(high), plane_move(-1, False)(low)
    up_low, later = lax.optimization_barrier((up_low, own))
    traded = trade_columns(later)
    far_low, far_high = plane_move(1, False)(up_low), plane_move(-1, False)(down_high)
    near = project([low, high, up_low, up_high, down_low, down_high], weight, 58)
    far_low, far_high, near = lax.optimization_barrier((far_low, far_high, near))
    keep, send = project_place([far_low, far_high], weight, near, core, x, y)
    mine, *away = join(keep, from_other_core(send), zl)
    top, mine, traded = lax.optimization_barrier((own[LEVELS - 1], mine, traded))
    halves = send_high(top, draft_index)
    every = lax.all_gather(turn(traded), "draft", axis=0, tiled=False)
    parts = [mine] + [from_zl(block, step) for step, block in zip((1, 2, 3), away)]
    odd = draft_index % 2
    grad = chain(parts, halves, mix_gain, tp_index * piece, zh, odd, lengths)
    fc_grad, mix_total = gather_grads(grad, every, zl, core)
    return (fc_grad.transpose(1, 0, 2), mix_total[0])


def solution(mesh):
    placed = (P(("dp", "draft"), None, "tp"), P("tp", None, "draft"), P("draft"), P())
    return jax.shard_map(
        local,
        mesh=mesh,
        in_specs=placed,
        out_specs=(P(("tp", "dp"), None, "draft"), P("draft")),
        check_vma=False,
    )
```

```python
import jax
import jax.numpy as jnp
from jax import lax
from jax.experimental import pallas as pl
from jax.experimental.pallas import tpu as pltpu
from jax.sharding import PartitionSpec as P

LEVELS = 3
UNROLL = 3
LOSS_SCALE = 64.0
HALO = 8
TAIL = 16
X, Y = 4, 4
ZL, CORES, ZH = 4, 2, 4
VMEM = pl.BlockSpec(memory_space=pltpu.VMEM)
SMEM = pl.BlockSpec(memory_space=pltpu.SMEM)


def params(mebibytes):
    return pltpu.CompilerParams(vmem_limit_bytes=mebibytes << 20)


def plane_move(step, first):
    pairs = []
    for t in range(ZL * CORES):
        for x in range(X):
            for y in range(Y):
                along_x = (t % CORES == 0) == first
                source = (x + step) % X * Y + y if along_x else x * Y + (y + step) % Y
                pairs.append((t * X * Y + source, t * X * Y + x * Y + y))
    return lambda block: lax.ppermute(block, ("tp", "draft"), pairs)


def from_other_core(block):
    return lax.ppermute(block, "tp", [(t ^ 1, t) for t in range(ZL * CORES)])


def from_zl(block, step):
    pairs = [((t // CORES + step) % ZL * CORES + t % CORES, t) for t in range(ZL * CORES)]
    return lax.ppermute(block, "tp", pairs)


def from_zh(block, step):
    return lax.ppermute(block, "dp", [((s + step) % ZH, s) for s in range(ZH)])


def from_z(block, step):
    pairs = []
    for t in range(ZL * CORES):
        for s in range(ZH):
            z = (s * ZL + t // CORES + step) % (ZL * ZH)
            pairs.append((((z % ZL) * CORES + t % CORES) * ZH + z // ZL, t * ZH + s))
    return lax.ppermute(block, ("tp", "dp"), pairs)


def pair_kernel(first_ref, second_ref, out_ref):
    out_ref[0] = first_ref[...]
    out_ref[1] = second_ref[...]


def pair(first, second):
    return pl.pallas_call(
        pair_kernel,
        out_shape=jax.ShapeDtypeStruct((2,) + first.shape, first.dtype),
        in_specs=[VMEM] * 2,
        out_specs=VMEM,
        compiler_params=params(4),
        cost_estimate=pl.CostEstimate(flops=0, bytes_accessed=8 * first.size, transcendentals=0),
        name="pair",
    )(first, second)


def rows_of(block_refs):
    return jnp.concatenate([r[...].reshape(-1, r.shape[-1]) for r in block_refs], axis=0)


def accumulate(total_ref, term):
    level = pl.program_id(0)

    @pl.when(level == 0)
    def _():
        total_ref[...] = term

    @pl.when(level > 0)
    def _():
        total_ref[...] += term


def project_kernel(*refs):
    *block_refs, weight_ref, out_ref, total_ref = refs
    accumulate(
        total_ref, jnp.dot(rows_of(block_refs), weight_ref[0], preferred_element_type=jnp.float32)
    )

    @pl.when(pl.program_id(0) == LEVELS - 1)
    def _():
        out_ref[...] = total_ref[...].astype(jnp.bfloat16).reshape(out_ref.shape)


def product_specs(blocks, weight):
    _, _, rows, depth = blocks[0].shape
    specs = [pl.BlockSpec((b.shape[0], 1, rows, depth), lambda l, *_: (0, l, 0, 0)) for b in blocks]
    return specs + [pl.BlockSpec((1, depth, weight.shape[2]), lambda l, *_: (l, 0, 0))]


def product_cost(blocks, weight):
    size = sum(b.size for b in blocks)
    return pl.CostEstimate(flops=0, bytes_accessed=2 * size, transcendentals=0)


def project(blocks, weight, mebibytes):
    rows, width = blocks[0].shape[2], weight.shape[2]
    count = sum(b.shape[0] for b in blocks)
    return pl.pallas_call(
        project_kernel,
        grid=(LEVELS,),
        out_shape=jax.ShapeDtypeStruct((count, rows, width), jnp.bfloat16),
        in_specs=product_specs(blocks, weight),
        out_specs=pl.BlockSpec((count, rows, width), lambda l: (0, 0, 0)),
        scratch_shapes=[pltpu.VMEM((count * rows, width), jnp.float32)],
        compiler_params=params(mebibytes),
        cost_estimate=product_cost(blocks, weight),
        name="project",
    )(*blocks, weight)


def project_place_kernel(meta_ref, *refs):
    *block_refs, weight_ref, near_ref, keep_ref, send_ref, total_ref, token_ref = refs
    accumulate(
        total_ref, jnp.dot(rows_of(block_refs), weight_ref[0], preferred_element_type=jnp.float32)
    )

    @pl.when(pl.program_id(0) == LEVELS - 1)
    def _():
        core, x, y = meta_ref[0], meta_ref[1], meta_ref[2]
        rows = near_ref.shape[1]
        total = rows * X * Y
        edge = jnp.zeros((HALO, token_ref.shape[1]), jnp.float32)
        token_ref[pl.ds(0, HALO), :] = edge
        token_ref[pl.ds(HALO + total, HALO), :] = edge
        for second in range(4):
            for first in range(4):
                dx = jnp.where(core == 0, first, second)
                dy = jnp.where(core == 0, second, first)
                e = lax.rem(x + dx, X) * Y + lax.rem(y + dy, Y)
                at = pl.multiple_of(e * rows + HALO, 8)
                if second == 2:
                    block = total_ref[pl.ds(first * rows, rows), :]
                else:
                    block = near_ref[(0, 4, 0, 8)[second] + first].astype(jnp.float32)
                token_ref[pl.ds(at, rows), :] = block
        piece = total // (ZL * CORES)
        for zl in range(ZL):
            for out_ref, whose in ((keep_ref, core), (send_ref, 1 - core)):
                at = pl.multiple_of((zl * CORES + whose) * piece, 8)
                out_ref[zl] = token_ref[pl.ds(at, piece + 2 * HALO), :].astype(jnp.bfloat16)


def project_place(blocks, weight, near, core, x, y):
    _, rows, width = near.shape
    count = sum(b.shape[0] for b in blocks)
    total = rows * X * Y
    pieces = (ZL, total // (ZL * CORES) + 2 * HALO, width)
    whole = lambda shape: pl.BlockSpec(shape, lambda l, *_: (0, 0, 0))
    return pl.pallas_call(
        project_place_kernel,
        out_shape=(jax.ShapeDtypeStruct(pieces, jnp.bfloat16),) * 2,
        grid_spec=pltpu.PrefetchScalarGridSpec(
            num_scalar_prefetch=1,
            grid=(LEVELS,),
            in_specs=product_specs(blocks, weight) + [whole(near.shape)],
            out_specs=(whole(pieces),) * 2,
            scratch_shapes=[
                pltpu.VMEM((count * rows, width), jnp.float32),
                pltpu.VMEM((total + 2 * HALO, width), jnp.float32),
            ],
        ),
        compiler_params=params(18),
        cost_estimate=product_cost(blocks, weight),
        name="project_place",
    )(jnp.stack([core, x, y]), *blocks, weight, near)


def join_kernel(meta_ref, keep_ref, got_ref, own_ref, *away_refs):
    zl = meta_ref[0]

    def piece(index):
        return keep_ref[index].astype(jnp.float32) + got_ref[index].astype(jnp.float32)

    own_ref[...] = piece(zl).astype(jnp.bfloat16)
    for step, away_ref in zip((1, 2, 3), away_refs):
        away_ref[...] = piece(lax.rem(zl + ZL - step, ZL)).astype(jnp.bfloat16)


def join(keep, got, zl):
    count, rows, width = keep.shape
    whole = pl.BlockSpec(keep.shape, lambda i, m: (0, 0, 0))
    piece = pl.BlockSpec((rows, width), lambda i, m: (0, 0))
    return pl.pallas_call(
        join_kernel,
        out_shape=(jax.ShapeDtypeStruct((rows, width), jnp.bfloat16),) * count,
        grid_spec=pltpu.PrefetchScalarGridSpec(
            num_scalar_prefetch=1, grid=(1,), in_specs=[whole] * 2, out_specs=(piece,) * count
        ),
        compiler_params=params(8),
        cost_estimate=pl.CostEstimate(
            flops=keep.size, bytes_accessed=6 * keep.size, transcendentals=0
        ),
        name="join",
    )(zl.reshape(1), keep, got)


def sigmoid(v):
    return 1.0 / (1.0 + jnp.exp(-v))


def chain_kernel(meta_ref, lengths_ref, *refs):
    *part_refs, one_ref, two_ref, left_ref, right_ref, gain_ref, grad_ref = refs
    rows, width = part_refs[0].shape
    own = rows - 2 * HALO
    joined = part_refs[0][...].astype(jnp.float32)
    for part_ref in part_refs[1:]:
        joined = joined + part_ref[...].astype(jnp.float32)
    even = meta_ref[2] == 0
    pick = lambda a, b: jnp.where(even, a[...].astype(jnp.float32), b[...].astype(jnp.float32))
    high = jnp.concatenate(
        [pick(one_ref, two_ref), pick(two_ref, one_ref), pick(left_ref, right_ref)], axis=0
    )
    gain = gain_ref[...]
    start, length = meta_ref[0], lengths_ref[meta_ref[1]]
    valid = jnp.int32(0)
    for step in range(1, UNROLL + 1):
        for sequence in range(lengths_ref.shape[0]):
            valid = valid + jnp.maximum(lengths_ref[sequence] - step, 0)
    scale = LOSS_SCALE / jnp.full((1, width), valid, jnp.int32).astype(jnp.float32)
    position = start - HALO + lax.broadcasted_iota(jnp.int32, (rows, width), 0)

    def down(values):
        return jnp.concatenate([jnp.zeros((1, width), jnp.float32), values[:-1]], axis=0)

    def up(values):
        return jnp.concatenate([values[1:], jnp.zeros((1, width), jnp.float32)], axis=0)

    def target(step):
        lead = jnp.zeros((HALO - step, width), jnp.float32)
        return jnp.concatenate([lead, high[: rows - HALO + step]], axis=0)

    def state_and_slope(v):
        gate = sigmoid(v)
        return v * gate, gate * (1.0 + v * (1.0 - gate))

    def residual(state, step):
        return jnp.where(position + step < length, scale * (state - target(step)), 0.0)

    state_1, slope_1 = state_and_slope(joined)
    before_1 = down(state_1)
    state_2, slope_2 = state_and_slope(joined + gain * before_1)
    before_2 = down(state_2)
    state_3, slope_3 = state_and_slope(joined + gain * before_2)
    delta_3 = residual(state_3, 3) * slope_3
    delta_2 = (residual(state_2, 2) + up(gain * delta_3)) * slope_2
    delta_1 = (residual(state_1, 1) + up(gain * delta_2)) * slope_1
    total = delta_1 + delta_2 + delta_3
    mix = (delta_2 * before_1 + delta_3 * before_2)[HALO : HALO + own]
    rest = jnp.sum(mix, axis=0, keepdims=True)
    tail = []
    for _ in range(3):
        term = rest.astype(jnp.bfloat16).astype(jnp.float32)
        tail.append(term)
        rest = rest - term
    tail.append(jnp.zeros((TAIL - 3, width), jnp.float32))
    grad_ref[pl.ds(0, own), :] = total[HALO : HALO + own].astype(jnp.bfloat16)
    grad_ref[pl.ds(own, TAIL), :] = jnp.concatenate(tail, axis=0).astype(jnp.bfloat16)


def chain(parts, halves, gain, start, zh, odd, lengths):
    rows, width = parts[0].shape
    own = rows - 2 * HALO
    return pl.pallas_call(
        chain_kernel,
        out_shape=jax.ShapeDtypeStruct((own + TAIL, width), jnp.bfloat16),
        in_specs=[SMEM, SMEM] + [VMEM] * (len(parts) + len(halves) + 1),
        out_specs=VMEM,
        compiler_params=params(14),
        cost_estimate=pl.CostEstimate(
            flops=60 * rows * width, bytes_accessed=10 * rows * width, transcendentals=3 * rows * width
        ),
        name="chain",
    )(jnp.stack([start, zh, odd]), lengths, *parts, *halves, gain.reshape(1, width))


def weight_grad_kernel(meta_ref, features_ref, *refs):
    *group_refs, out_ref, mix_ref, grads_ref, held_ref, sem = refs
    half = grads_ref.shape[1] // ZH
    width = grads_ref.shape[2]
    held = [
        pltpu.make_async_copy(features_ref.at[:, at], held_ref.at[at], sem.at[at])
        for at in range(LEVELS)
    ]
    for copy in held:
        copy.start()
    mix = jnp.zeros((TAIL, width), jnp.float32)
    for at, group_ref in enumerate(group_refs):
        for part in range(2):
            slab = grads_ref.at[meta_ref[at] * 2 + part]
            for sequence in range(ZH):
                rows = group_ref[sequence, pl.ds(part * half, half), :]
                slab[pl.ds(sequence * half, half), :] = rows
        for sequence in range(ZH):
            mix = mix + group_ref[sequence, pl.ds(2 * half, TAIL), :].astype(jnp.float32)
    mix_ref[...] = jnp.sum(mix, axis=0, keepdims=True)
    blocks = held_ref.shape[1]
    for level, copy in enumerate(held):
        copy.wait()
        left = jnp.concatenate([held_ref[level, e] for e in range(blocks)], axis=1)
        right = grads_ref[...].reshape(-1, width)
        term = jnp.dot(left, right, preferred_element_type=jnp.float32)
        out_ref[level] = term.astype(jnp.bfloat16)


def weight_grad(features, groups, members):
    draft, _, columns, tokens = features.shape
    count, width = len(groups), groups[0].shape[2]
    return pl.pallas_call(
        weight_grad_kernel,
        out_shape=(
            jax.ShapeDtypeStruct((LEVELS, columns, width), jnp.bfloat16),
            jax.ShapeDtypeStruct((1, width), jnp.float32),
        ),
        in_specs=[SMEM, pl.BlockSpec(memory_space=pltpu.HBM)] + [VMEM] * count,
        out_specs=(VMEM, VMEM),
        scratch_shapes=[
            pltpu.VMEM((draft, tokens, width), jnp.bfloat16),
            pltpu.VMEM((LEVELS, draft, columns, tokens), jnp.bfloat16),
            pltpu.SemaphoreType.DMA((LEVELS,)),
        ],
        compiler_params=params(46),
        cost_estimate=pl.CostEstimate(
            flops=2 * draft * LEVELS * columns * tokens * width,
            bytes_accessed=2 * features.size + 2 * draft * tokens * width,
            transcendentals=0,
        ),
        name="weight_grad",
    )(jnp.stack(members), features, *groups)


def turn_kernel(traded_ref, out_ref):
    rows = traded_ref[:, 0].reshape(-1, traded_ref.shape[3])
    out_ref[0] = rows.astype(jnp.float32).T.astype(jnp.bfloat16)


def turn(traded):
    sequences, levels, rows, columns = traded.shape
    return pl.pallas_call(
        turn_kernel,
        grid=(levels,),
        out_shape=jax.ShapeDtypeStruct((levels, columns, sequences * rows), jnp.bfloat16),
        in_specs=[pl.BlockSpec((sequences, 1, rows, columns), lambda l: (0, l, 0, 0))],
        out_specs=pl.BlockSpec((1, columns, sequences * rows), lambda l: (l, 0, 0)),
        compiler_params=params(8),
        cost_estimate=pl.CostEstimate(flops=0, bytes_accessed=4 * traded.size, transcendentals=0),
        name="turn",
    )(traded)


def send_high(top, draft_index):
    members, draft_count = ZL * CORES, X * Y
    width = top.shape[1] // 2
    even = draft_index % 2 == 0
    left, right = top[:, :width], top[:, width:]
    straight, crossed, after_left, after_right = [], [], [], []
    for t in range(members):
        for e in range(draft_count):
            source = t * draft_count + e
            target = e // 2 * draft_count + 2 * t
            straight.append((source, target + e % 2))
            crossed.append((source, target + 1 - e % 2))
            if e % 2 == 0 and e > 0:
                after_left.append((source, target - draft_count))
                after_right.append((source, target - draft_count + 1))
    axes = ("tp", "draft")
    return (
        lax.ppermute(jnp.where(even, left, right), axes, straight),
        lax.ppermute(jnp.where(even, right, left), axes, crossed),
        lax.ppermute(left[:TAIL], axes, after_left),
        lax.ppermute(right[:TAIL], axes, after_right),
    )


def trade_columns(own):
    levels, rows, depth = own.shape
    quarters = own.reshape(levels, rows, ZH, depth // ZH).transpose(2, 0, 1, 3)
    return lax.all_to_all(quarters, "dp", split_axis=0, concat_axis=0, tiled=True)


def gather_grads(grad, features, zl, core):
    stack = lax.all_gather(grad, "dp", axis=0, tiled=False)
    above, below = from_z(stack, 1), from_z(stack, -1)
    far = jnp.concatenate([from_z(stack[:2], 2), from_z(stack[2:], -2)])
    other = from_other_core(stack)
    above, below, other, far, features = lax.optimization_barrier(
        (above, below, other, far, features)
    )
    swapped = [from_other_core(block) for block in (above, below, far)]

    def member(step, of_core):
        return (zl + step) % ZL * CORES + of_core

    groups = [stack, other, above, below, far] + swapped
    members = [member(0, core), member(0, 1 - core)]
    members += [member(step, core) for step in (1, 3, 2)]
    members += [member(step, 1 - core) for step in (1, 3, 2)]
    return weight_grad(features, groups, members)


def local(features, fc_weight, mix_gain, lengths):
    tp_index, zh = lax.axis_index("tp"), lax.axis_index("dp")
    draft_index = lax.axis_index("draft")
    zl, core = tp_index // CORES, tp_index % CORES
    x, y = draft_index // Y, draft_index % Y
    own_rows = features.shape[0]
    piece = own_rows * X * Y // (ZL * CORES)
    own = features.transpose(1, 0, 2)
    weight = fc_weight.transpose(1, 0, 2)

    next_, last, across = (plane_move(step, True)(own) for step in (1, 3, 2))
    low, high = pair(own, next_), pair(across, last)
    up_low, down_high = plane_move(1, False)(low), plane_move(-1, False)(high)
    up_high, down_low = plane_move(1, False)(high), plane_move(-1, False)(low)
    up_low, later = lax.optimization_barrier((up_low, own))
    traded = trade_columns(later)
    far_low, far_high = plane_move(1, False)(up_low), plane_move(-1, False)(down_high)
    near = project([low, high, up_low, up_high, down_low, down_high], weight, 58)
    far_low, far_high, near = lax.optimization_barrier((far_low, far_high, near))
    keep, send = project_place([far_low, far_high], weight, near, core, x, y)
    mine, *away = join(keep, from_other_core(send), zl)
    top, mine = lax.optimization_barrier((own[LEVELS - 1], mine))
    halves = send_high(top, draft_index)
    parts = [mine] + [from_zl(block, step) for step, block in zip((1, 2, 3), away)]
    parts[1], traded = lax.optimization_barrier((parts[1], traded))
    every = lax.all_gather(turn(traded), "draft", axis=0, tiled=False)
    odd = draft_index % 2
    grad = chain(parts, halves, mix_gain, tp_index * piece, zh, odd, lengths)
    fc_grad, mix_total = gather_grads(grad, every, zl, core)
    return (fc_grad.transpose(1, 0, 2), mix_total[0])


def solution(mesh):
    placed = (P(("dp", "draft"), None, "tp"), P("tp", None, "draft"), P("draft"), P())
    return jax.shard_map(
        local,
        mesh=mesh,
        in_specs=placed,
        out_specs=(P(("tp", "dp"), None, "draft"), P("draft")),
        check_vma=False,
    )
```
